256 devices in a mesh: ctx: 64 (over x, y, z_hi), grp: 4 (over z_lo, core).
Axes of the slice: x: 4, y: 4, z: 8 (z_hi: 4, z_lo: 2; z = z_hi * 2 + z_lo), core: 2. Of those that a mesh axis runs over, the one named last changes fastest.
Arguments:
- q_latent: bfloat16 [8, 128, 512], P('grp', 'ctx'), parts along dimension 0, may hold values from -48 to 48
- q_rope: bfloat16 [8, 128, 64], P('grp', 'ctx'), parts along dimension 0, may hold values from -48 to 48
- latent_cache: bfloat16 [2048, 64, 576], P(('grp', 'ctx')), parts along dimension 0, may hold values from -6 to 6
- page_table: int32 [8, 256], P('grp'), parts along dimension 0, may hold values from 0 to 511, as said below
- lengths: int32 [8], P('grp'), parts along dimension 0, may hold values from 1 to 16384, 20480 in all
- w_uv: bfloat16 [128, 512, 128], P('ctx'), may hold values from -6 to 6
- w_out: bfloat16 [16384, 7168], P('ctx'), may hold values from -0.046875 to 0.046875
Outputs:
- layer_out: bfloat16 [8, 7168], P('grp'), parts along dimension 0
The draws below stay inside these ranges and needn't reach their ends.
There are 4 independent parts, one for each index of `grp`. The reference program is written for one: setup_inputs(seed, part) draws one part's arguments, and reference() takes and returns one part's arrays. A program takes and returns all parts, laid end to end along the dimension named above; an argument that names none is the same for every part. Nothing has to cross between parts.
Inputs may be any that keep to these rules, and one draw needn't show every extreme that they name: `page_table`: every page number stands exactly once in the table. The longest row is at most 16384; all lengths sum to 20480.
All inputs are finite; a program needn't handle non-finite values.
Results may differ from the reference program's by a relative error of at most 0.03.
Values may be sent and summed in bfloat16 or wider, within the bound.
No kernel may reach another device: no remote copies, remote signals or barrier semaphores. Data moves between devices by JAX's collectives and lax.ppermute only.
A program may use at most 128 MiB of HBM per device.

```python
import math
import jax
import jax.numpy as jnp
import numpy as np
from jax import lax

H = 128
C = 512
ROPE = 64
V = 128
D = 7168
PAGE = 64
ROWS = 2
PAGES = 512
MAXP = 256


def page_order(key):
    order = jax.random.permutation(jax.random.fold_in(key, 7), PAGES)
    return order.astype(jnp.int32).reshape(ROWS, MAXP)


def cache_base(key):
    base = jax.random.normal(jax.random.fold_in(key, 11), (PAGES, PAGE, C + ROPE), jnp.float32)
    return jnp.clip(base, -6.0, 6.0)


def query_full(key, strength):
    base = jnp.clip(jax.random.normal(jax.random.fold_in(key, 13), (ROWS, H, C + ROPE), jnp.float32), -6.0, 6.0)
    chosen = (jnp.arange(H) % 8 == 0).astype(jnp.float32) * jnp.float32(strength)
    return base * (1.0 - chosen[None, :, None])


def draw_page_table(key, part):
    table = page_order(key)
    return table


def draw_latent_cache(key, part):
    base = cache_base(key)
    return base.astype(jnp.bfloat16)


def draw_q_latent(key, part):
    strength = 0.0
    full = query_full(key, strength)
    return full[:, :, :C].astype(jnp.bfloat16)


def draw_q_rope(key, part):
    strength = 0.0
    full = query_full(key, strength)
    return full[:, :, C:].astype(jnp.bfloat16)


def level_of(stream_key, dims, shards, low, high):
    level = 1.0
    for dim, blocks in shards:
        draws = jax.random.uniform(jax.random.fold_in(jax.random.fold_in(stream_key, 6), dim), (blocks,), jnp.float32, low / len(shards), high / len(shards))
        level = level * jnp.repeat(jnp.exp(draws), dims[dim] // blocks).reshape((-1,) + (1,) * (len(dims) - 1 - dim))
    return level


def profile(number_of, total, limit, lean):
    weights = [(1 << 20) // math.isqrt(standing ** lean) + 1 for standing in range(2, number_of + 1)]
    rest, counts = total - limit - (number_of - 1), [1] * (number_of - 1)
    while rest > 0:
        free = [i for i in range(number_of - 1) if counts[i] < limit]
        whole, left = sum([weights[i] for i in free]), rest
        for i in free:
            extra = min(limit - counts[i], max(1, left * weights[i] // whole), rest)
            counts[i] = counts[i] + extra
            rest = rest - extra
    return np.array([limit] + counts)


def ragged(own_key, number_of, total, limit, slope):
    if number_of == 2:
        one = jax.random.randint(own_key, (), max(1, total - limit), min(limit, total - 1) + 1)
        return jnp.stack([one, total - one])
    sizes = jnp.asarray(profile(number_of, total, limit, slope), jnp.int32)
    couples = (number_of - 1) // 2
    donor, taker = sizes[1:1 + 2 * couples:2], sizes[2:2 + 2 * couples:2]
    slack = jnp.minimum(donor - 1, limit - taker)
    moved = jax.random.randint(jax.random.fold_in(own_key, 1), (couples,), 0, 1 << 20) % (slack + 1)
    sizes = sizes.at[1:1 + 2 * couples:2].set(donor - moved).at[2:2 + 2 * couples:2].set(taker + moved)
    return sizes[jax.random.permutation(jax.random.fold_in(own_key, 2), number_of)]


def scatter_about(stream_key, dims, spread, limit, cuts=(), held_as=jnp.bfloat16):
    values = jax.random.normal(stream_key, dims, jnp.float32) * spread
    if len(cuts) > 0:
        values = level_of(stream_key, dims, cuts, -0.22, 0.18) * values
    return jnp.clip(values, min=-limit, max=limit).astype(held_as)


def setup_inputs(seed: int = 0, part: int = 0) -> dict:
    seeds = jax.random.split(jax.random.key(seed), 8)
    own_keys = jax.random.split(jax.random.fold_in(seeds[7], part), 8)
    return {
        "q_latent": draw_q_latent(jax.random.fold_in(jax.random.fold_in(seeds[7], part), 71), part),
        "q_rope": draw_q_rope(jax.random.fold_in(jax.random.fold_in(seeds[7], part), 71), part),
        "latent_cache": draw_latent_cache(jax.random.fold_in(jax.random.fold_in(seeds[7], part), 71), part),
        "page_table": draw_page_table(jax.random.fold_in(jax.random.fold_in(seeds[7], part), 71), part),
        "lengths": ragged(own_keys[4], ROWS, ROWS * MAXP * PAGE * 5 // 8, MAXP * PAGE, 2).astype(jnp.int32),
        "w_uv": scatter_about(seeds[5], (H, C, V), (16.0 / C ** 0.5), 6.0, ((0, 64),)),
        "w_out": scatter_about(seeds[6], (H * V, D), (H * V) ** -0.5, 0.046875, ((0, 64),)),
    }


NEG = -1e30


def reference(q_latent, q_rope, latent_cache, page_table, lengths, w_uv, w_out):
    score_scale = (V + ROPE) ** -0.5
    query = jnp.concatenate([q_latent, q_rope], axis=2)
    position = jnp.arange(MAXP * PAGE, dtype=jnp.int32)

    def one_row(packed):
        row_query, row_pages, length = packed
        row_keys = latent_cache[row_pages].reshape(MAXP * PAGE, C + ROPE)
        scores = jnp.dot(row_query, row_keys.T, preferred_element_type=jnp.float32) * score_scale
        live_mask = (position < length)[None, :]
        scores = jnp.where(live_mask, scores, jnp.float32(NEG))
        top_score = jnp.max(scores, axis=1)
        weights = jnp.where(live_mask, jnp.exp(scores - top_score[:, None]), jnp.float32(0.0)).astype(jnp.bfloat16)
        row_total = jnp.sum(weights.astype(jnp.float32), axis=1)
        summed = jnp.dot(weights, row_keys[:, :C], preferred_element_type=jnp.float32)
        return (summed / row_total[:, None]).astype(jnp.bfloat16)

    attended = lax.map(one_row, (query, page_table, lengths))
    head_out = jnp.einsum("rhc,hcv->rhv", attended.astype(jnp.float32), w_uv.astype(jnp.float32)).astype(jnp.bfloat16)
    flat = head_out.reshape(ROWS, H * V)
    return jnp.dot(flat, w_out, preferred_element_type=jnp.float32).astype(jnp.bfloat16)
```

```python
import jax
import jax.numpy as jnp
from jax import lax
from jax.sharding import PartitionSpec as P

ROPE = 64
V = 128
NEG = -1e30
CTX = "ctx"


def xor_pairs(count, mask):
    return [(i, i ^ mask) for i in range(count)]


def sum_of_four(x, count, low):
    a, b, c = (lax.ppermute(x, CTX, xor_pairs(count, k << low)) for k in (1, 2, 3))
    return (x + a) + (b + c)


def local(q_latent, q_rope, latent_cache, page_table, lengths, w_uv, w_out):
    score_scale = (V + ROPE) ** (-0.5)
    rows, heads, latent = q_latent.shape
    pages, page_len, width = latent_cache.shape
    count = lax.axis_size(CTX)
    mixed = rows * heads

    query = jnp.concatenate([q_latent, q_rope], axis=2).reshape(1, mixed, width)
    queries = lax.all_to_all(
        jnp.broadcast_to(query, (count, mixed, width)), CTX, split_axis=0, concat_axis=0, tiled=True
    ).reshape(count * mixed, width)

    slots = page_table.size
    page_ids = lax.axis_index(CTX) * pages + jnp.arange(pages, dtype=jnp.int32)
    table = page_table.reshape(1, slots)
    slot = jnp.sum(
        jnp.where(table == page_ids[:, None], jnp.arange(slots, dtype=jnp.int32)[None], 0), axis=1
    )
    owner = slot // page_table.shape[1]
    logical = slot % page_table.shape[1]
    position = logical[:, None] * page_len + jnp.arange(page_len, dtype=jnp.int32)[None]
    rank = jnp.arange(rows, dtype=jnp.int32)
    live = (owner[None, :, None] == rank[:, None, None]) & (
        position[None] < lengths[:, None, None]
    )
    live = live.reshape(rows, pages * page_len)
    live = jnp.broadcast_to(live[None, :, None], (count, rows, heads, pages * page_len))
    live = live.reshape(count * mixed, pages * page_len)

    keys = latent_cache.reshape(pages * page_len, width)
    scores = (
        lax.dot_general(queries, keys, (((1,), (1,)), ((), ())), preferred_element_type=jnp.float32)
        * score_scale
    )
    scores = jnp.where(live, scores, jnp.float32(NEG))
    shift = jnp.max(scores, axis=1, keepdims=True).astype(jnp.bfloat16)
    weights = jnp.where(live, jnp.exp(scores - shift.astype(jnp.float32)), 0.0).astype(jnp.bfloat16)
    sums = jnp.sum(weights.astype(jnp.float32), axis=1, keepdims=True)
    outs = jnp.dot(weights, keys[:, :latent], preferred_element_type=jnp.float32)
    sums_hi = sums.astype(jnp.bfloat16)
    sums_lo = (sums - sums_hi.astype(jnp.float32)).astype(jnp.bfloat16)
    state = jnp.concatenate([outs.astype(jnp.bfloat16), shift, sums_hi, sums_lo], axis=1)
    state = jnp.pad(state, ((0, 0), (0, 125))).reshape(count, mixed, latent + 128)

    state = lax.all_to_all(state, CTX, split_axis=0, concat_axis=0, tiled=True)
    shift = state[:, :, latent].astype(jnp.float32)
    sums = state[:, :, latent + 1].astype(jnp.float32) + state[:, :, latent + 2].astype(jnp.float32)
    factor = jnp.exp(shift - jnp.max(shift, axis=0, keepdims=True))
    total = jnp.sum(factor * sums, axis=0)
    merged = jnp.sum(factor[:, :, None] * state[:, :, :latent].astype(jnp.float32), axis=0)
    attended = (merged / total[:, None]).astype(jnp.bfloat16).reshape(rows, heads, latent)
    head_out = jnp.einsum("rhc,hcv->rhv", attended, w_uv, preferred_element_type=jnp.float32)
    flat = head_out.astype(jnp.bfloat16).reshape(rows, -1)
    term = jnp.dot(flat, w_out, preferred_element_type=jnp.float32)
    for low in (4, 2, 0):
        term = sum_of_four(term, count, low)
    return term.astype(jnp.bfloat16)


def solution(mesh):
    in_specs = (
        P("grp", "ctx", None),
        P("grp", "ctx", None),
        P(("grp", "ctx"), None, None),
        P("grp", None),
        P("grp"),
        P("ctx", None, None),
        P("ctx", None),
    )
    return jax.shard_map(local, mesh=mesh, in_specs=in_specs, out_specs=P("grp", None), check_vma=False)
```

```python
import functools
import jax
import jax.numpy as jnp
from jax import lax
from jax.experimental import pallas as pl
from jax.experimental.pallas import tpu as pltpu
from jax.sharding import PartitionSpec as P

ROPE = 64
V = 128
NEG = -1e30
CTX = "ctx"
LANES = 128


def xor_pairs(count, mask):
    return [(i, i ^ mask) for i in range(count)]


def sum_of_four(x, count, low):
    a, b, c = (lax.ppermute(x, CTX, xor_pairs(count, k << low)) for k in (1, 2, 3))
    f = jnp.float32
    return (x.astype(f) + a.astype(f)) + (b.astype(f) + c.astype(f))


def attend_kernel(rows, heads, page_len, latent, here_ref, lengths_ref, table_ref, q_ref, keys_ref, state_ref):
    tokens = keys_ref.shape[0]
    pages = tokens // page_len
    slots = table_ref.shape[1]
    page = here_ref[0] * pages + lax.broadcasted_iota(jnp.int32, (pages, slots), 0)
    place = lax.broadcasted_iota(jnp.int32, (pages, slots), 1)
    token = lax.broadcasted_iota(jnp.int32, (pages, tokens), 1)
    mine = token // page_len == lax.broadcasted_iota(jnp.int32, (pages, tokens), 0)
    lives = []
    for r in range(rows):
        hit = jnp.broadcast_to(table_ref[r : r + 1, :], (pages, slots)) == page
        room = jnp.where(hit, lengths_ref[r] - place * page_len, 0)
        room = jnp.max(room, axis=1, keepdims=True)
        alive = mine & (token % page_len < room)
        lives.append(jnp.max(jnp.where(alive, 1.0, 0.0), axis=0, keepdims=True))
    count = q_ref.shape[0]
    row = lax.broadcasted_iota(jnp.int32, (count, 1), 0) // heads % rows
    live = jnp.broadcast_to(lives[0], (count, tokens))
    for r in range(1, rows):
        live = jnp.where(row == r, lives[r], live)
    live = live > 0.5

    scores = lax.dot_general(
        q_ref[...], keys_ref[...], (((1,), (1,)), ((), ())), preferred_element_type=jnp.float32
    ) * ((V + ROPE) ** (-0.5))
    scores = jnp.where(live, scores, NEG)
    shift = jnp.max(scores, axis=1, keepdims=True).astype(jnp.bfloat16).astype(jnp.float32)
    weights = jnp.where(live, jnp.exp(scores - shift), 0.0).astype(jnp.bfloat16)
    total = jnp.sum(weights.astype(jnp.float32), axis=1, keepdims=True)
    outs = jnp.dot(weights, keys_ref[:, :latent], preferred_element_type=jnp.float32)
    state_ref[:, :latent] = outs.astype(jnp.bfloat16)
    high = total.astype(jnp.bfloat16).astype(jnp.float32)
    lane = lax.broadcasted_iota(jnp.int32, (count, LANES), 1)
    stats = jnp.where(lane == 0, shift, jnp.where(lane == 1, high, jnp.where(lane == 2, total - high, 0.0)))
    state_ref[:, latent:] = stats.astype(jnp.bfloat16)


def project_kernel(rows, heads, latent, state_ref, w_uv_ref, w_out_ref, term_ref):
    count = state_ref.shape[0]
    mixed = rows * heads
    lane = lax.broadcasted_iota(jnp.int32, (count, LANES), 1)
    kind = lax.broadcasted_iota(jnp.int32, (count, LANES), 0) % mixed
    own = (lane % mixed == kind) & (lane < 2 * mixed)
    shift = state_ref[:, latent : latent + 1].astype(jnp.float32)
    shift = jnp.where(own, shift, 2 * NEG)
    best = jnp.max(shift, axis=0, keepdims=True)
    factor = jnp.where(own, jnp.exp(shift - best), 0.0)
    high = factor.astype(jnp.bfloat16).astype(jnp.float32)
    factor = jnp.where(lane < mixed, high, factor - high).astype(jnp.bfloat16)
    merged = lax.dot_general(
        factor, state_ref[...], (((0,), (0,)), ((), ())), preferred_element_type=jnp.float32
    )
    merged = merged[:mixed] + merged[mixed : 2 * mixed]
    total = merged[:, latent + 1 : latent + 2] + merged[:, latent + 2 : latent + 3]
    attended = (merged[:, :latent] / total).astype(jnp.bfloat16)
    parts = [
        jnp.dot(attended, w_uv_ref[h], preferred_element_type=jnp.float32) for h in range(heads)
    ]
    flat = jnp.concatenate(
        [
            jnp.concatenate([parts[h][r * heads + h : r * heads + h + 1] for h in range(heads)], axis=1)
            for r in range(rows)
        ],
        axis=0,
    ).astype(jnp.bfloat16)
    term_ref[...] = jnp.dot(flat, w_out_ref[...], preferred_element_type=jnp.float32).astype(
        term_ref.dtype
    )


def local(q_latent, q_rope, latent_cache, page_table, lengths, w_uv, w_out):
    rows, heads, latent = q_latent.shape
    pages, page_len, width = latent_cache.shape
    count = lax.axis_size(CTX)
    mixed = rows * heads
    vmem = pl.BlockSpec(memory_space=pltpu.VMEM)
    smem = pl.BlockSpec(memory_space=pltpu.SMEM)

    query = jnp.concatenate([q_latent, q_rope], axis=2).reshape(1, mixed, width)
    queries = lax.all_to_all(
        jnp.broadcast_to(query, (count, mixed, width)), CTX, split_axis=0, concat_axis=0, tiled=True
    ).reshape(count * mixed, width)

    here = lax.axis_index(CTX).reshape(1).astype(jnp.int32)
    state = pl.pallas_call(
        functools.partial(attend_kernel, rows, heads, page_len, latent),
        out_shape=jax.ShapeDtypeStruct((count * mixed, latent + LANES), jnp.bfloat16),
        in_specs=[smem, smem, vmem, vmem, vmem],
        out_specs=vmem,
        compiler_params=pltpu.CompilerParams(vmem_limit_bytes=16 << 20),
        name="attend",
    )(here, lengths, page_table, queries, latent_cache.reshape(pages * page_len, width))

    state = lax.all_to_all(
        state.reshape(count, mixed, latent + LANES), CTX, split_axis=0, concat_axis=0, tiled=True
    ).reshape(count * mixed, latent + LANES)
    term = pl.pallas_call(
        functools.partial(project_kernel, rows, heads, latent),
        out_shape=jax.ShapeDtypeStruct((rows, w_out.shape[1]), jnp.bfloat16),
        in_specs=[vmem, vmem, vmem],
        out_specs=vmem,
        compiler_params=pltpu.CompilerParams(vmem_limit_bytes=16 << 20),
        name="project",
    )(state, w_uv, w_out)
    for low in (4, 2, 0):
        term = sum_of_four(term, count, low).astype(jnp.bfloat16)
    return term


def solution(mesh):
    in_specs = (
        P("grp", "ctx", None),
        P("grp", "ctx", None),
        P(("grp", "ctx"), None, None),
        P("grp", None),
        P("grp"),
        P("ctx", None, None),
        P("ctx", None),
    )
    return jax.shard_map(local, mesh=mesh, in_specs=in_specs, out_specs=P("grp", None), check_vma=False)
```

```python
import functools
import jax
import jax.numpy as jnp
from jax import lax
from jax.experimental import pallas as pl
from jax.experimental.pallas import tpu as pltpu
from jax.sharding import PartitionSpec as P

ROPE = 64
V = 128
NEG = -1e30
CTX = "ctx"
LANES = 128
F32 = jnp.float32
BF16 = jnp.bfloat16


def xor_pairs(count, mask):
    return [(i, i ^ mask) for i in range(count)]


def sum_of_four(x, count, low):
    a, b, c = (lax.ppermute(x, CTX, xor_pairs(count, k << low)) for k in (1, 2, 3))
    return (x.astype(F32) + a.astype(F32)) + (b.astype(F32) + c.astype(F32))


def prepare_kernel(
    page_len, here_ref, lengths_hbm, table_hbm, q_latent_hbm, q_rope_hbm, cache_hbm,
    query_ref, live_ref, keys_ref, lengths_ref, table_ref, q_latent_ref, q_rope_ref, sems,
):
    pairs = (
        (q_latent_hbm, q_latent_ref), (q_rope_hbm, q_rope_ref), (lengths_hbm, lengths_ref),
        (table_hbm, table_ref), (cache_hbm, keys_ref),
    )
    copies = [pltpu.make_async_copy(a, b, sems.at[k]) for k, (a, b) in enumerate(pairs)]
    for copy in copies:
        copy.start()
    rows, heads, latent = q_latent_ref.shape
    rope = q_rope_ref.shape[2]
    copies[0].wait()
    copies[1].wait()
    q_latent = q_latent_ref[...].astype(F32)
    q_rope = q_rope_ref[...].astype(F32)
    message = jnp.concatenate(
        [
            jnp.concatenate(
                [q_latent[r, h : h + 1] for h in range(heads)] + [q_rope[r, h : h + 1] for h in range(heads)],
                axis=1,
            )
            for r in range(rows)
        ],
        axis=0,
    )
    query_ref[...] = jnp.broadcast_to(message[None], query_ref.shape).astype(BF16)
    copies[2].wait()
    copies[3].wait()
    tokens = keys_ref.shape[0]
    pages = tokens // page_len
    slots = table_ref.shape[1]
    page = here_ref[0] * pages + lax.broadcasted_iota(jnp.int32, (pages, slots), 0)
    place = lax.broadcasted_iota(jnp.int32, (pages, slots), 1)
    token = lax.broadcasted_iota(jnp.int32, (pages, tokens), 1)
    mine = token // page_len == lax.broadcasted_iota(jnp.int32, (pages, tokens), 0)
    for r in range(rows):
        hit = jnp.broadcast_to(table_ref[r : r + 1, :], (pages, slots)) == page
        room = jnp.where(hit, lengths_ref[r] - place * page_len, 0)
        room = jnp.max(room, axis=1, keepdims=True)
        alive = mine & (token % page_len < room)
        live_ref[r : r + 1, :] = jnp.max(jnp.where(alive, 1.0, 0.0), axis=0, keepdims=True)
    copies[4].wait()


def attend_kernel(
    rows, heads, latent, rope, q_ref, keys_ref, live_ref, w_uv_hbm, w_out_hbm,
    state_ref, w_uv_ref, w_out_ref, sems,
):
    copies = [
        pltpu.make_async_copy(w_uv_hbm, w_uv_ref, sems.at[0]),
        pltpu.make_async_copy(w_out_hbm, w_out_ref, sems.at[1]),
    ]
    for copy in copies:
        copy.start()
    count = q_ref.shape[0]
    tokens = keys_ref.shape[0]
    row = lax.broadcasted_iota(jnp.int32, (count, 1), 0) % rows
    live = jnp.broadcast_to(live_ref[0:1, :], (count, tokens))
    for r in range(1, rows):
        live = jnp.where(row == r, live_ref[r : r + 1, :], live)
    live = live > 0.5
    side = heads * latent
    lane = lax.broadcasted_iota(jnp.int32, (count, state_ref.shape[1] - side), 1)
    stats = jnp.zeros(lane.shape, F32)
    for h in range(heads):
        query = jnp.concatenate(
            [q_ref[:, h * latent : (h + 1) * latent], q_ref[:, side + h * rope : side + (h + 1) * rope]], axis=1
        )
        scores = lax.dot_general(
            query, keys_ref[...], (((1,), (1,)), ((), ())), preferred_element_type=F32
        ) * ((V + ROPE) ** (-0.5))
        scores = jnp.where(live, scores, NEG)
        shift = jnp.max(scores, axis=1, keepdims=True).astype(BF16).astype(F32)
        weights = jnp.where(live, jnp.exp(scores - shift), 0.0).astype(BF16)
        total = jnp.sum(weights.astype(F32), axis=1, keepdims=True)
        outs = jnp.dot(weights, keys_ref[:, :latent], preferred_element_type=F32)
        state_ref[:, h * latent : (h + 1) * latent] = outs.astype(BF16)
        high = total.astype(BF16).astype(F32)
        for k, value in enumerate((shift, high, total - high)):
            stats = jnp.where(lane == 3 * h + k, value, stats)
    state_ref[:, side:] = stats.astype(BF16)
    for copy in copies:
        copy.wait()


def project_kernel(rows, heads, latent, state_ref, w_uv_ref, w_out_ref, term_ref):
    count = state_ref.shape[0]
    mixed = rows * heads
    side = heads * latent
    lane = lax.broadcasted_iota(jnp.int32, (count, LANES), 1)
    row = lax.broadcasted_iota(jnp.int32, (count, LANES), 0) % rows
    column = lane % mixed
    own = (column // heads == row) & (lane < 2 * mixed)
    stats = state_ref[:, side:].astype(F32)
    shift = jnp.full((count, LANES), 2 * NEG, F32)
    for h in range(heads):
        shift = jnp.where(own & (column % heads == h), stats[:, 3 * h : 3 * h + 1], shift)
    best = jnp.max(shift, axis=0, keepdims=True)
    factor = jnp.where(own, jnp.exp(shift - best), 0.0)
    high = factor.astype(BF16).astype(F32)
    factor = jnp.where(lane < mixed, high, factor - high).astype(BF16)
    merged = lax.dot_general(
        factor, state_ref[...], (((0,), (0,)), ((), ())), preferred_element_type=F32
    )
    merged = merged[:mixed] + merged[mixed : 2 * mixed]
    parts = []
    for h in range(heads):
        total = merged[:, side + 3 * h + 1 : side + 3 * h + 2] + merged[:, side + 3 * h + 2 : side + 3 * h + 3]
        attended = (merged[:, h * latent : (h + 1) * latent] / total).astype(BF16)
        parts.append(jnp.dot(attended, w_uv_ref[h], preferred_element_type=F32))
    flat = jnp.concatenate(
        [
            jnp.concatenate([parts[h][r * heads + h : r * heads + h + 1] for h in range(heads)], axis=1)
            for r in range(rows)
        ],
        axis=0,
    ).astype(BF16)
    term_ref[...] = jnp.dot(flat, w_out_ref[...], preferred_element_type=F32).astype(term_ref.dtype)


def local(q_latent, q_rope, latent_cache, page_table, lengths, w_uv, w_out):
    rows, heads, latent = q_latent.shape
    rope = q_rope.shape[2]
    pages, page_len, width = latent_cache.shape
    tokens = pages * page_len
    count = lax.axis_size(CTX)
    size = heads * (latent + rope)
    vmem = pl.BlockSpec(memory_space=pltpu.VMEM)
    smem = pl.BlockSpec(memory_space=pltpu.SMEM)
    hbm = pl.BlockSpec(memory_space=pltpu.HBM)
    params = pltpu.CompilerParams(vmem_limit_bytes=16 << 20)
    dma = pltpu.SemaphoreType.DMA

    here = lax.axis_index(CTX).reshape(1).astype(jnp.int32)
    query, live, keys = pl.pallas_call(
        functools.partial(prepare_kernel, page_len),
        out_shape=(
            jax.ShapeDtypeStruct((count, rows, size), BF16),
            jax.ShapeDtypeStruct((rows, tokens), F32),
            jax.ShapeDtypeStruct((tokens, width), BF16),
        ),
        in_specs=[smem, hbm, hbm, hbm, hbm, hbm],
        out_specs=(vmem, vmem, vmem),
        scratch_shapes=[
            pltpu.SMEM(lengths.shape, jnp.int32),
            pltpu.VMEM(page_table.shape, jnp.int32),
            pltpu.VMEM(q_latent.shape, BF16),
            pltpu.VMEM(q_rope.shape, BF16),
            dma((5,)),
        ],
        compiler_params=params,
        name="prepare",
    )(here, lengths, page_table, q_latent, q_rope, latent_cache.reshape(tokens, width))

    query = lax.all_to_all(query, CTX, split_axis=0, concat_axis=0, tiled=True)

    state_size = heads * latent + LANES
    state, w_uv, w_out = pl.pallas_call(
        functools.partial(attend_kernel, rows, heads, latent, rope),
        out_shape=(
            jax.ShapeDtypeStruct((count * rows, state_size), BF16),
            jax.ShapeDtypeStruct(w_uv.shape, BF16),
            jax.ShapeDtypeStruct(w_out.shape, BF16),
        ),
        in_specs=[vmem, vmem, vmem, hbm, hbm],
        out_specs=(vmem, vmem, vmem),
        scratch_shapes=[dma((2,))],
        compiler_params=params,
        name="attend",
    )(query.reshape(count * rows, size), keys, live, w_uv, w_out)

    state = lax.all_to_all(
        state.reshape(count, rows, state_size), CTX, split_axis=0, concat_axis=0, tiled=True
    )
    term = pl.pallas_call(
        functools.partial(project_kernel, rows, heads, latent),
        out_shape=jax.ShapeDtypeStruct((rows, w_out.shape[1]), BF16),
        in_specs=[vmem, vmem, vmem],
        out_specs=vmem,
        compiler_params=params,
        name="project",
    )(state.reshape(count * rows, state_size), w_uv, w_out)
    for low in (4, 2, 0):
        term = sum_of_four(term, count, low).astype(BF16)
    return term


def solution(mesh):
    in_specs = (
        P("grp", "ctx", None),
        P("grp", "ctx", None),
        P(("grp", "ctx"), None, None),
        P("grp", None),
        P("grp"),
        P("ctx", None, None),
        P("ctx", None),
    )
    return jax.shard_map(local, mesh=mesh, in_specs=in_specs, out_specs=P("grp", None), check_vma=False)
```

```python
import functools
import jax
import jax.numpy as jnp
from jax import lax
from jax.experimental import pallas as pl
from jax.experimental.pallas import tpu as pltpu
from jax.sharding import PartitionSpec as P

ROPE = 64
V = 128
NEG = -1e30
CTX = "ctx"
LANES = 128
F32 = jnp.float32
BF16 = jnp.bfloat16


def xor_pairs(count, mask):
    return [(i, i ^ mask) for i in range(count)]


def sum_of_four(x, count, low):
    a, b, c = (lax.ppermute(x, CTX, xor_pairs(count, k << low)) for k in (1, 2, 3))
    return (x.astype(F32) + a.astype(F32)) + (b.astype(F32) + c.astype(F32))


def prepare_kernel(
    page_len, here_ref, lengths_hbm, table_hbm, q_latent_hbm, q_rope_hbm, cache_hbm,
    query_ref, live_ref, keys_ref, lengths_ref, table_ref, q_latent_ref, q_rope_ref, sems,
):
    pairs = (
        (q_latent_hbm, q_latent_ref), (q_rope_hbm, q_rope_ref), (lengths_hbm, lengths_ref),
        (table_hbm, table_ref), (cache_hbm, keys_ref),
    )
    copies = [pltpu.make_async_copy(a, b, sems.at[k]) for k, (a, b) in enumerate(pairs)]
    for copy in copies:
        copy.start()
    rows, heads, latent = q_latent_ref.shape
    rope = q_rope_ref.shape[2]
    copies[0].wait()
    copies[1].wait()
    q_latent = q_latent_ref[...].astype(F32)
    q_rope = q_rope_ref[...].astype(F32)
    message = jnp.concatenate(
        [
            jnp.concatenate(
                [q_latent[r, h : h + 1] for h in range(heads)] + [q_rope[r, h : h + 1] for h in range(heads)],
                axis=1,
            )
            for r in range(rows)
        ],
        axis=0,
    )
    query_ref[...] = jnp.broadcast_to(message[None], query_ref.shape).astype(BF16)
    copies[2].wait()
    copies[3].wait()
    tokens = keys_ref.shape[0]
    pages = tokens // page_len
    slots = table_ref.shape[1]
    page = here_ref[0] * pages + lax.broadcasted_iota(jnp.int32, (pages, slots), 0)
    place = lax.broadcasted_iota(jnp.int32, (pages, slots), 1)
    token = lax.broadcasted_iota(jnp.int32, (pages, tokens), 1)
    mine = token // page_len == lax.broadcasted_iota(jnp.int32, (pages, tokens), 0)
    for r in range(rows):
        hit = jnp.broadcast_to(table_ref[r : r + 1, :], (pages, slots)) == page
        room = jnp.where(hit, lengths_ref[r] - place * page_len, 0)
        room = jnp.max(room, axis=1, keepdims=True)
        alive = mine & (token % page_len < room)
        live_ref[r : r + 1, :] = jnp.max(jnp.where(alive, 1.0, 0.0), axis=0, keepdims=True)
    copies[4].wait()


def attend_kernel(
    rows, heads, latent, rope, q_ref, keys_ref, live_ref, w_uv_hbm, w_out_hbm,
    state_ref, w_uv_ref, w_out_ref, sems,
):
    copies = [
        pltpu.make_async_copy(w_uv_hbm, w_uv_ref, sems.at[0]),
        pltpu.make_async_copy(w_out_hbm, w_out_ref, sems.at[1]),
    ]
    for copy in copies:
        copy.start()
    count = q_ref.shape[0]
    tokens = keys_ref.shape[0]
    row = lax.broadcasted_iota(jnp.int32, (count, 1), 0) % rows
    live = jnp.broadcast_to(live_ref[0:1, :], (count, tokens))
    for r in range(1, rows):
        live = jnp.where(row == r, live_ref[r : r + 1, :], live)
    live = live > 0.5
    side = heads * latent
    lane = lax.broadcasted_iota(jnp.int32, (count, state_ref.shape[1] - side), 1)
    stats = jnp.zeros(lane.shape, F32)
    for h in range(heads):
        query = jnp.concatenate(
            [q_ref[:, h * latent : (h + 1) * latent], q_ref[:, side + h * rope : side + (h + 1) * rope]], axis=1
        )
        scores = lax.dot_general(
            query, keys_ref[...], (((1,), (1,)), ((), ())), preferred_element_type=F32
        ) * ((V + ROPE) ** (-0.5))
        scores = jnp.where(live, scores, NEG)
        shift = jnp.max(scores, axis=1, keepdims=True).astype(BF16).astype(F32)
        weights = jnp.where(live, jnp.exp(scores - shift), 0.0).astype(BF16)
        total = jnp.sum(weights.astype(F32), axis=1, keepdims=True)
        outs = jnp.dot(weights, keys_ref[:, :latent], preferred_element_type=F32)
        state_ref[:, h * latent : (h + 1) * latent] = outs.astype(BF16)
        high = total.astype(BF16).astype(F32)
        for k, value in enumerate((shift, high, total - high)):
            stats = jnp.where(lane == 3 * h + k, value, stats)
    state_ref[:, side:] = stats.astype(BF16)
    for copy in copies:
        copy.wait()


def project_kernel(rows, heads, latent, state_ref, w_uv_ref, w_out_ref, term_ref):
    count = state_ref.shape[0]
    mixed = rows * heads
    side = heads * latent
    lane = lax.broadcasted_iota(jnp.int32, (count, LANES), 1)
    row = lax.broadcasted_iota(jnp.int32, (count, LANES), 0) % rows
    column = lane % mixed
    own = (column // heads == row) & (lane < 2 * mixed)
    stats = state_ref[:, side:].astype(F32)
    shift = jnp.full((count, LANES), 2 * NEG, F32)
    for h in range(heads):
        shift = jnp.where(own & (column % heads == h), stats[:, 3 * h : 3 * h + 1], shift)
    best = jnp.max(shift, axis=0, keepdims=True)
    factor = jnp.where(own, jnp.exp(shift - best), 0.0)
    high = factor.astype(BF16).astype(F32)
    factor = jnp.where(lane < mixed, high, factor - high).astype(BF16)
    merged = lax.dot_general(
        factor, state_ref[...], (((0,), (0,)), ((), ())), preferred_element_type=F32
    )
    merged = merged[:mixed] + merged[mixed : 2 * mixed]
    parts = []
    for h in range(heads):
        total = merged[:, side + 3 * h + 1 : side + 3 * h + 2] + merged[:, side + 3 * h + 2 : side + 3 * h + 3]
        attended = (merged[:, h * latent : (h + 1) * latent] / total).astype(BF16)
        parts.append(jnp.dot(attended, w_uv_ref[h], preferred_element_type=F32))
    flat = jnp.concatenate(
        [
            jnp.concatenate([parts[h][r * heads + h : r * heads + h + 1] for h in range(heads)], axis=1)
            for r in range(rows)
        ],
        axis=0,
    ).astype(BF16)
    term_ref[...] = jnp.dot(flat, w_out_ref[...], preferred_element_type=F32).astype(term_ref.dtype)


def local(q_latent, q_rope, latent_cache, page_table, lengths, w_uv, w_out):
    rows, heads, latent = q_latent.shape
    rope = q_rope.shape[2]
    pages, page_len, width = latent_cache.shape
    tokens = pages * page_len
    count = lax.axis_size(CTX)
    size = heads * (latent + rope)
    vmem = pl.BlockSpec(memory_space=pltpu.VMEM)
    smem = pl.BlockSpec(memory_space=pltpu.SMEM)
    hbm = pl.BlockSpec(memory_space=pl.ANY)
    stay = functools.partial(pltpu.with_memory_space_constraint, memory_space=pltpu.HBM)
    params = pltpu.CompilerParams(vmem_limit_bytes=16 << 20)
    dma = pltpu.SemaphoreType.DMA

    here = lax.axis_index(CTX).reshape(1).astype(jnp.int32)
    query, live, keys = pl.pallas_call(
        functools.partial(prepare_kernel, page_len),
        out_shape=(
            jax.ShapeDtypeStruct((count, rows, size), BF16),
            pltpu.VMEM((rows, tokens), F32),
            pltpu.VMEM((tokens, width), BF16),
        ),
        in_specs=[smem, hbm, hbm, hbm, hbm, hbm],
        out_specs=(vmem, vmem, vmem),
        scratch_shapes=[
            pltpu.SMEM(lengths.shape, jnp.int32),
            pltpu.VMEM(page_table.shape, jnp.int32),
            pltpu.VMEM(q_latent.shape, BF16),
            pltpu.VMEM(q_rope.shape, BF16),
            dma((5,)),
        ],
        compiler_params=params,
        name="prepare",
    )(here, stay(lengths), stay(page_table), stay(q_latent), stay(q_rope), stay(latent_cache.reshape(tokens, width)))

    query = lax.all_to_all(query, CTX, split_axis=0, concat_axis=0, tiled=True)

    state_size = heads * latent + LANES
    state, w_uv, w_out = pl.pallas_call(
        functools.partial(attend_kernel, rows, heads, latent, rope),
        out_shape=(
            jax.ShapeDtypeStruct((count * rows, state_size), BF16),
            pltpu.VMEM(w_uv.shape, BF16),
            pltpu.VMEM(w_out.shape, BF16),
        ),
        in_specs=[vmem, vmem, vmem, hbm, hbm],
        out_specs=(vmem, vmem, vmem),
        scratch_shapes=[dma((2,))],
        compiler_params=params,
        name="attend",
    )(query.reshape(count * rows, size), keys, live, stay(w_uv), stay(w_out))

    state = lax.all_to_all(
        state.reshape(count, rows, state_size), CTX, split_axis=0, concat_axis=0, tiled=True
    )
    term = pl.pallas_call(
        functools.partial(project_kernel, rows, heads, latent),
        out_shape=jax.ShapeDtypeStruct((rows, w_out.shape[1]), BF16),
        in_specs=[vmem, vmem, vmem],
        out_specs=vmem,
        compiler_params=params,
        name="project",
    )(state.reshape(count * rows, state_size), w_uv, w_out)
    for low in (4, 2, 0):
        term = sum_of_four(term, count, low).astype(BF16)
    return term


def solution(mesh):
    in_specs = (
        P("grp", "ctx", None),
        P("grp", "ctx", None),
        P(("grp", "ctx"), None, None),
        P("grp", None),
        P("grp"),
        P("ctx", None, None),
        P("ctx", None),
    )
    return jax.shard_map(local, mesh=mesh, in_specs=in_specs, out_specs=P("grp", None), check_vma=False)
```

```python
import functools
import jax
import jax.numpy as jnp
from jax import lax
from jax.experimental import pallas as pl
from jax.experimental.pallas import tpu as pltpu
from jax.sharding import PartitionSpec as P

ROPE = 64
V = 128
NEG = -1e30
CTX = "ctx"
LANES = 128
F32 = jnp.float32
BF16 = jnp.bfloat16


def xor_pairs(count, mask):
    return [(i, i ^ mask) for i in range(count)]


def sum_of_four(x, count, low):
    a, b, c = (lax.ppermute(x, CTX, xor_pairs(count, k << low)) for k in (1, 2, 3))
    return (x.astype(F32) + a.astype(F32)) + (b.astype(F32) + c.astype(F32))


def message_kernel(q_latent_hbm, q_rope_hbm, message_ref, q_latent_ref, q_rope_ref, sems):
    copies = [
        pltpu.make_async_copy(q_latent_hbm, q_latent_ref, sems.at[0]),
        pltpu.make_async_copy(q_rope_hbm, q_rope_ref, sems.at[1]),
    ]
    for copy in copies:
        copy.start()
    for copy in copies:
        copy.wait()
    rows, heads, _ = q_latent_ref.shape
    q_latent = q_latent_ref[...].astype(F32)
    q_rope = q_rope_ref[...].astype(F32)
    message = [
        jnp.concatenate(
            [q_latent[r, h : h + 1] for h in range(heads)] + [q_rope[r, h : h + 1] for h in range(heads)],
            axis=1,
        )
        for r in range(rows)
    ]
    message_ref[...] = jnp.concatenate(message, axis=0).astype(BF16)


def fetch_kernel(
    page_len, here_ref, lengths_hbm, table_hbm, cache_hbm, w_uv_hbm, w_out_hbm,
    live_ref, keys_ref, w_uv_ref, *rest,
):
    *w_out_refs, lengths_ref, table_ref, sems = rest
    columns = w_out_refs[0].shape[1]
    pairs = [
        (lengths_hbm, lengths_ref), (table_hbm, table_ref), (cache_hbm, keys_ref), (w_uv_hbm, w_uv_ref),
    ]
    for k, ref in enumerate(w_out_refs):
        pairs.append((w_out_hbm.at[:, k * columns : (k + 1) * columns], ref))
    copies = [pltpu.make_async_copy(a, b, sems.at[k]) for k, (a, b) in enumerate(pairs)]
    for copy in copies:
        copy.start()
    copies[0].wait()
    copies[1].wait()
    rows = live_ref.shape[0]
    tokens = keys_ref.shape[0]
    pages = tokens // page_len
    slots = table_ref.shape[1]
    page = here_ref[0] * pages + lax.broadcasted_iota(jnp.int32, (pages, slots), 0)
    place = lax.broadcasted_iota(jnp.int32, (pages, slots), 1)
    token = lax.broadcasted_iota(jnp.int32, (pages, tokens), 1)
    mine = token // page_len == lax.broadcasted_iota(jnp.int32, (pages, tokens), 0)
    for r in range(rows):
        hit = jnp.broadcast_to(table_ref[r : r + 1, :], (pages, slots)) == page
        room = jnp.where(hit, lengths_ref[r] - place * page_len, 0)
        room = jnp.max(room, axis=1, keepdims=True)
        alive = mine & (token % page_len < room)
        live_ref[r : r + 1, :] = jnp.max(jnp.where(alive, 1.0, 0.0), axis=0, keepdims=True)
    for copy in copies[2:]:
        copy.wait()


def attend_kernel(rows, heads, latent, rope, q_ref, keys_ref, live_ref, state_ref):
    count = q_ref.shape[0]
    tokens = keys_ref.shape[0]
    row = lax.broadcasted_iota(jnp.int32, (count, 1), 0) % rows
    live = jnp.broadcast_to(live_ref[0:1, :], (count, tokens))
    for r in range(1, rows):
        live = jnp.where(row == r, live_ref[r : r + 1, :], live)
    live = live > 0.5
    side = heads * latent
    lane = lax.broadcasted_iota(jnp.int32, (count, state_ref.shape[1] - side), 1)
    stats = jnp.zeros(lane.shape, F32)
    for h in range(heads):
        query = jnp.concatenate(
            [q_ref[:, h * latent : (h + 1) * latent], q_ref[:, side + h * rope : side + (h + 1) * rope]], axis=1
        )
        scores = lax.dot_general(
            query, keys_ref[...], (((1,), (1,)), ((), ())), preferred_element_type=F32
        ) * ((V + ROPE) ** (-0.5))
        scores = jnp.where(live, scores, NEG)
        shift = jnp.max(scores, axis=1, keepdims=True).astype(BF16).astype(F32)
        weights = jnp.where(live, jnp.exp(scores - shift), 0.0).astype(BF16)
        total = jnp.sum(weights.astype(F32), axis=1, keepdims=True)
        outs = jnp.dot(weights, keys_ref[:, :latent], preferred_element_type=F32)
        state_ref[:, h * latent : (h + 1) * latent] = outs.astype(BF16)
        high = total.astype(BF16).astype(F32)
        for k, value in enumerate((shift, high, total - high)):
            stats = jnp.where(lane == 3 * h + k, value, stats)
    state_ref[:, side:] = stats.astype(BF16)


def project_kernel(rows, heads, latent, state_ref, w_uv_ref, *rest):
    *w_out_refs, term_ref = rest
    count = state_ref.shape[0]
    mixed = rows * heads
    side = heads * latent
    lane = lax.broadcasted_iota(jnp.int32, (count, LANES), 1)
    row = lax.broadcasted_iota(jnp.int32, (count, LANES), 0) % rows
    column = lane % mixed
    own = (column // heads == row) & (lane < 2 * mixed)
    stats = state_ref[:, side:].astype(F32)
    shift = jnp.full((count, LANES), 2 * NEG, F32)
    for h in range(heads):
        shift = jnp.where(own & (column % heads == h), stats[:, 3 * h : 3 * h + 1], shift)
    best = jnp.max(shift, axis=0, keepdims=True)
    factor = jnp.where(own, jnp.exp(shift - best), 0.0)
    high = factor.astype(BF16).astype(F32)
    factor = jnp.where(lane < mixed, high, factor - high).astype(BF16)
    merged = lax.dot_general(
        factor, state_ref[...], (((0,), (0,)), ((), ())), preferred_element_type=F32
    )
    merged = merged[:mixed] + merged[mixed : 2 * mixed]
    parts = []
    for h in range(heads):
        total = merged[:, side + 3 * h + 1 : side + 3 * h + 2] + merged[:, side + 3 * h + 2 : side + 3 * h + 3]
        attended = (merged[:, h * latent : (h + 1) * latent] / total).astype(BF16)
        parts.append(jnp.dot(attended, w_uv_ref[h], preferred_element_type=F32))
    flat = jnp.concatenate(
        [
            jnp.concatenate([parts[h][r * heads + h : r * heads + h + 1] for h in range(heads)], axis=1)
            for r in range(rows)
        ],
        axis=0,
    ).astype(BF16)
    columns = w_out_refs[0].shape[1]
    for k, ref in enumerate(w_out_refs):
        term_ref[:, k * columns : (k + 1) * columns] = jnp.dot(
            flat, ref[...], preferred_element_type=F32
        ).astype(term_ref.dtype)


def local(q_latent, q_rope, latent_cache, page_table, lengths, w_uv, w_out):
    rows, heads, latent = q_latent.shape
    rope = q_rope.shape[2]
    pages, page_len, width = latent_cache.shape
    tokens = pages * page_len
    count = lax.axis_size(CTX)
    size = heads * (latent + rope)
    vmem = pl.BlockSpec(memory_space=pltpu.VMEM)
    smem = pl.BlockSpec(memory_space=pltpu.SMEM)
    hbm = pl.BlockSpec(memory_space=pl.ANY)
    stay = functools.partial(pltpu.with_memory_space_constraint, memory_space=pltpu.HBM)
    params = pltpu.CompilerParams(vmem_limit_bytes=16 << 20)
    dma = pltpu.SemaphoreType.DMA
    here = lax.axis_index(CTX).astype(jnp.int32)

    message = pl.pallas_call(
        message_kernel,
        out_shape=jax.ShapeDtypeStruct((rows, size), BF16),
        in_specs=[hbm, hbm],
        out_specs=vmem,
        scratch_shapes=[pltpu.VMEM(q_latent.shape, BF16), pltpu.VMEM(q_rope.shape, BF16), dma((2,))],
        compiler_params=params,
        name="message",
    )(stay(q_latent), stay(q_rope))

    near = 4
    others = [lax.ppermute(message, CTX, xor_pairs(count, k)) for k in range(1, near)]
    parts = w_out.shape[1] // 1024
    live, keys, w_uv, *w_outs = pl.pallas_call(
        functools.partial(fetch_kernel, page_len),
        out_shape=(
            pltpu.VMEM((rows, tokens), F32),
            pltpu.VMEM((tokens, width), BF16),
            pltpu.VMEM(w_uv.shape, BF16),
            *[pltpu.VMEM((w_out.shape[0], w_out.shape[1] // parts), BF16) for _ in range(parts)],
        ),
        in_specs=[smem, hbm, hbm, hbm, hbm, hbm],
        out_specs=(vmem,) * (3 + parts),
        scratch_shapes=[
            pltpu.SMEM(lengths.shape, jnp.int32), pltpu.VMEM(page_table.shape, jnp.int32), dma((4 + parts,)),
        ],
        compiler_params=params,
        cost_estimate=pl.CostEstimate(flops=0, bytes_accessed=9 << 20, transcendentals=0),
        name="fetch",
    )(
        here.reshape(1), stay(lengths), stay(page_table), stay(latent_cache.reshape(tokens, width)),
        stay(w_uv), stay(w_out),
    )
    away = lax.broadcasted_iota(jnp.int32, (near, 1, 1), 0) ^ (here % near)
    column = jnp.broadcast_to(message[None], (near, rows, size))
    for k in range(1, near):
        column = jnp.where(away == k, others[k - 1][None], column)
    planes = [[i * near + k for i in range(count // near)] for k in range(near)]
    query = lax.all_to_all(
        jnp.broadcast_to(column[None], (count // near, near, rows, size)),
        CTX, split_axis=0, concat_axis=0, axis_index_groups=planes, tiled=True,
    )

    state_size = heads * latent + LANES
    state = pl.pallas_call(
        functools.partial(attend_kernel, rows, heads, latent, rope),
        out_shape=jax.ShapeDtypeStruct((count * rows, state_size), BF16),
        in_specs=[vmem, vmem, vmem],
        out_specs=vmem,
        compiler_params=params,
        name="attend",
    )(query.reshape(count * rows, size), keys, live)

    state = lax.all_to_all(
        state.reshape(count, rows, state_size), CTX, split_axis=0, concat_axis=0, tiled=True
    )
    term = pl.pallas_call(
        functools.partial(project_kernel, rows, heads, latent),
        out_shape=jax.ShapeDtypeStruct((rows, w_out.shape[1]), BF16),
        in_specs=[vmem] * (2 + parts),
        out_specs=vmem,
        compiler_params=params,
        name="project",
    )(state.reshape(count * rows, state_size), w_uv, *w_outs)
    for low in (4, 2, 0):
        term = sum_of_four(term, count, low).astype(BF16)
    return term


def solution(mesh):
    in_specs = (
        P("grp", "ctx", None),
        P("grp", "ctx", None),
        P(("grp", "ctx"), None, None),
        P("grp", None),
        P("grp"),
        P("ctx", None, None),
        P("ctx", None),
    )
    return jax.shard_map(local, mesh=mesh, in_specs=in_specs, out_specs=P("grp", None), check_vma=False)
```

```python
import functools
import jax
import jax.numpy as jnp
from jax import lax
from jax.experimental import pallas as pl
from jax.experimental.pallas import tpu as pltpu
from jax.sharding import PartitionSpec as P

ROPE = 64
V = 128
NEG = -1e30
CTX = "ctx"
LANES = 128
F32 = jnp.float32
BF16 = jnp.bfloat16


def xor_pairs(count, mask):
    return [(i, i ^ mask) for i in range(count)]


def sum_of_four(x, count, low):
    a, b, c = (lax.ppermute(x, CTX, xor_pairs(count, k << low)) for k in (1, 2, 3))
    return (x.astype(F32) + a.astype(F32)) + (b.astype(F32) + c.astype(F32))


def message_kernel(q_latent_hbm, q_rope_hbm, message_ref, q_latent_ref, q_rope_ref, sems):
    copies = [
        pltpu.make_async_copy(q_latent_hbm, q_latent_ref, sems.at[0]),
        pltpu.make_async_copy(q_rope_hbm, q_rope_ref, sems.at[1]),
    ]
    for copy in copies:
        copy.start()
    for copy in copies:
        copy.wait()
    rows, heads, _ = q_latent_ref.shape
    q_latent = q_latent_ref[...].astype(F32)
    q_rope = q_rope_ref[...].astype(F32)
    message = [
        jnp.concatenate(
            [q_latent[r, h : h + 1] for h in range(heads)] + [q_rope[r, h : h + 1] for h in range(heads)],
            axis=1,
        )
        for r in range(rows)
    ]
    message_ref[...] = jnp.concatenate(message, axis=0).astype(BF16)


def fetch_kernel(
    page_len, here_ref, lengths_hbm, table_hbm, cache_hbm, live_ref, keys_ref, lengths_ref, table_ref, sems
):
    pairs = [(lengths_hbm, lengths_ref), (table_hbm, table_ref), (cache_hbm, keys_ref)]
    copies = [pltpu.make_async_copy(a, b, sems.at[k]) for k, (a, b) in enumerate(pairs)]
    for copy in copies:
        copy.start()
    copies[0].wait()
    copies[1].wait()
    rows = live_ref.shape[0]
    tokens = keys_ref.shape[0]
    pages = tokens // page_len
    slots = table_ref.shape[1]
    page = here_ref[0] * pages + lax.broadcasted_iota(jnp.int32, (pages, slots), 0)
    place = lax.broadcasted_iota(jnp.int32, (pages, slots), 1)
    token = lax.broadcasted_iota(jnp.int32, (pages, tokens), 1)
    mine = token // page_len == lax.broadcasted_iota(jnp.int32, (pages, tokens), 0)
    for r in range(rows):
        hit = jnp.broadcast_to(table_ref[r : r + 1, :], (pages, slots)) == page
        room = jnp.where(hit, lengths_ref[r] - place * page_len, 0)
        room = jnp.max(room, axis=1, keepdims=True)
        alive = mine & (token % page_len < room)
        live_ref[r : r + 1, :] = jnp.max(jnp.where(alive, 1.0, 0.0), axis=0, keepdims=True)
    copies[2].wait()


def attend_kernel(
    rows, heads, latent, rope, q_ref, keys_ref, live_ref, w_uv_hbm, w_out_hbm,
    state_ref, w_uv_ref, w_out_ref, sems,
):
    copies = [
        pltpu.make_async_copy(w_uv_hbm, w_uv_ref, sems.at[0]),
        pltpu.make_async_copy(w_out_hbm.at[:, : w_out_ref.shape[1]], w_out_ref, sems.at[1]),
    ]
    for copy in copies:
        copy.start()
    count = q_ref.shape[0]
    tokens = keys_ref.shape[0]
    row = lax.broadcasted_iota(jnp.int32, (count, 1), 0) % rows
    live = jnp.broadcast_to(live_ref[0:1, :], (count, tokens))
    for r in range(1, rows):
        live = jnp.where(row == r, live_ref[r : r + 1, :], live)
    live = live > 0.5
    side = heads * latent
    lane = lax.broadcasted_iota(jnp.int32, (count, state_ref.shape[1] - side), 1)
    stats = jnp.zeros(lane.shape, F32)
    for h in range(heads):
        query = jnp.concatenate(
            [q_ref[:, h * latent : (h + 1) * latent], q_ref[:, side + h * rope : side + (h + 1) * rope]], axis=1
        )
        scores = lax.dot_general(
            query, keys_ref[...], (((1,), (1,)), ((), ())), preferred_element_type=F32
        ) * ((V + ROPE) ** (-0.5))
        scores = jnp.where(live, scores, NEG)
        shift = jnp.max(scores, axis=1, keepdims=True).astype(BF16).astype(F32)
        weights = jnp.where(live, jnp.exp(scores - shift), 0.0).astype(BF16)
        total = jnp.sum(weights.astype(F32), axis=1, keepdims=True)
        outs = jnp.dot(weights, keys_ref[:, :latent], preferred_element_type=F32)
        state_ref[:, h * latent : (h + 1) * latent] = outs.astype(BF16)
        high = total.astype(BF16).astype(F32)
        for k, value in enumerate((shift, high, total - high)):
            stats = jnp.where(lane == 3 * h + k, value, stats)
    state_ref[:, side:] = stats.astype(BF16)
    for copy in copies:
        copy.wait()


def project_kernel(rows, heads, latent, state_ref, w_uv_ref, first_ref, w_out_hbm, term_ref, second_ref, sem):
    split = first_ref.shape[1]
    copy = pltpu.make_async_copy(w_out_hbm.at[:, split:], second_ref, sem)
    copy.start()
    count = state_ref.shape[0]
    mixed = rows * heads
    side = heads * latent
    lane = lax.broadcasted_iota(jnp.int32, (count, LANES), 1)
    row = lax.broadcasted_iota(jnp.int32, (count, LANES), 0) % rows
    column = lane % mixed
    own = (column // heads == row) & (lane < 2 * mixed)
    stats = state_ref[:, side:].astype(F32)
    shift = jnp.full((count, LANES), 2 * NEG, F32)
    for h in range(heads):
        shift = jnp.where(own & (column % heads == h), stats[:, 3 * h : 3 * h + 1], shift)
    best = jnp.max(shift, axis=0, keepdims=True)
    factor = jnp.where(own, jnp.exp(shift - best), 0.0)
    high = factor.astype(BF16).astype(F32)
    factor = jnp.where(lane < mixed, high, factor - high).astype(BF16)
    merged = lax.dot_general(
        factor, state_ref[...], (((0,), (0,)), ((), ())), preferred_element_type=F32
    )
    merged = merged[:mixed] + merged[mixed : 2 * mixed]
    parts = []
    for h in range(heads):
        total = merged[:, side + 3 * h + 1 : side + 3 * h + 2] + merged[:, side + 3 * h + 2 : side + 3 * h + 3]
        attended = (merged[:, h * latent : (h + 1) * latent] / total).astype(BF16)
        parts.append(jnp.dot(attended, w_uv_ref[h], preferred_element_type=F32))
    flat = jnp.concatenate(
        [
            jnp.concatenate([parts[h][r * heads + h : r * heads + h + 1] for h in range(heads)], axis=1)
            for r in range(rows)
        ],
        axis=0,
    ).astype(BF16)
    term_ref[:, :split] = jnp.dot(flat, first_ref[...], preferred_element_type=F32).astype(term_ref.dtype)
    copy.wait()
    term_ref[:, split:] = jnp.dot(flat, second_ref[...], preferred_element_type=F32).astype(term_ref.dtype)


def local(q_latent, q_rope, latent_cache, page_table, lengths, w_uv, w_out):
    rows, heads, latent = q_latent.shape
    rope = q_rope.shape[2]
    pages, page_len, width = latent_cache.shape
    tokens = pages * page_len
    count = lax.axis_size(CTX)
    size = heads * (latent + rope)
    vmem = pl.BlockSpec(memory_space=pltpu.VMEM)
    smem = pl.BlockSpec(memory_space=pltpu.SMEM)
    hbm = pl.BlockSpec(memory_space=pl.ANY)
    stay = functools.partial(pltpu.with_memory_space_constraint, memory_space=pltpu.HBM)
    params = pltpu.CompilerParams(vmem_limit_bytes=16 << 20)
    dma = pltpu.SemaphoreType.DMA
    here = lax.axis_index(CTX).astype(jnp.int32)

    message = pl.pallas_call(
        message_kernel,
        out_shape=jax.ShapeDtypeStruct((rows, size), BF16),
        in_specs=[hbm, hbm],
        out_specs=vmem,
        scratch_shapes=[pltpu.VMEM(q_latent.shape, BF16), pltpu.VMEM(q_rope.shape, BF16), dma((2,))],
        compiler_params=params,
        name="message",
    )(stay(q_latent), stay(q_rope))

    near = 4
    others = [lax.ppermute(message, CTX, xor_pairs(count, k)) for k in range(1, near)]
    live, keys = pl.pallas_call(
        functools.partial(fetch_kernel, page_len),
        out_shape=(
            pltpu.VMEM((rows, tokens), F32),
            pltpu.VMEM((tokens, width), BF16),
        ),
        in_specs=[smem, hbm, hbm, hbm],
        out_specs=(vmem, vmem),
        scratch_shapes=[
            pltpu.SMEM(lengths.shape, jnp.int32), pltpu.VMEM(page_table.shape, jnp.int32), dma((3,)),
        ],
        compiler_params=params,
        cost_estimate=pl.CostEstimate(flops=0, bytes_accessed=2 << 20, transcendentals=0),
        name="fetch",
    )(
        here.reshape(1), stay(lengths), stay(page_table), stay(latent_cache.reshape(tokens, width)),
    )
    away = lax.broadcasted_iota(jnp.int32, (near, 1, 1), 0) ^ (here % near)
    column = jnp.broadcast_to(message[None], (near, rows, size))
    for k in range(1, near):
        column = jnp.where(away == k, others[k - 1][None], column)
    column, live, keys = lax.optimization_barrier((column, live, keys))
    planes = [[i * near + k for i in range(count // near)] for k in range(near)]
    query = lax.all_to_all(
        jnp.broadcast_to(column[None], (count // near, near, rows, size)),
        CTX, split_axis=0, concat_axis=0, axis_index_groups=planes, tiled=True,
    )

    state_size = heads * latent + LANES
    split = w_out.shape[1] * 4 // 7 // LANES * LANES
    state, w_uv, w_first = pl.pallas_call(
        functools.partial(attend_kernel, rows, heads, latent, rope),
        out_shape=(
            jax.ShapeDtypeStruct((count * rows, state_size), BF16),
            pltpu.VMEM(w_uv.shape, BF16),
            pltpu.VMEM((w_out.shape[0], split), BF16),
        ),
        in_specs=[vmem, vmem, vmem, hbm, hbm],
        out_specs=(vmem, vmem, vmem),
        scratch_shapes=[dma((2,))],
        compiler_params=params,
        name="attend",
    )(query.reshape(count * rows, size), keys, live, stay(w_uv), stay(w_out))

    state = lax.all_to_all(
        state.reshape(count, rows, state_size), CTX, split_axis=0, concat_axis=0, tiled=True
    )
    term = pl.pallas_call(
        functools.partial(project_kernel, rows, heads, latent),
        out_shape=jax.ShapeDtypeStruct((rows, w_out.shape[1]), BF16),
        in_specs=[vmem, vmem, vmem, hbm],
        out_specs=vmem,
        scratch_shapes=[pltpu.VMEM((w_out.shape[0], w_out.shape[1] - split), BF16), dma],
        compiler_params=params,
        name="project",
    )(state.reshape(count * rows, state_size), w_uv, w_first, stay(w_out))
    for low in (4, 2, 0):
        term = sum_of_four(term, count, low).astype(BF16)
    return term


def solution(mesh):
    in_specs = (
        P("grp", "ctx", None),
        P("grp", "ctx", None),
        P(("grp", "ctx"), None, None),
        P("grp", None),
        P("grp"),
        P("ctx", None, None),
        P("ctx", None),
    )
    return jax.shard_map(local, mesh=mesh, in_specs=in_specs, out_specs=P("grp", None), check_vma=False)
```

```python
import functools
import jax
import jax.numpy as jnp
from jax import lax
from jax.experimental import pallas as pl
from jax.experimental.pallas import tpu as pltpu
from jax.sharding import PartitionSpec as P

ROPE = 64
V = 128
NEG = -1e30
CTX = "ctx"
LANES = 128
F32 = jnp.float32
BF16 = jnp.bfloat16


def xor_pairs(count, mask):
    return [(i, i ^ mask) for i in range(count)]


def sum_of_four(x, count, low):
    a, b, c = (lax.ppermute(x, CTX, xor_pairs(count, k << low)) for k in (1, 2, 3))
    return (x.astype(F32) + a.astype(F32)) + (b.astype(F32) + c.astype(F32))


def message_kernel(q_latent_hbm, q_rope_hbm, message_ref, q_latent_ref, q_rope_ref, sems):
    copies = [
        pltpu.make_async_copy(q_latent_hbm, q_latent_ref, sems.at[0]),
        pltpu.make_async_copy(q_rope_hbm, q_rope_ref, sems.at[1]),
    ]
    for copy in copies:
        copy.start()
    for copy in copies:
        copy.wait()
    rows, heads, _ = q_latent_ref.shape
    q_latent = q_latent_ref[...].astype(F32)
    q_rope = q_rope_ref[...].astype(F32)
    message = [
        jnp.concatenate(
            [q_latent[r, h : h + 1] for h in range(heads)] + [q_rope[r, h : h + 1] for h in range(heads)],
            axis=1,
        )
        for r in range(rows)
    ]
    message_ref[...] = jnp.concatenate(message, axis=0).astype(BF16)


def fetch_kernel(
    page_len, here_ref, lengths_hbm, table_hbm, cache_hbm, live_ref, keys_ref, lengths_ref, table_ref, sems
):
    pairs = [(lengths_hbm, lengths_ref), (table_hbm, table_ref), (cache_hbm, keys_ref)]
    copies = [pltpu.make_async_copy(a, b, sems.at[k]) for k, (a, b) in enumerate(pairs)]
    for copy in copies:
        copy.start()
    copies[0].wait()
    copies[1].wait()
    rows = live_ref.shape[0]
    tokens = keys_ref.shape[0]
    pages = tokens // page_len
    slots = table_ref.shape[1]
    page = here_ref[0] * pages + lax.broadcasted_iota(jnp.int32, (pages, slots), 0)
    place = lax.broadcasted_iota(jnp.int32, (pages, slots), 1)
    token = lax.broadcasted_iota(jnp.int32, (pages, tokens), 1)
    mine = token // page_len == lax.broadcasted_iota(jnp.int32, (pages, tokens), 0)
    for r in range(rows):
        hit = jnp.broadcast_to(table_ref[r : r + 1, :], (pages, slots)) == page
        room = jnp.where(hit, lengths_ref[r] - place * page_len, 0)
        room = jnp.max(room, axis=1, keepdims=True)
        alive = mine & (token % page_len < room)
        live_ref[r : r + 1, :] = jnp.max(jnp.where(alive, 1.0, 0.0), axis=0, keepdims=True)
    copies[2].wait()


def attend_kernel(
    rows, heads, latent, rope, q_ref, keys_ref, live_ref, w_out_hbm, state_ref, w_out_ref, sem
):
    copy = pltpu.make_async_copy(w_out_hbm.at[:, : w_out_ref.shape[1]], w_out_ref, sem)
    copy.start()
    count = q_ref.shape[0]
    tokens = keys_ref.shape[0]
    row = lax.broadcasted_iota(jnp.int32, (count, 1), 0) % rows
    live = jnp.broadcast_to(live_ref[0:1, :], (count, tokens))
    for r in range(1, rows):
        live = jnp.where(row == r, live_ref[r : r + 1, :], live)
    live = live > 0.5
    side = heads * latent
    lane = lax.broadcasted_iota(jnp.int32, (count, state_ref.shape[1] - side), 1)
    stats = jnp.zeros(lane.shape, F32)
    for h in range(heads):
        query = jnp.concatenate(
            [q_ref[:, h * latent : (h + 1) * latent], q_ref[:, side + h * rope : side + (h + 1) * rope]], axis=1
        )
        scores = lax.dot_general(
            query, keys_ref[...], (((1,), (1,)), ((), ())), preferred_element_type=F32
        ) * ((V + ROPE) ** (-0.5))
        scores = jnp.where(live, scores, NEG)
        shift = jnp.max(scores, axis=1, keepdims=True).astype(BF16).astype(F32)
        weights = jnp.where(live, jnp.exp(scores - shift), 0.0).astype(BF16)
        total = jnp.sum(weights.astype(F32), axis=1, keepdims=True)
        outs = jnp.dot(weights, keys_ref[:, :latent], preferred_element_type=F32)
        state_ref[:, h * latent : (h + 1) * latent] = outs.astype(BF16)
        high = total.astype(BF16).astype(F32)
        for k, value in enumerate((shift, high, total - high)):
            stats = jnp.where(lane == 3 * h + k, value, stats)
    state_ref[:, side:] = stats.astype(BF16)
    copy.wait()


def project_kernel(
    rows, heads, latent, state_ref, first_ref, w_uv_hbm, w_out_hbm, term_ref, w_uv_ref, second_ref, sems
):
    split = first_ref.shape[1]
    copies = [
        pltpu.make_async_copy(w_uv_hbm, w_uv_ref, sems.at[0]),
        pltpu.make_async_copy(w_out_hbm.at[:, split:], second_ref, sems.at[1]),
    ]
    for copy in copies:
        copy.start()
    count = state_ref.shape[0]
    mixed = rows * heads
    side = heads * latent
    lane = lax.broadcasted_iota(jnp.int32, (count, LANES), 1)
    row = lax.broadcasted_iota(jnp.int32, (count, LANES), 0) % rows
    column = lane % mixed
    own = (column // heads == row) & (lane < 2 * mixed)
    stats = state_ref[:, side:].astype(F32)
    shift = jnp.full((count, LANES), 2 * NEG, F32)
    for h in range(heads):
        shift = jnp.where(own & (column % heads == h), stats[:, 3 * h : 3 * h + 1], shift)
    best = jnp.max(shift, axis=0, keepdims=True)
    factor = jnp.where(own, jnp.exp(shift - best), 0.0)
    high = factor.astype(BF16).astype(F32)
    factor = jnp.where(lane < mixed, high, factor - high).astype(BF16)
    merged = lax.dot_general(
        factor, state_ref[...], (((0,), (0,)), ((), ())), preferred_element_type=F32
    )
    merged = merged[:mixed] + merged[mixed : 2 * mixed]
    copies[0].wait()
    parts = []
    for h in range(heads):
        total = merged[:, side + 3 * h + 1 : side + 3 * h + 2] + merged[:, side + 3 * h + 2 : side + 3 * h + 3]
        attended = (merged[:, h * latent : (h + 1) * latent] / total).astype(BF16)
        parts.append(jnp.dot(attended, w_uv_ref[h], preferred_element_type=F32))
    flat = jnp.concatenate(
        [
            jnp.concatenate([parts[h][r * heads + h : r * heads + h + 1] for h in range(heads)], axis=1)
            for r in range(rows)
        ],
        axis=0,
    ).astype(BF16)
    term_ref[:, :split] = jnp.dot(flat, first_ref[...], preferred_element_type=F32).astype(term_ref.dtype)
    copies[1].wait()
    term_ref[:, split:] = jnp.dot(flat, second_ref[...], preferred_element_type=F32).astype(term_ref.dtype)


def local(q_latent, q_rope, latent_cache, page_table, lengths, w_uv, w_out):
    rows, heads, latent = q_latent.shape
    rope = q_rope.shape[2]
    pages, page_len, width = latent_cache.shape
    tokens = pages * page_len
    count = lax.axis_size(CTX)
    size = heads * (latent + rope)
    vmem = pl.BlockSpec(memory_space=pltpu.VMEM)
    smem = pl.BlockSpec(memory_space=pltpu.SMEM)
    hbm = pl.BlockSpec(memory_space=pl.ANY)
    stay = functools.partial(pltpu.with_memory_space_constraint, memory_space=pltpu.HBM)
    params = pltpu.CompilerParams(vmem_limit_bytes=16 << 20)
    dma = pltpu.SemaphoreType.DMA
    here = lax.axis_index(CTX).astype(jnp.int32)

    message = pl.pallas_call(
        message_kernel,
        out_shape=jax.ShapeDtypeStruct((rows, size), BF16),
        in_specs=[hbm, hbm],
        out_specs=vmem,
        scratch_shapes=[pltpu.VMEM(q_latent.shape, BF16), pltpu.VMEM(q_rope.shape, BF16), dma((2,))],
        compiler_params=params,
        name="message",
    )(stay(q_latent), stay(q_rope))

    near = 4
    others = [lax.ppermute(message, CTX, xor_pairs(count, k)) for k in range(1, near)]
    live, keys = pl.pallas_call(
        functools.partial(fetch_kernel, page_len),
        out_shape=(
            pltpu.VMEM((rows, tokens), F32),
            pltpu.VMEM((tokens, width), BF16),
        ),
        in_specs=[smem, hbm, hbm, hbm],
        out_specs=(vmem, vmem),
        scratch_shapes=[
            pltpu.SMEM(lengths.shape, jnp.int32), pltpu.VMEM(page_table.shape, jnp.int32), dma((3,)),
        ],
        compiler_params=params,
        cost_estimate=pl.CostEstimate(flops=0, bytes_accessed=2 << 20, transcendentals=0),
        name="fetch",
    )(
        here.reshape(1), stay(lengths), stay(page_table), stay(latent_cache.reshape(tokens, width)),
    )
    away = lax.broadcasted_iota(jnp.int32, (near, 1, 1), 0) ^ (here % near)
    column = jnp.broadcast_to(message[None], (near, rows, size))
    for k in range(1, near):
        column = jnp.where(away == k, others[k - 1][None], column)
    column, live, keys = lax.optimization_barrier((column, live, keys))
    planes = [[i * near + k for i in range(count // near)] for k in range(near)]
    query = lax.all_to_all(
        jnp.broadcast_to(column[None], (count // near, near, rows, size)),
        CTX, split_axis=0, concat_axis=0, axis_index_groups=planes, tiled=True,
    )

    state_size = heads * latent + LANES
    split = w_out.shape[1] * 5 // 7 // LANES * LANES
    state, w_first = pl.pallas_call(
        functools.partial(attend_kernel, rows, heads, latent, rope),
        out_shape=(
            jax.ShapeDtypeStruct((count * rows, state_size), BF16),
            pltpu.VMEM((w_out.shape[0], split), BF16),
        ),
        in_specs=[vmem, vmem, vmem, hbm],
        out_specs=(vmem, vmem),
        scratch_shapes=[dma],
        compiler_params=params,
        name="attend",
    )(query.reshape(count * rows, size), keys, live, stay(w_out))

    state = lax.all_to_all(
        state.reshape(count, rows, state_size), CTX, split_axis=0, concat_axis=0, tiled=True
    )
    term = pl.pallas_call(
        functools.partial(project_kernel, rows, heads, latent),
        out_shape=jax.ShapeDtypeStruct((rows, w_out.shape[1]), BF16),
        in_specs=[vmem, vmem, hbm, hbm],
        out_specs=vmem,
        scratch_shapes=[
            pltpu.VMEM(w_uv.shape, BF16), pltpu.VMEM((w_out.shape[0], w_out.shape[1] - split), BF16), dma((2,)),
        ],
        compiler_params=params,
        name="project",
    )(state.reshape(count * rows, state_size), w_first, stay(w_uv), stay(w_out))
    for low in (4, 2, 0):
        term = sum_of_four(term, count, low).astype(BF16)
    return term


def solution(mesh):
    in_specs = (
        P("grp", "ctx", None),
        P("grp", "ctx", None),
        P(("grp", "ctx"), None, None),
        P("grp", None),
        P("grp"),
        P("ctx", None, None),
        P("ctx", None),
    )
    return jax.shard_map(local, mesh=mesh, in_specs=in_specs, out_specs=P("grp", None), check_vma=False)
```

```python
import functools
import jax
import jax.numpy as jnp
from jax import lax
from jax.experimental import pallas as pl
from jax.experimental.pallas import tpu as pltpu
from jax.sharding import PartitionSpec as P

ROPE = 64
V = 128
NEG = -1e30
CTX = "ctx"
LANES = 128
F32 = jnp.float32
BF16 = jnp.bfloat16


def xor_pairs(count, mask):
    return [(i, i ^ mask) for i in range(count)]


def sum_of_four(x, count, low):
    a, b, c = (lax.ppermute(x, CTX, xor_pairs(count, k << low)) for k in (1, 2, 3))
    return (x.astype(F32) + a.astype(F32)) + (b.astype(F32) + c.astype(F32))


def message_kernel(q_latent_hbm, q_rope_hbm, message_ref, q_latent_ref, q_rope_ref, sems):
    copies = [
        pltpu.make_async_copy(q_latent_hbm, q_latent_ref, sems.at[0]),
        pltpu.make_async_copy(q_rope_hbm, q_rope_ref, sems.at[1]),
    ]
    for copy in copies:
        copy.start()
    for copy in copies:
        copy.wait()
    rows, heads, _ = q_latent_ref.shape
    q_latent = q_latent_ref[...].astype(F32)
    q_rope = q_rope_ref[...].astype(F32)
    message = [
        jnp.concatenate(
            [q_latent[r, h : h + 1] for h in range(heads)] + [q_rope[r, h : h + 1] for h in range(heads)],
            axis=1,
        )
        for r in range(rows)
    ]
    message_ref[...] = jnp.concatenate(message, axis=0).astype(BF16)


def fetch_kernel(
    page_len, here_ref, lengths_hbm, table_hbm, cache_hbm, w_uv_hbm, w_out_hbm,
    live_ref, keys_ref, w_uv_ref, w_out_ref, lengths_ref, table_ref, sems,
):
    pairs = [
        (lengths_hbm, lengths_ref), (table_hbm, table_ref), (cache_hbm, keys_ref), (w_uv_hbm, w_uv_ref),
        (w_out_hbm.at[:, : w_out_ref.shape[1]], w_out_ref),
    ]
    copies = [pltpu.make_async_copy(a, b, sems.at[k]) for k, (a, b) in enumerate(pairs)]
    for copy in copies:
        copy.start()
    copies[0].wait()
    copies[1].wait()
    rows = live_ref.shape[0]
    tokens = keys_ref.shape[0]
    pages = tokens // page_len
    slots = table_ref.shape[1]
    page = here_ref[0] * pages + lax.broadcasted_iota(jnp.int32, (pages, slots), 0)
    place = lax.broadcasted_iota(jnp.int32, (pages, slots), 1)
    token = lax.broadcasted_iota(jnp.int32, (pages, tokens), 1)
    mine = token // page_len == lax.broadcasted_iota(jnp.int32, (pages, tokens), 0)
    for r in range(rows):
        hit = jnp.broadcast_to(table_ref[r : r + 1, :], (pages, slots)) == page
        room = jnp.where(hit, lengths_ref[r] - place * page_len, 0)
        room = jnp.max(room, axis=1, keepdims=True)
        alive = mine & (token % page_len < room)
        live_ref[r : r + 1, :] = jnp.max(jnp.where(alive, 1.0, 0.0), axis=0, keepdims=True)
    for copy in copies[2:]:
        copy.wait()


def attend_kernel(rows, heads, latent, rope, q_ref, keys_ref, live_ref, state_ref):
    count = q_ref.shape[0]
    tokens = keys_ref.shape[0]
    row = lax.broadcasted_iota(jnp.int32, (count, 1), 0) % rows
    live = jnp.broadcast_to(live_ref[0:1, :], (count, tokens))
    for r in range(1, rows):
        live = jnp.where(row == r, live_ref[r : r + 1, :], live)
    live = live > 0.5
    side = heads * latent
    lane = lax.broadcasted_iota(jnp.int32, (count, state_ref.shape[1] - side), 1)
    stats = jnp.zeros(lane.shape, F32)
    for h in range(heads):
        query = jnp.concatenate(
            [q_ref[:, h * latent : (h + 1) * latent], q_ref[:, side + h * rope : side + (h + 1) * rope]], axis=1
        )
        scores = lax.dot_general(
            query, keys_ref[...], (((1,), (1,)), ((), ())), preferred_element_type=F32
        ) * ((V + ROPE) ** (-0.5))
        scores = jnp.where(live, scores, NEG)
        shift = jnp.max(scores, axis=1, keepdims=True).astype(BF16).astype(F32)
        weights = jnp.where(live, jnp.exp(scores - shift), 0.0).astype(BF16)
        total = jnp.sum(weights.astype(F32), axis=1, keepdims=True)
        outs = jnp.dot(weights, keys_ref[:, :latent], preferred_element_type=F32)
        state_ref[:, h * latent : (h + 1) * latent] = outs.astype(BF16)
        high = total.astype(BF16).astype(F32)
        for k, value in enumerate((shift, high, total - high)):
            stats = jnp.where(lane == 3 * h + k, value, stats)
    state_ref[:, side:] = stats.astype(BF16)


def project_kernel(rows, heads, latent, state_ref, w_uv_ref, first_ref, w_out_hbm, term_ref, second_ref, sem):
    split = first_ref.shape[1]
    copy = pltpu.make_async_copy(w_out_hbm.at[:, split:], second_ref, sem)
    copy.start()
    count = state_ref.shape[0]
    mixed = rows * heads
    side = heads * latent
    lane = lax.broadcasted_iota(jnp.int32, (count, LANES), 1)
    row = lax.broadcasted_iota(jnp.int32, (count, LANES), 0) % rows
    column = lane % mixed
    own = (column // heads == row) & (lane < 2 * mixed)
    stats = state_ref[:, side:].astype(F32)
    shift = jnp.full((count, LANES), 2 * NEG, F32)
    for h in range(heads):
        shift = jnp.where(own & (column % heads == h), stats[:, 3 * h : 3 * h + 1], shift)
    best = jnp.max(shift, axis=0, keepdims=True)
    factor = jnp.where(own, jnp.exp(shift - best), 0.0)
    high = factor.astype(BF16).astype(F32)
    factor = jnp.where(lane < mixed, high, factor - high).astype(BF16)
    merged = lax.dot_general(
        factor, state_ref[...], (((0,), (0,)), ((), ())), preferred_element_type=F32
    )
    merged = merged[:mixed] + merged[mixed : 2 * mixed]
    parts = []
    for h in range(heads):
        total = merged[:, side + 3 * h + 1 : side + 3 * h + 2] + merged[:, side + 3 * h + 2 : side + 3 * h + 3]
        attended = (merged[:, h * latent : (h + 1) * latent] / total).astype(BF16)
        parts.append(jnp.dot(attended, w_uv_ref[h], preferred_element_type=F32))
    flat = jnp.concatenate(
        [
            jnp.concatenate([parts[h][r * heads + h : r * heads + h + 1] for h in range(heads)], axis=1)
            for r in range(rows)
        ],
        axis=0,
    ).astype(BF16)
    term_ref[:, :split] = jnp.dot(flat, first_ref[...], preferred_element_type=F32).astype(term_ref.dtype)
    copy.wait()
    term_ref[:, split:] = jnp.dot(flat, second_ref[...], preferred_element_type=F32).astype(term_ref.dtype)


def local(q_latent, q_rope, latent_cache, page_table, lengths, w_uv, w_out):
    rows, heads, latent = q_latent.shape
    rope = q_rope.shape[2]
    pages, page_len, width = latent_cache.shape
    tokens = pages * page_len
    count = lax.axis_size(CTX)
    size = heads * (latent + rope)
    vmem = pl.BlockSpec(memory_space=pltpu.VMEM)
    smem = pl.BlockSpec(memory_space=pltpu.SMEM)
    hbm = pl.BlockSpec(memory_space=pl.ANY)
    stay = functools.partial(pltpu.with_memory_space_constraint, memory_space=pltpu.HBM)
    params = pltpu.CompilerParams(vmem_limit_bytes=16 << 20)
    dma = pltpu.SemaphoreType.DMA
    here = lax.axis_index(CTX).astype(jnp.int32)

    message = pl.pallas_call(
        message_kernel,
        out_shape=jax.ShapeDtypeStruct((rows, size), BF16),
        in_specs=[hbm, hbm],
        out_specs=vmem,
        scratch_shapes=[pltpu.VMEM(q_latent.shape, BF16), pltpu.VMEM(q_rope.shape, BF16), dma((2,))],
        compiler_params=params,
        name="message",
    )(stay(q_latent), stay(q_rope))

    near = 4
    others = [lax.ppermute(message, CTX, xor_pairs(count, k)) for k in range(1, near)]
    split = w_out.shape[1] // 2 // LANES * LANES
    live, keys, w_uv, w_first = pl.pallas_call(
        functools.partial(fetch_kernel, page_len),
        out_shape=(
            pltpu.VMEM((rows, tokens), F32),
            pltpu.VMEM((tokens, width), BF16),
            pltpu.VMEM(w_uv.shape, BF16),
            pltpu.VMEM((w_out.shape[0], split), BF16),
        ),
        in_specs=[smem, hbm, hbm, hbm, hbm, hbm],
        out_specs=(vmem, vmem, vmem, vmem),
        scratch_shapes=[
            pltpu.SMEM(lengths.shape, jnp.int32), pltpu.VMEM(page_table.shape, jnp.int32), dma((5,)),
        ],
        compiler_params=params,
        cost_estimate=pl.CostEstimate(flops=0, bytes_accessed=5 << 20, transcendentals=0),
        name="fetch",
    )(
        here.reshape(1), stay(lengths), stay(page_table), stay(latent_cache.reshape(tokens, width)),
        stay(w_uv), stay(w_out),
    )
    away = lax.broadcasted_iota(jnp.int32, (near, 1, 1), 0) ^ (here % near)
    column = jnp.broadcast_to(message[None], (near, rows, size))
    for k in range(1, near):
        column = jnp.where(away == k, others[k - 1][None], column)
    column, live, keys, w_uv, w_first = lax.optimization_barrier((column, live, keys, w_uv, w_first))
    planes = [[i * near + k for i in range(count // near)] for k in range(near)]
    query = lax.all_to_all(
        jnp.broadcast_to(column[None], (count // near, near, rows, size)),
        CTX, split_axis=0, concat_axis=0, axis_index_groups=planes, tiled=True,
    )

    state_size = heads * latent + LANES
    state = pl.pallas_call(
        functools.partial(attend_kernel, rows, heads, latent, rope),
        out_shape=jax.ShapeDtypeStruct((count * rows, state_size), BF16),
        in_specs=[vmem, vmem, vmem],
        out_specs=vmem,
        compiler_params=params,
        name="attend",
    )(query.reshape(count * rows, size), keys, live)

    state = lax.all_to_all(
        state.reshape(count, rows, state_size), CTX, split_axis=0, concat_axis=0, tiled=True
    )
    term = pl.pallas_call(
        functools.partial(project_kernel, rows, heads, latent),
        out_shape=jax.ShapeDtypeStruct((rows, w_out.shape[1]), BF16),
        in_specs=[vmem, vmem, vmem, hbm],
        out_specs=vmem,
        scratch_shapes=[pltpu.VMEM((w_out.shape[0], w_out.shape[1] - split), BF16), dma],
        compiler_params=params,
        name="project",
    )(state.reshape(count * rows, state_size), w_uv, w_first, stay(w_out))
    for low in (4, 2, 0):
        term = sum_of_four(term, count, low).astype(BF16)
    return term


def solution(mesh):
    in_specs = (
        P("grp", "ctx", None),
        P("grp", "ctx", None),
        P(("grp", "ctx"), None, None),
        P("grp", None),
        P("grp"),
        P("ctx", None, None),
        P("ctx", None),
    )
    return jax.shard_map(local, mesh=mesh, in_specs=in_specs, out_specs=P("grp", None), check_vma=False)
```

```python
import functools
import jax
import jax.numpy as jnp
from jax import lax
from jax.experimental import pallas as pl
from jax.experimental.pallas import tpu as pltpu
from jax.sharding import PartitionSpec as P

ROPE = 64
V = 128
NEG = -1e30
CTX = "ctx"
LANES = 128
F32 = jnp.float32
BF16 = jnp.bfloat16


def xor_pairs(count, mask):
    return [(i, i ^ mask) for i in range(count)]


def sum_of_four(x, count, low):
    a, b, c = (lax.ppermute(x, CTX, xor_pairs(count, k << low)) for k in (1, 2, 3))
    return (x.astype(F32) + a.astype(F32)) + (b.astype(F32) + c.astype(F32))


def message_kernel(q_latent_hbm, q_rope_hbm, message_ref, q_latent_ref, q_rope_ref, sems):
    copies = [
        pltpu.make_async_copy(q_latent_hbm, q_latent_ref, sems.at[0]),
        pltpu.make_async_copy(q_rope_hbm, q_rope_ref, sems.at[1]),
    ]
    for copy in copies:
        copy.start()
    for copy in copies:
        copy.wait()
    rows, heads, _ = q_latent_ref.shape
    q_latent = q_latent_ref[...].astype(F32)
    q_rope = q_rope_ref[...].astype(F32)
    message = [
        jnp.concatenate(
            [q_latent[r, h : h + 1] for h in range(heads)] + [q_rope[r, h : h + 1] for h in range(heads)],
            axis=1,
        )
        for r in range(rows)
    ]
    message_ref[...] = jnp.concatenate(message, axis=0).astype(BF16)


def fetch_kernel(
    page_len, here_ref, lengths_hbm, table_hbm, cache_hbm, w_uv_hbm, w_out_hbm,
    live_ref, keys_ref, w_uv_ref, w_out_ref, lengths_ref, table_ref, sems,
):
    pairs = [
        (lengths_hbm, lengths_ref), (table_hbm, table_ref), (cache_hbm, keys_ref), (w_uv_hbm, w_uv_ref),
        (w_out_hbm.at[:, : w_out_ref.shape[1]], w_out_ref),
    ]
    copies = [pltpu.make_async_copy(a, b, sems.at[k]) for k, (a, b) in enumerate(pairs)]
    for copy in copies:
        copy.start()
    copies[0].wait()
    copies[1].wait()
    rows = live_ref.shape[0]
    tokens = keys_ref.shape[0]
    pages = tokens // page_len
    slots = table_ref.shape[1]
    page = here_ref[0] * pages + lax.broadcasted_iota(jnp.int32, (pages, slots), 0)
    place = lax.broadcasted_iota(jnp.int32, (pages, slots), 1)
    token = lax.broadcasted_iota(jnp.int32, (pages, tokens), 1)
    mine = token // page_len == lax.broadcasted_iota(jnp.int32, (pages, tokens), 0)
    for r in range(rows):
        hit = jnp.broadcast_to(table_ref[r : r + 1, :], (pages, slots)) == page
        room = jnp.where(hit, lengths_ref[r] - place * page_len, 0)
        room = jnp.max(room, axis=1, keepdims=True)
        alive = mine & (token % page_len < room)
        live_ref[r : r + 1, :] = jnp.max(jnp.where(alive, 1.0, 0.0), axis=0, keepdims=True)
    for copy in copies[2:]:
        copy.wait()


def attend_kernel(rows, heads, latent, rope, q_ref, keys_ref, live_ref, state_ref):
    count = q_ref.shape[0]
    tokens = keys_ref.shape[0]
    row = lax.broadcasted_iota(jnp.int32, (count, 1), 0) % rows
    live = jnp.broadcast_to(live_ref[0:1, :], (count, tokens))
    for r in range(1, rows):
        live = jnp.where(row == r, live_ref[r : r + 1, :], live)
    live = live > 0.5
    side = heads * latent
    lane = lax.broadcasted_iota(jnp.int32, (count, state_ref.shape[1] - side), 1)
    stats = jnp.zeros(lane.shape, F32)
    for h in range(heads):
        query = jnp.concatenate(
            [q_ref[:, h * latent : (h + 1) * latent], q_ref[:, side + h * rope : side + (h + 1) * rope]], axis=1
        )
        scores = lax.dot_general(
            query, keys_ref[...], (((1,), (1,)), ((), ())), preferred_element_type=F32
        ) * ((V + ROPE) ** (-0.5))
        scores = jnp.where(live, scores, NEG)
        shift = jnp.max(scores, axis=1, keepdims=True).astype(BF16).astype(F32)
        weights = jnp.where(live, jnp.exp(scores - shift), 0.0).astype(BF16)
        total = jnp.sum(weights.astype(F32), axis=1, keepdims=True)
        outs = jnp.dot(weights, keys_ref[:, :latent], preferred_element_type=F32)
        state_ref[:, h * latent : (h + 1) * latent] = outs.astype(BF16)
        high = total.astype(BF16).astype(F32)
        for k, value in enumerate((shift, high, total - high)):
            stats = jnp.where(lane == 3 * h + k, value, stats)
    state_ref[:, side:] = stats.astype(BF16)


def project_kernel(rows, heads, latent, state_ref, w_uv_ref, first_ref, w_out_hbm, term_ref, second_ref, sems):
    split = first_ref.shape[1]
    parts, _, step = second_ref.shape
    copies = [
        pltpu.make_async_copy(
            w_out_hbm.at[:, split + k * step : split + (k + 1) * step], second_ref.at[k], sems.at[k]
        )
        for k in range(parts)
    ]
    for copy in copies:
        copy.start()
    count = state_ref.shape[0]
    mixed = rows * heads
    side = heads * latent
    lane = lax.broadcasted_iota(jnp.int32, (count, LANES), 1)
    row = lax.broadcasted_iota(jnp.int32, (count, LANES), 0) % rows
    column = lane % mixed
    own = (column // heads == row) & (lane < 2 * mixed)
    stats = state_ref[:, side:].astype(F32)
    shift = jnp.full((count, LANES), 2 * NEG, F32)
    for h in range(heads):
        shift = jnp.where(own & (column % heads == h), stats[:, 3 * h : 3 * h + 1], shift)
    best = jnp.max(shift, axis=0, keepdims=True)
    factor = jnp.where(own, jnp.exp(shift - best), 0.0)
    high = factor.astype(BF16).astype(F32)
    factor = jnp.where(lane < mixed, high, factor - high).astype(BF16)
    merged = lax.dot_general(
        factor, state_ref[...], (((0,), (0,)), ((), ())), preferred_element_type=F32
    )
    merged = merged[:mixed] + merged[mixed : 2 * mixed]
    parts = []
    for h in range(heads):
        total = merged[:, side + 3 * h + 1 : side + 3 * h + 2] + merged[:, side + 3 * h + 2 : side + 3 * h + 3]
        attended = (merged[:, h * latent : (h + 1) * latent] / total).astype(BF16)
        parts.append(jnp.dot(attended, w_uv_ref[h], preferred_element_type=F32))
    flat = jnp.concatenate(
        [
            jnp.concatenate([parts[h][r * heads + h : r * heads + h + 1] for h in range(heads)], axis=1)
            for r in range(rows)
        ],
        axis=0,
    ).astype(BF16)
    term_ref[:, :split] = jnp.dot(flat, first_ref[...], preferred_element_type=F32).astype(term_ref.dtype)
    for k, copy in enumerate(copies):
        copy.wait()
        term_ref[:, split + k * step : split + (k + 1) * step] = jnp.dot(
            flat, second_ref[k], preferred_element_type=F32
        ).astype(term_ref.dtype)


def local(q_latent, q_rope, latent_cache, page_table, lengths, w_uv, w_out):
    rows, heads, latent = q_latent.shape
    rope = q_rope.shape[2]
    pages, page_len, width = latent_cache.shape
    tokens = pages * page_len
    count = lax.axis_size(CTX)
    size = heads * (latent + rope)
    vmem = pl.BlockSpec(memory_space=pltpu.VMEM)
    smem = pl.BlockSpec(memory_space=pltpu.SMEM)
    hbm = pl.BlockSpec(memory_space=pl.ANY)
    stay = functools.partial(pltpu.with_memory_space_constraint, memory_space=pltpu.HBM)
    params = pltpu.CompilerParams(vmem_limit_bytes=16 << 20)
    dma = pltpu.SemaphoreType.DMA
    here = lax.axis_index(CTX).astype(jnp.int32)

    message = pl.pallas_call(
        message_kernel,
        out_shape=jax.ShapeDtypeStruct((rows, size), BF16),
        in_specs=[hbm, hbm],
        out_specs=vmem,
        scratch_shapes=[pltpu.VMEM(q_latent.shape, BF16), pltpu.VMEM(q_rope.shape, BF16), dma((2,))],
        compiler_params=params,
        name="message",
    )(stay(q_latent), stay(q_rope))

    near = 4
    others = [lax.ppermute(message, CTX, xor_pairs(count, k)) for k in range(1, near)]
    split = w_out.shape[1] // 2 // LANES * LANES
    live, keys, w_uv, w_first = pl.pallas_call(
        functools.partial(fetch_kernel, page_len),
        out_shape=(
            pltpu.VMEM((rows, tokens), F32),
            pltpu.VMEM((tokens, width), BF16),
            pltpu.VMEM(w_uv.shape, BF16),
            pltpu.VMEM((w_out.shape[0], split), BF16),
        ),
        in_specs=[smem, hbm, hbm, hbm, hbm, hbm],
        out_specs=(vmem, vmem, vmem, vmem),
        scratch_shapes=[
            pltpu.SMEM(lengths.shape, jnp.int32), pltpu.VMEM(page_table.shape, jnp.int32), dma((5,)),
        ],
        compiler_params=params,
        cost_estimate=pl.CostEstimate(flops=0, bytes_accessed=5 << 20, transcendentals=0),
        name="fetch",
    )(
        here.reshape(1), stay(lengths), stay(page_table), stay(latent_cache.reshape(tokens, width)),
        stay(w_uv), stay(w_out),
    )
    away = lax.broadcasted_iota(jnp.int32, (near, 1, 1), 0) ^ (here % near)
    column = jnp.broadcast_to(message[None], (near, rows, size))
    for k in range(1, near):
        column = jnp.where(away == k, others[k - 1][None], column)
    column, live, keys, w_uv, w_first = lax.optimization_barrier((column, live, keys, w_uv, w_first))
    planes = [[i * near + k for i in range(count // near)] for k in range(near)]
    query = lax.all_to_all(
        jnp.broadcast_to(column[None], (count // near, near, rows, size)),
        CTX, split_axis=0, concat_axis=0, axis_index_groups=planes, tiled=True,
    )

    state_size = heads * latent + LANES
    state = pl.pallas_call(
        functools.partial(attend_kernel, rows, heads, latent, rope),
        out_shape=jax.ShapeDtypeStruct((count * rows, state_size), BF16),
        in_specs=[vmem, vmem, vmem],
        out_specs=vmem,
        compiler_params=params,
        name="attend",
    )(query.reshape(count * rows, size), keys, live)

    state = lax.all_to_all(
        state.reshape(count, rows, state_size), CTX, split_axis=0, concat_axis=0, tiled=True
    )
    parts = 4
    term = pl.pallas_call(
        functools.partial(project_kernel, rows, heads, latent),
        out_shape=jax.ShapeDtypeStruct((rows, w_out.shape[1]), BF16),
        in_specs=[vmem, vmem, vmem, hbm],
        out_specs=vmem,
        scratch_shapes=[pltpu.VMEM((parts, w_out.shape[0], (w_out.shape[1] - split) // parts), BF16), dma((parts,))],
        compiler_params=params,
        name="project",
    )(state.reshape(count * rows, state_size), w_uv, w_first, stay(w_out))
    for low in (4, 2, 0):
        term = sum_of_four(term, count, low).astype(BF16)
    return term


def solution(mesh):
    in_specs = (
        P("grp", "ctx", None),
        P("grp", "ctx", None),
        P(("grp", "ctx"), None, None),
        P("grp", None),
        P("grp"),
        P("ctx", None, None),
        P("ctx", None),
    )
    return jax.shard_map(local, mesh=mesh, in_specs=in_specs, out_specs=P("grp", None), check_vma=False)
```

```python
import functools
import jax
import jax.numpy as jnp
from jax import lax
from jax.experimental import pallas as pl
from jax.experimental.pallas import tpu as pltpu
from jax.sharding import PartitionSpec as P

ROPE = 64
V = 128
NEG = -1e30
CTX = "ctx"
LANES = 128
F32 = jnp.float32
BF16 = jnp.bfloat16


def xor_pairs(count, mask):
    return [(i, i ^ mask) for i in range(count)]


def sum_of_four(x, count, low):
    a, b, c = (lax.ppermute(x, CTX, xor_pairs(count, k << low)) for k in (1, 2, 3))
    return (x.astype(F32) + a.astype(F32)) + (b.astype(F32) + c.astype(F32))


def message_kernel(q_latent_hbm, q_rope_hbm, message_ref, q_latent_ref, q_rope_ref, sems):
    copies = [
        pltpu.make_async_copy(q_latent_hbm, q_latent_ref, sems.at[0]),
        pltpu.make_async_copy(q_rope_hbm, q_rope_ref, sems.at[1]),
    ]
    for copy in copies:
        copy.start()
    for copy in copies:
        copy.wait()
    rows, heads, _ = q_latent_ref.shape
    q_latent = q_latent_ref[...].astype(F32)
    q_rope = q_rope_ref[...].astype(F32)
    message = [
        jnp.concatenate(
            [q_latent[r, h : h + 1] for h in range(heads)] + [q_rope[r, h : h + 1] for h in range(heads)],
            axis=1,
        )
        for r in range(rows)
    ]
    message_ref[...] = jnp.concatenate(message, axis=0).astype(BF16)


def fetch_kernel(
    page_len, here_ref, lengths_hbm, table_hbm, cache_hbm, w_uv_hbm, w_out_hbm,
    live_ref, keys_ref, w_uv_ref, w_out_ref, lengths_ref, table_ref, sems,
):
    pairs = [
        (lengths_hbm, lengths_ref), (table_hbm, table_ref), (cache_hbm, keys_ref), (w_uv_hbm, w_uv_ref),
        (w_out_hbm.at[: w_out_ref.shape[0]], w_out_ref),
    ]
    copies = [pltpu.make_async_copy(a, b, sems.at[k]) for k, (a, b) in enumerate(pairs)]
    for copy in copies:
        copy.start()
    copies[0].wait()
    copies[1].wait()
    rows = live_ref.shape[0]
    tokens = keys_ref.shape[0]
    pages = tokens // page_len
    slots = table_ref.shape[1]
    page = here_ref[0] * pages + lax.broadcasted_iota(jnp.int32, (pages, slots), 0)
    place = lax.broadcasted_iota(jnp.int32, (pages, slots), 1)
    token = lax.broadcasted_iota(jnp.int32, (pages, tokens), 1)
    mine = token // page_len == lax.broadcasted_iota(jnp.int32, (pages, tokens), 0)
    for r in range(rows):
        hit = jnp.broadcast_to(table_ref[r : r + 1, :], (pages, slots)) == page
        room = jnp.where(hit, lengths_ref[r] - place * page_len, 0)
        room = jnp.max(room, axis=1, keepdims=True)
        alive = mine & (token % page_len < room)
        live_ref[r : r + 1, :] = jnp.max(jnp.where(alive, 1.0, 0.0), axis=0, keepdims=True)
    for copy in copies[2:]:
        copy.wait()


def attend_kernel(rows, heads, latent, rope, q_ref, keys_ref, live_ref, state_ref):
    count = q_ref.shape[0]
    tokens = keys_ref.shape[0]
    row = lax.broadcasted_iota(jnp.int32, (count, 1), 0) % rows
    live = jnp.broadcast_to(live_ref[0:1, :], (count, tokens))
    for r in range(1, rows):
        live = jnp.where(row == r, live_ref[r : r + 1, :], live)
    live = live > 0.5
    side = heads * latent
    lane = lax.broadcasted_iota(jnp.int32, (count, state_ref.shape[1] - side), 1)
    stats = jnp.zeros(lane.shape, F32)
    for h in range(heads):
        query = jnp.concatenate(
            [q_ref[:, h * latent : (h + 1) * latent], q_ref[:, side + h * rope : side + (h + 1) * rope]], axis=1
        )
        scores = lax.dot_general(
            query, keys_ref[...], (((1,), (1,)), ((), ())), preferred_element_type=F32
        ) * ((V + ROPE) ** (-0.5))
        scores = jnp.where(live, scores, NEG)
        shift = jnp.max(scores, axis=1, keepdims=True).astype(BF16).astype(F32)
        weights = jnp.where(live, jnp.exp(scores - shift), 0.0).astype(BF16)
        total = jnp.sum(weights.astype(F32), axis=1, keepdims=True)
        outs = jnp.dot(weights, keys_ref[:, :latent], preferred_element_type=F32)
        state_ref[:, h * latent : (h + 1) * latent] = outs.astype(BF16)
        high = total.astype(BF16).astype(F32)
        for k, value in enumerate((shift, high, total - high)):
            stats = jnp.where(lane == 3 * h + k, value, stats)
    state_ref[:, side:] = stats.astype(BF16)


def project_kernel(rows, heads, latent, state_ref, w_uv_ref, first_ref, w_out_hbm, term_ref, second_ref, sems):
    split = first_ref.shape[0]
    parts = sems.shape[0]
    step = second_ref.shape[0] // parts
    copies = [
        pltpu.make_async_copy(
            w_out_hbm.at[split + k * step : split + (k + 1) * step], second_ref.at[k * step : (k + 1) * step], sems.at[k]
        )
        for k in range(parts)
    ]
    for copy in copies:
        copy.start()
    count = state_ref.shape[0]
    mixed = rows * heads
    side = heads * latent
    lane = lax.broadcasted_iota(jnp.int32, (count, LANES), 1)
    row = lax.broadcasted_iota(jnp.int32, (count, LANES), 0) % rows
    column = lane % mixed
    own = (column // heads == row) & (lane < 2 * mixed)
    stats = state_ref[:, side:].astype(F32)
    shift = jnp.full((count, LANES), 2 * NEG, F32)
    for h in range(heads):
        shift = jnp.where(own & (column % heads == h), stats[:, 3 * h : 3 * h + 1], shift)
    best = jnp.max(shift, axis=0, keepdims=True)
    factor = jnp.where(own, jnp.exp(shift - best), 0.0)
    high = factor.astype(BF16).astype(F32)
    factor = jnp.where(lane < mixed, high, factor - high).astype(BF16)
    merged = lax.dot_general(
        factor, state_ref[...], (((0,), (0,)), ((), ())), preferred_element_type=F32
    )
    merged = merged[:mixed] + merged[mixed : 2 * mixed]
    parts = []
    for h in range(heads):
        total = merged[:, side + 3 * h + 1 : side + 3 * h + 2] + merged[:, side + 3 * h + 2 : side + 3 * h + 3]
        attended = (merged[:, h * latent : (h + 1) * latent] / total).astype(BF16)
        parts.append(jnp.dot(attended, w_uv_ref[h], preferred_element_type=F32))
    flat = jnp.concatenate(
        [
            jnp.concatenate([parts[h][r * heads + h : r * heads + h + 1] for h in range(heads)], axis=1)
            for r in range(rows)
        ],
        axis=0,
    ).astype(BF16)
    term = jnp.dot(flat[:, :split], first_ref[...], preferred_element_type=F32)
    for copy in copies:
        copy.wait()
    term += jnp.dot(flat[:, split:], second_ref[...], preferred_element_type=F32)
    term_ref[...] = term.astype(term_ref.dtype)


def local(q_latent, q_rope, latent_cache, page_table, lengths, w_uv, w_out):
    rows, heads, latent = q_latent.shape
    rope = q_rope.shape[2]
    pages, page_len, width = latent_cache.shape
    tokens = pages * page_len
    count = lax.axis_size(CTX)
    size = heads * (latent + rope)
    vmem = pl.BlockSpec(memory_space=pltpu.VMEM)
    smem = pl.BlockSpec(memory_space=pltpu.SMEM)
    hbm = pl.BlockSpec(memory_space=pl.ANY)
    stay = functools.partial(pltpu.with_memory_space_constraint, memory_space=pltpu.HBM)
    params = pltpu.CompilerParams(vmem_limit_bytes=16 << 20)
    dma = pltpu.SemaphoreType.DMA
    here = lax.axis_index(CTX).astype(jnp.int32)

    message = pl.pallas_call(
        message_kernel,
        out_shape=jax.ShapeDtypeStruct((rows, size), BF16),
        in_specs=[hbm, hbm],
        out_specs=vmem,
        scratch_shapes=[pltpu.VMEM(q_latent.shape, BF16), pltpu.VMEM(q_rope.shape, BF16), dma((2,))],
        compiler_params=params,
        name="message",
    )(stay(q_latent), stay(q_rope))

    near = 4
    others = [lax.ppermute(message, CTX, xor_pairs(count, k)) for k in range(1, near)]
    split = w_out.shape[0] // 2
    live, keys, w_uv, w_first = pl.pallas_call(
        functools.partial(fetch_kernel, page_len),
        out_shape=(
            pltpu.VMEM((rows, tokens), F32),
            pltpu.VMEM((tokens, width), BF16),
            pltpu.VMEM(w_uv.shape, BF16),
            pltpu.VMEM((split, w_out.shape[1]), BF16),
        ),
        in_specs=[smem, hbm, hbm, hbm, hbm, hbm],
        out_specs=(vmem, vmem, vmem, vmem),
        scratch_shapes=[
            pltpu.SMEM(lengths.shape, jnp.int32), pltpu.VMEM(page_table.shape, jnp.int32), dma((5,)),
        ],
        compiler_params=params,
        cost_estimate=pl.CostEstimate(flops=0, bytes_accessed=5 << 20, transcendentals=0),
        name="fetch",
    )(
        here.reshape(1), stay(lengths), stay(page_table), stay(latent_cache.reshape(tokens, width)),
        stay(w_uv), stay(w_out),
    )
    away = lax.broadcasted_iota(jnp.int32, (near, 1, 1), 0) ^ (here % near)
    column = jnp.broadcast_to(message[None], (near, rows, size))
    for k in range(1, near):
        column = jnp.where(away == k, others[k - 1][None], column)
    column, live, keys, w_uv, w_first = lax.optimization_barrier((column, live, keys, w_uv, w_first))
    planes = [[i * near + k for i in range(count // near)] for k in range(near)]
    query = lax.all_to_all(
        jnp.broadcast_to(column[None], (count // near, near, rows, size)),
        CTX, split_axis=0, concat_axis=0, axis_index_groups=planes, tiled=True,
    )

    state_size = heads * latent + LANES
    state = pl.pallas_call(
        functools.partial(attend_kernel, rows, heads, latent, rope),
        out_shape=jax.ShapeDtypeStruct((count * rows, state_size), BF16),
        in_specs=[vmem, vmem, vmem],
        out_specs=vmem,
        compiler_params=params,
        name="attend",
    )(query.reshape(count * rows, size), keys, live)

    state = lax.all_to_all(
        state.reshape(count, rows, state_size), CTX, split_axis=0, concat_axis=0, tiled=True
    )
    parts = 4
    term = pl.pallas_call(
        functools.partial(project_kernel, rows, heads, latent),
        out_shape=jax.ShapeDtypeStruct((rows, w_out.shape[1]), BF16),
        in_specs=[vmem, vmem, vmem, hbm],
        out_specs=vmem,
        scratch_shapes=[pltpu.VMEM((w_out.shape[0] - split, w_out.shape[1]), BF16), dma((parts,))],
        compiler_params=params,
        name="project",
    )(state.reshape(count * rows, state_size), w_uv, w_first, stay(w_out))
    for low in (4, 2, 0):
        term = sum_of_four(term, count, low).astype(BF16)
    return term


def solution(mesh):
    in_specs = (
        P("grp", "ctx", None),
        P("grp", "ctx", None),
        P(("grp", "ctx"), None, None),
        P("grp", None),
        P("grp"),
        P("ctx", None, None),
        P("ctx", None),
    )
    return jax.shard_map(local, mesh=mesh, in_specs=in_specs, out_specs=P("grp", None), check_vma=False)
```

```python
import functools
import jax
import jax.numpy as jnp
from jax import lax
from jax.experimental import pallas as pl
from jax.experimental.pallas import tpu as pltpu
from jax.sharding import PartitionSpec as P

ROPE = 64
V = 128
NEG = -1e30
CTX = "ctx"
LANES = 128
F32 = jnp.float32
BF16 = jnp.bfloat16


def xor_pairs(count, mask):
    return [(i, i ^ mask) for i in range(count)]


def sum_of_two(x, count, mask):
    return x.astype(F32) + lax.ppermute(x, CTX, xor_pairs(count, mask)).astype(F32)


def sum_of_four(x, count, low):
    a, b, c = (lax.ppermute(x, CTX, xor_pairs(count, k << low)) for k in (1, 2, 3))
    return (x.astype(F32) + a.astype(F32)) + (b.astype(F32) + c.astype(F32))


def message_kernel(q_latent_hbm, q_rope_hbm, message_ref, q_latent_ref, q_rope_ref, sems):
    copies = [
        pltpu.make_async_copy(q_latent_hbm, q_latent_ref, sems.at[0]),
        pltpu.make_async_copy(q_rope_hbm, q_rope_ref, sems.at[1]),
    ]
    for copy in copies:
        copy.start()
    for copy in copies:
        copy.wait()
    rows, heads, _ = q_latent_ref.shape
    q_latent = q_latent_ref[...].astype(F32)
    q_rope = q_rope_ref[...].astype(F32)
    message = [
        jnp.concatenate(
            [q_latent[r, h : h + 1] for h in range(heads)] + [q_rope[r, h : h + 1] for h in range(heads)],
            axis=1,
        )
        for r in range(rows)
    ]
    message_ref[...] = jnp.concatenate(message, axis=0).astype(BF16)


def fetch_kernel(
    page_len, here_ref, lengths_hbm, table_hbm, cache_hbm, w_uv_hbm, w_out_hbm,
    live_ref, keys_ref, w_uv_ref, w_out_ref, lengths_ref, table_ref, sems,
):
    pairs = [
        (lengths_hbm, lengths_ref), (table_hbm, table_ref), (cache_hbm, keys_ref), (w_uv_hbm, w_uv_ref),
        (w_out_hbm.at[: w_out_ref.shape[0]], w_out_ref),
    ]
    copies = [pltpu.make_async_copy(a, b, sems.at[k]) for k, (a, b) in enumerate(pairs)]
    for copy in copies:
        copy.start()
    copies[0].wait()
    copies[1].wait()
    rows = live_ref.shape[0]
    tokens = keys_ref.shape[0]
    pages = tokens // page_len
    slots = table_ref.shape[1]
    page = here_ref[0] * pages + lax.broadcasted_iota(jnp.int32, (pages, slots), 0)
    place = lax.broadcasted_iota(jnp.int32, (pages, slots), 1)
    token = lax.broadcasted_iota(jnp.int32, (pages, tokens), 1)
    mine = token // page_len == lax.broadcasted_iota(jnp.int32, (pages, tokens), 0)
    for r in range(rows):
        hit = jnp.broadcast_to(table_ref[r : r + 1, :], (pages, slots)) == page
        room = jnp.where(hit, lengths_ref[r] - place * page_len, 0)
        room = jnp.max(room, axis=1, keepdims=True)
        alive = mine & (token % page_len < room)
        live_ref[r : r + 1, :] = jnp.max(jnp.where(alive, 1.0, 0.0), axis=0, keepdims=True)
    for copy in copies[2:]:
        copy.wait()


def attend_kernel(rows, heads, latent, rope, q_ref, keys_ref, live_ref, state_ref):
    count = q_ref.shape[0]
    tokens = keys_ref.shape[0]
    row = lax.broadcasted_iota(jnp.int32, (count, 1), 0) % rows
    live = jnp.broadcast_to(live_ref[0:1, :], (count, tokens))
    for r in range(1, rows):
        live = jnp.where(row == r, live_ref[r : r + 1, :], live)
    live = live > 0.5
    side = heads * latent
    lane = lax.broadcasted_iota(jnp.int32, (count, state_ref.shape[1] - side), 1)
    stats = jnp.zeros(lane.shape, F32)
    for h in range(heads):
        query = jnp.concatenate(
            [q_ref[:, h * latent : (h + 1) * latent], q_ref[:, side + h * rope : side + (h + 1) * rope]], axis=1
        )
        scores = lax.dot_general(
            query, keys_ref[...], (((1,), (1,)), ((), ())), preferred_element_type=F32
        ) * ((V + ROPE) ** (-0.5))
        scores = jnp.where(live, scores, NEG)
        shift = jnp.max(scores, axis=1, keepdims=True).astype(BF16).astype(F32)
        weights = jnp.where(live, jnp.exp(scores - shift), 0.0).astype(BF16)
        total = jnp.sum(weights.astype(F32), axis=1, keepdims=True)
        outs = jnp.dot(weights, keys_ref[:, :latent], preferred_element_type=F32)
        state_ref[:, h * latent : (h + 1) * latent] = outs.astype(BF16)
        high = total.astype(BF16).astype(F32)
        for k, value in enumerate((shift, high, total - high)):
            stats = jnp.where(lane == 3 * h + k, value, stats)
    state_ref[:, side:] = stats.astype(BF16)


def project_kernel(rows, heads, latent, state_ref, w_uv_ref, first_ref, w_out_hbm, term_ref, second_ref, sems):
    split = first_ref.shape[0]
    parts = sems.shape[0]
    step = second_ref.shape[0] // parts
    copies = [
        pltpu.make_async_copy(
            w_out_hbm.at[split + k * step : split + (k + 1) * step], second_ref.at[k * step : (k + 1) * step], sems.at[k]
        )
        for k in range(parts)
    ]
    for copy in copies:
        copy.start()
    count = state_ref.shape[0]
    mixed = rows * heads
    side = heads * latent
    lane = lax.broadcasted_iota(jnp.int32, (count, LANES), 1)
    row = lax.broadcasted_iota(jnp.int32, (count, LANES), 0) % rows
    column = lane % mixed
    own = (column // heads == row) & (lane < 2 * mixed)
    stats = state_ref[:, side:].astype(F32)
    shift = jnp.full((count, LANES), 2 * NEG, F32)
    for h in range(heads):
        shift = jnp.where(own & (column % heads == h), stats[:, 3 * h : 3 * h + 1], shift)
    best = jnp.max(shift, axis=0, keepdims=True)
    factor = jnp.where(own, jnp.exp(shift - best), 0.0)
    high = factor.astype(BF16).astype(F32)
    factor = jnp.where(lane < mixed, high, factor - high).astype(BF16)
    merged = lax.dot_general(
        factor, state_ref[...], (((0,), (0,)), ((), ())), preferred_element_type=F32
    )
    merged = merged[:mixed] + merged[mixed : 2 * mixed]
    parts = []
    for h in range(heads):
        total = merged[:, side + 3 * h + 1 : side + 3 * h + 2] + merged[:, side + 3 * h + 2 : side + 3 * h + 3]
        attended = (merged[:, h * latent : (h + 1) * latent] / total).astype(BF16)
        parts.append(jnp.dot(attended, w_uv_ref[h], preferred_element_type=F32))
    flat = jnp.concatenate(
        [
            jnp.concatenate([parts[h][r * heads + h : r * heads + h + 1] for h in range(heads)], axis=1)
            for r in range(rows)
        ],
        axis=0,
    ).astype(BF16)
    term = jnp.dot(flat[:, :split], first_ref[...], preferred_element_type=F32)
    for copy in copies:
        copy.wait()
    term += jnp.dot(flat[:, split:], second_ref[...], preferred_element_type=F32)
    term_ref[...] = term.astype(term_ref.dtype)


def local(q_latent, q_rope, latent_cache, page_table, lengths, w_uv, w_out):
    rows, heads, latent = q_latent.shape
    rope = q_rope.shape[2]
    pages, page_len, width = latent_cache.shape
    tokens = pages * page_len
    count = lax.axis_size(CTX)
    size = heads * (latent + rope)
    vmem = pl.BlockSpec(memory_space=pltpu.VMEM)
    smem = pl.BlockSpec(memory_space=pltpu.SMEM)
    hbm = pl.BlockSpec(memory_space=pl.ANY)
    stay = functools.partial(pltpu.with_memory_space_constraint, memory_space=pltpu.HBM)
    params = pltpu.CompilerParams(vmem_limit_bytes=16 << 20)
    dma = pltpu.SemaphoreType.DMA
    here = lax.axis_index(CTX).astype(jnp.int32)

    message = pl.pallas_call(
        message_kernel,
        out_shape=jax.ShapeDtypeStruct((rows, size), BF16),
        in_specs=[hbm, hbm],
        out_specs=vmem,
        scratch_shapes=[pltpu.VMEM(q_latent.shape, BF16), pltpu.VMEM(q_rope.shape, BF16), dma((2,))],
        compiler_params=params,
        name="message",
    )(stay(q_latent), stay(q_rope))

    near = 4
    others = [lax.ppermute(message, CTX, xor_pairs(count, k)) for k in range(1, near)]
    split = w_out.shape[0] // 2
    live, keys, w_uv, w_first = pl.pallas_call(
        functools.partial(fetch_kernel, page_len),
        out_shape=(
            pltpu.VMEM((rows, tokens), F32),
            pltpu.VMEM((tokens, width), BF16),
            pltpu.VMEM(w_uv.shape, BF16),
            pltpu.VMEM((split, w_out.shape[1]), BF16),
        ),
        in_specs=[smem, hbm, hbm, hbm, hbm, hbm],
        out_specs=(vmem, vmem, vmem, vmem),
        scratch_shapes=[
            pltpu.SMEM(lengths.shape, jnp.int32), pltpu.VMEM(page_table.shape, jnp.int32), dma((5,)),
        ],
        compiler_params=params,
        cost_estimate=pl.CostEstimate(flops=0, bytes_accessed=5 << 20, transcendentals=0),
        name="fetch",
    )(
        here.reshape(1), stay(lengths), stay(page_table), stay(latent_cache.reshape(tokens, width)),
        stay(w_uv), stay(w_out),
    )
    away = lax.broadcasted_iota(jnp.int32, (near, 1, 1), 0) ^ (here % near)
    column = jnp.broadcast_to(message[None], (near, rows, size))
    for k in range(1, near):
        column = jnp.where(away == k, others[k - 1][None], column)
    column, live, keys, w_uv, w_first = lax.optimization_barrier((column, live, keys, w_uv, w_first))
    planes = [[i * near + k for i in range(count // near)] for k in range(near)]
    query = lax.all_to_all(
        jnp.broadcast_to(column[None], (count // near, near, rows, size)),
        CTX, split_axis=0, concat_axis=0, axis_index_groups=planes, tiled=True,
    )

    state_size = heads * latent + LANES
    state = pl.pallas_call(
        functools.partial(attend_kernel, rows, heads, latent, rope),
        out_shape=jax.ShapeDtypeStruct((count * rows, state_size), BF16),
        in_specs=[vmem, vmem, vmem],
        out_specs=vmem,
        compiler_params=params,
        name="attend",
    )(query.reshape(count * rows, size), keys, live)

    state = lax.all_to_all(
        state.reshape(count, rows, state_size), CTX, split_axis=0, concat_axis=0, tiled=True
    )
    parts = 4
    term = pl.pallas_call(
        functools.partial(project_kernel, rows, heads, latent),
        out_shape=jax.ShapeDtypeStruct((rows, w_out.shape[1]), BF16),
        in_specs=[vmem, vmem, vmem, hbm],
        out_specs=vmem,
        scratch_shapes=[pltpu.VMEM((w_out.shape[0] - split, w_out.shape[1]), BF16), dma((parts,))],
        compiler_params=params,
        name="project",
    )(state.reshape(count * rows, state_size), w_uv, w_first, stay(w_out))
    for mask in (1, 3):
        term = sum_of_two(term, count, mask).astype(BF16)
    for low in (4, 2):
        term = sum_of_four(term, count, low).astype(BF16)
    return term


def solution(mesh):
    in_specs = (
        P("grp", "ctx", None),
        P("grp", "ctx", None),
        P(("grp", "ctx"), None, None),
        P("grp", None),
        P("grp"),
        P("ctx", None, None),
        P("ctx", None),
    )
    return jax.shard_map(local, mesh=mesh, in_specs=in_specs, out_specs=P("grp", None), check_vma=False)
```

```python
import functools
import jax
import jax.numpy as jnp
from jax import lax
from jax.experimental import pallas as pl
from jax.experimental.pallas import tpu as pltpu
from jax.sharding import PartitionSpec as P

ROPE = 64
V = 128
NEG = -1e30
CTX = "ctx"
LANES = 128
F32 = jnp.float32
BF16 = jnp.bfloat16


def xor_pairs(count, mask):
    return [(i, i ^ mask) for i in range(count)]


def sum_of_four(x, count, low):
    a, c, b = (lax.ppermute(x, CTX, xor_pairs(count, k << low)) for k in (1, 3, 2))
    return (x.astype(F32) + a.astype(F32)) + (b.astype(F32) + c.astype(F32))


def message_kernel(q_latent_hbm, q_rope_hbm, message_ref, q_latent_ref, q_rope_ref, sems):
    copies = [
        pltpu.make_async_copy(q_latent_hbm, q_latent_ref, sems.at[0]),
        pltpu.make_async_copy(q_rope_hbm, q_rope_ref, sems.at[1]),
    ]
    for copy in copies:
        copy.start()
    for copy in copies:
        copy.wait()
    rows, heads, _ = q_latent_ref.shape
    q_latent = q_latent_ref[...].astype(F32)
    q_rope = q_rope_ref[...].astype(F32)
    message = [
        jnp.concatenate(
            [q_latent[r, h : h + 1] for h in range(heads)] + [q_rope[r, h : h + 1] for h in range(heads)],
            axis=1,
        )
        for r in range(rows)
    ]
    message_ref[...] = jnp.concatenate(message, axis=0).astype(BF16)


def fetch_kernel(
    page_len, here_ref, lengths_hbm, table_hbm, cache_hbm, w_uv_hbm, w_out_hbm,
    live_ref, keys_ref, w_uv_ref, w_out_ref, lengths_ref, table_ref, sems,
):
    pairs = [
        (lengths_hbm, lengths_ref), (table_hbm, table_ref), (cache_hbm, keys_ref), (w_uv_hbm, w_uv_ref),
        (w_out_hbm.at[: w_out_ref.shape[0]], w_out_ref),
    ]
    copies = [pltpu.make_async_copy(a, b, sems.at[k]) for k, (a, b) in enumerate(pairs)]
    for copy in copies:
        copy.start()
    copies[0].wait()
    copies[1].wait()
    rows = live_ref.shape[0]
    tokens = keys_ref.shape[0]
    pages = tokens // page_len
    slots = table_ref.shape[1]
    page = here_ref[0] * pages + lax.broadcasted_iota(jnp.int32, (pages, slots), 0)
    place = lax.broadcasted_iota(jnp.int32, (pages, slots), 1)
    token = lax.broadcasted_iota(jnp.int32, (pages, tokens), 1)
    mine = token // page_len == lax.broadcasted_iota(jnp.int32, (pages, tokens), 0)
    for r in range(rows):
        hit = jnp.broadcast_to(table_ref[r : r + 1, :], (pages, slots)) == page
        room = jnp.where(hit, lengths_ref[r] - place * page_len, 0)
        room = jnp.max(room, axis=1, keepdims=True)
        alive = mine & (token % page_len < room)
        live_ref[r : r + 1, :] = jnp.max(jnp.where(alive, 1.0, 0.0), axis=0, keepdims=True)
    for copy in copies[2:]:
        copy.wait()


def attend_kernel(rows, heads, latent, rope, q_ref, keys_ref, live_ref, state_ref):
    count = q_ref.shape[0]
    tokens = keys_ref.shape[0]
    row = lax.broadcasted_iota(jnp.int32, (count, 1), 0) % rows
    live = jnp.broadcast_to(live_ref[0:1, :], (count, tokens))
    for r in range(1, rows):
        live = jnp.where(row == r, live_ref[r : r + 1, :], live)
    live = live > 0.5
    side = heads * latent
    lane = lax.broadcasted_iota(jnp.int32, (count, state_ref.shape[1] - side), 1)
    stats = jnp.zeros(lane.shape, F32)
    for h in range(heads):
        query = jnp.concatenate(
            [q_ref[:, h * latent : (h + 1) * latent], q_ref[:, side + h * rope : side + (h + 1) * rope]], axis=1
        )
        scores = lax.dot_general(
            query, keys_ref[...], (((1,), (1,)), ((), ())), preferred_element_type=F32
        ) * ((V + ROPE) ** (-0.5))
        scores = jnp.where(live, scores, NEG)
        shift = jnp.max(scores, axis=1, keepdims=True).astype(BF16).astype(F32)
        weights = jnp.where(live, jnp.exp(scores - shift), 0.0).astype(BF16)
        total = jnp.sum(weights.astype(F32), axis=1, keepdims=True)
        outs = jnp.dot(weights, keys_ref[:, :latent], preferred_element_type=F32)
        state_ref[:, h * latent : (h + 1) * latent] = outs.astype(BF16)
        high = total.astype(BF16).astype(F32)
        for k, value in enumerate((shift, high, total - high)):
            stats = jnp.where(lane == 3 * h + k, value, stats)
    state_ref[:, side:] = stats.astype(BF16)


def project_kernel(rows, heads, latent, state_ref, w_uv_ref, first_ref, w_out_hbm, term_ref, second_ref, sems):
    split = first_ref.shape[0]
    parts = sems.shape[0]
    step = second_ref.shape[0] // parts
    copies = [
        pltpu.make_async_copy(
            w_out_hbm.at[split + k * step : split + (k + 1) * step], second_ref.at[k * step : (k + 1) * step], sems.at[k]
        )
        for k in range(parts)
    ]
    for copy in copies:
        copy.start()
    count = state_ref.shape[0]
    mixed = rows * heads
    side = heads * latent
    lane = lax.broadcasted_iota(jnp.int32, (count, LANES), 1)
    row = lax.broadcasted_iota(jnp.int32, (count, LANES), 0) % rows
    column = lane % mixed
    own = (column // heads == row) & (lane < 2 * mixed)
    stats = state_ref[:, side:].astype(F32)
    shift = jnp.full((count, LANES), 2 * NEG, F32)
    for h in range(heads):
        shift = jnp.where(own & (column % heads == h), stats[:, 3 * h : 3 * h + 1], shift)
    best = jnp.max(shift, axis=0, keepdims=True)
    factor = jnp.where(own, jnp.exp(shift - best), 0.0)
    high = factor.astype(BF16).astype(F32)
    factor = jnp.where(lane < mixed, high, factor - high).astype(BF16)
    merged = lax.dot_general(
        factor, state_ref[...], (((0,), (0,)), ((), ())), preferred_element_type=F32
    )
    merged = merged[:mixed] + merged[mixed : 2 * mixed]
    parts = []
    for h in range(heads):
        total = merged[:, side + 3 * h + 1 : side + 3 * h + 2] + merged[:, side + 3 * h + 2 : side + 3 * h + 3]
        attended = (merged[:, h * latent : (h + 1) * latent] / total).astype(BF16)
        parts.append(jnp.dot(attended, w_uv_ref[h], preferred_element_type=F32))
    flat = jnp.concatenate(
        [
            jnp.concatenate([parts[h][r * heads + h : r * heads + h + 1] for h in range(heads)], axis=1)
            for r in range(rows)
        ],
        axis=0,
    ).astype(BF16)
    term = jnp.dot(flat[:, :split], first_ref[...], preferred_element_type=F32)
    for copy in copies:
        copy.wait()
    term += jnp.dot(flat[:, split:], second_ref[...], preferred_element_type=F32)
    term_ref[...] = term.astype(term_ref.dtype)


def local(q_latent, q_rope, latent_cache, page_table, lengths, w_uv, w_out):
    rows, heads, latent = q_latent.shape
    rope = q_rope.shape[2]
    pages, page_len, width = latent_cache.shape
    tokens = pages * page_len
    count = lax.axis_size(CTX)
    size = heads * (latent + rope)
    vmem = pl.BlockSpec(memory_space=pltpu.VMEM)
    smem = pl.BlockSpec(memory_space=pltpu.SMEM)
    hbm = pl.BlockSpec(memory_space=pl.ANY)
    stay = functools.partial(pltpu.with_memory_space_constraint, memory_space=pltpu.HBM)
    params = pltpu.CompilerParams(vmem_limit_bytes=16 << 20)
    dma = pltpu.SemaphoreType.DMA
    here = lax.axis_index(CTX).astype(jnp.int32)

    message = pl.pallas_call(
        message_kernel,
        out_shape=jax.ShapeDtypeStruct((rows, size), BF16),
        in_specs=[hbm, hbm],
        out_specs=vmem,
        scratch_shapes=[pltpu.VMEM(q_latent.shape, BF16), pltpu.VMEM(q_rope.shape, BF16), dma((2,))],
        compiler_params=params,
        name="message",
    )(stay(q_latent), stay(q_rope))

    near = 4
    others = {k: lax.ppermute(message, CTX, xor_pairs(count, k)) for k in (1, 3, 2)}
    split = w_out.shape[0] // 2
    live, keys, w_uv, w_first = pl.pallas_call(
        functools.partial(fetch_kernel, page_len),
        out_shape=(
            pltpu.VMEM((rows, tokens), F32),
            pltpu.VMEM((tokens, width), BF16),
            pltpu.VMEM(w_uv.shape, BF16),
            pltpu.VMEM((split, w_out.shape[1]), BF16),
        ),
        in_specs=[smem, hbm, hbm, hbm, hbm, hbm],
        out_specs=(vmem, vmem, vmem, vmem),
        scratch_shapes=[
            pltpu.SMEM(lengths.shape, jnp.int32), pltpu.VMEM(page_table.shape, jnp.int32), dma((5,)),
        ],
        compiler_params=params,
        cost_estimate=pl.CostEstimate(flops=0, bytes_accessed=5 << 20, transcendentals=0),
        name="fetch",
    )(
        here.reshape(1), stay(lengths), stay(page_table), stay(latent_cache.reshape(tokens, width)),
        stay(w_uv), stay(w_out),
    )
    away = lax.broadcasted_iota(jnp.int32, (near, 1, 1), 0) ^ (here % near)
    column = jnp.broadcast_to(message[None], (near, rows, size))
    for k in range(1, near):
        column = jnp.where(away == k, others[k][None], column)
    column, live, keys, w_uv, w_first = lax.optimization_barrier((column, live, keys, w_uv, w_first))
    planes = [[i * near + k for i in range(count // near)] for k in range(near)]
    query = lax.all_to_all(
        jnp.broadcast_to(column[None], (count // near, near, rows, size)),
        CTX, split_axis=0, concat_axis=0, axis_index_groups=planes, tiled=True,
    )

    state_size = heads * latent + LANES
    state = pl.pallas_call(
        functools.partial(attend_kernel, rows, heads, latent, rope),
        out_shape=jax.ShapeDtypeStruct((count * rows, state_size), BF16),
        in_specs=[vmem, vmem, vmem],
        out_specs=vmem,
        compiler_params=params,
        name="attend",
    )(query.reshape(count * rows, size), keys, live)

    state = lax.all_to_all(
        state.reshape(count, rows, state_size), CTX, split_axis=0, concat_axis=0, tiled=True
    )
    parts = 4
    term = pl.pallas_call(
        functools.partial(project_kernel, rows, heads, latent),
        out_shape=jax.ShapeDtypeStruct((rows, w_out.shape[1]), BF16),
        in_specs=[vmem, vmem, vmem, hbm],
        out_specs=vmem,
        scratch_shapes=[pltpu.VMEM((w_out.shape[0] - split, w_out.shape[1]), BF16), dma((parts,))],
        compiler_params=params,
        name="project",
    )(state.reshape(count * rows, state_size), w_uv, w_first, stay(w_out))
    for low in (4, 2, 0):
        term = sum_of_four(term, count, low).astype(BF16)
    return term


def solution(mesh):
    in_specs = (
        P("grp", "ctx", None),
        P("grp", "ctx", None),
        P(("grp", "ctx"), None, None),
        P("grp", None),
        P("grp"),
        P("ctx", None, None),
        P("ctx", None),
    )
    return jax.shard_map(local, mesh=mesh, in_specs=in_specs, out_specs=P("grp", None), check_vma=False)
```

```python
import functools
import jax
import jax.numpy as jnp
from jax import lax
from jax.experimental import pallas as pl
from jax.experimental.pallas import tpu as pltpu
from jax.sharding import PartitionSpec as P

ROPE = 64
V = 128
NEG = -1e30
CTX = "ctx"
LANES = 128
F32 = jnp.float32
BF16 = jnp.bfloat16


def xor_pairs(count, mask):
    return [(i, i ^ mask) for i in range(count)]


def sum_of_four(x, count, low):
    a, c, b = (lax.ppermute(x, CTX, xor_pairs(count, k << low)) for k in (1, 3, 2))
    return (x.astype(F32) + a.astype(F32)) + (c.astype(F32) + b.astype(F32))


def message_kernel(q_latent_hbm, q_rope_hbm, message_ref, q_latent_ref, q_rope_ref, sems):
    copies = [
        pltpu.make_async_copy(q_latent_hbm, q_latent_ref, sems.at[0]),
        pltpu.make_async_copy(q_rope_hbm, q_rope_ref, sems.at[1]),
    ]
    for copy in copies:
        copy.start()
    for copy in copies:
        copy.wait()
    rows, heads, _ = q_latent_ref.shape
    q_latent = q_latent_ref[...].astype(F32)
    q_rope = q_rope_ref[...].astype(F32)
    message = [
        jnp.concatenate(
            [q_latent[r, h : h + 1] for h in range(heads)] + [q_rope[r, h : h + 1] for h in range(heads)],
            axis=1,
        )
        for r in range(rows)
    ]
    message_ref[...] = jnp.concatenate(message, axis=0).astype(BF16)


def fetch_kernel(
    page_len, here_ref, lengths_hbm, table_hbm, cache_hbm, w_uv_hbm, w_out_hbm,
    live_ref, keys_ref, w_uv_ref, w_out_ref, lengths_ref, table_ref, sems,
):
    pairs = [
        (lengths_hbm, lengths_ref), (table_hbm, table_ref), (cache_hbm, keys_ref), (w_uv_hbm, w_uv_ref),
        (w_out_hbm.at[: w_out_ref.shape[0]], w_out_ref),
    ]
    copies = [pltpu.make_async_copy(a, b, sems.at[k]) for k, (a, b) in enumerate(pairs)]
    for copy in copies:
        copy.start()
    copies[0].wait()
    copies[1].wait()
    rows = live_ref.shape[0]
    tokens = keys_ref.shape[0]
    pages = tokens // page_len
    slots = table_ref.shape[1]
    page = here_ref[0] * pages + lax.broadcasted_iota(jnp.int32, (pages, slots), 0)
    place = lax.broadcasted_iota(jnp.int32, (pages, slots), 1)
    token = lax.broadcasted_iota(jnp.int32, (pages, tokens), 1)
    mine = token // page_len == lax.broadcasted_iota(jnp.int32, (pages, tokens), 0)
    for r in range(rows):
        hit = jnp.broadcast_to(table_ref[r : r + 1, :], (pages, slots)) == page
        room = jnp.where(hit, lengths_ref[r] - place * page_len, 0)
        room = jnp.max(room, axis=1, keepdims=True)
        alive = mine & (token % page_len < room)
        live_ref[r : r + 1, :] = jnp.max(jnp.where(alive, 1.0, 0.0), axis=0, keepdims=True)
    for copy in copies[2:]:
        copy.wait()


def attend_kernel(rows, heads, latent, rope, q_ref, keys_ref, live_ref, state_ref):
    count = q_ref.shape[0]
    tokens = keys_ref.shape[0]
    row = lax.broadcasted_iota(jnp.int32, (count, 1), 0) % rows
    live = jnp.broadcast_to(live_ref[0:1, :], (count, tokens))
    for r in range(1, rows):
        live = jnp.where(row == r, live_ref[r : r + 1, :], live)
    live = live > 0.5
    side = heads * latent
    lane = lax.broadcasted_iota(jnp.int32, (count, state_ref.shape[1] - side), 1)
    stats = jnp.zeros(lane.shape, F32)
    for h in range(heads):
        query = jnp.concatenate(
            [q_ref[:, h * latent : (h + 1) * latent], q_ref[:, side + h * rope : side + (h + 1) * rope]], axis=1
        )
        scores = lax.dot_general(
            query, keys_ref[...], (((1,), (1,)), ((), ())), preferred_element_type=F32
        ) * ((V + ROPE) ** (-0.5))
        scores = jnp.where(live, scores, NEG)
        shift = jnp.max(scores, axis=1, keepdims=True).astype(BF16).astype(F32)
        weights = jnp.where(live, jnp.exp(scores - shift), 0.0).astype(BF16)
        total = jnp.sum(weights.astype(F32), axis=1, keepdims=True)
        outs = jnp.dot(weights, keys_ref[:, :latent], preferred_element_type=F32)
        state_ref[:, h * latent : (h + 1) * latent] = outs.astype(BF16)
        high = total.astype(BF16).astype(F32)
        for k, value in enumerate((shift, high, total - high)):
            stats = jnp.where(lane == 3 * h + k, value, stats)
    state_ref[:, side:] = stats.astype(BF16)


def project_kernel(rows, heads, latent, state_ref, w_uv_ref, first_ref, w_out_hbm, term_ref, second_ref, sems):
    split = first_ref.shape[0]
    parts = sems.shape[0]
    step = second_ref.shape[0] // parts
    copies = [
        pltpu.make_async_copy(
            w_out_hbm.at[split + k * step : split + (k + 1) * step], second_ref.at[k * step : (k + 1) * step], sems.at[k]
        )
        for k in range(parts)
    ]
    for copy in copies:
        copy.start()
    count = state_ref.shape[0]
    mixed = rows * heads
    side = heads * latent
    lane = lax.broadcasted_iota(jnp.int32, (count, LANES), 1)
    row = lax.broadcasted_iota(jnp.int32, (count, LANES), 0) % rows
    column = lane % mixed
    own = (column // heads == row) & (lane < 2 * mixed)
    stats = state_ref[:, side:].astype(F32)
    shift = jnp.full((count, LANES), 2 * NEG, F32)
    for h in range(heads):
        shift = jnp.where(own & (column % heads == h), stats[:, 3 * h : 3 * h + 1], shift)
    best = jnp.max(shift, axis=0, keepdims=True)
    factor = jnp.where(own, jnp.exp(shift - best), 0.0)
    high = factor.astype(BF16).astype(F32)
    factor = jnp.where(lane < mixed, high, factor - high).astype(BF16)
    merged = lax.dot_general(
        factor, state_ref[...], (((0,), (0,)), ((), ())), preferred_element_type=F32
    )
    merged = merged[:mixed] + merged[mixed : 2 * mixed]
    parts = []
    for h in range(heads):
        total = merged[:, side + 3 * h + 1 : side + 3 * h + 2] + merged[:, side + 3 * h + 2 : side + 3 * h + 3]
        attended = (merged[:, h * latent : (h + 1) * latent] / total).astype(BF16)
        parts.append(jnp.dot(attended, w_uv_ref[h], preferred_element_type=F32))
    flat = jnp.concatenate(
        [
            jnp.concatenate([parts[h][r * heads + h : r * heads + h + 1] for h in range(heads)], axis=1)
            for r in range(rows)
        ],
        axis=0,
    ).astype(BF16)
    term = jnp.dot(flat[:, :split], first_ref[...], preferred_element_type=F32)
    for copy in copies:
        copy.wait()
    term += jnp.dot(flat[:, split:], second_ref[...], preferred_element_type=F32)
    term_ref[...] = term.astype(term_ref.dtype)


def local(q_latent, q_rope, latent_cache, page_table, lengths, w_uv, w_out):
    rows, heads, latent = q_latent.shape
    rope = q_rope.shape[2]
    pages, page_len, width = latent_cache.shape
    tokens = pages * page_len
    count = lax.axis_size(CTX)
    size = heads * (latent + rope)
    vmem = pl.BlockSpec(memory_space=pltpu.VMEM)
    smem = pl.BlockSpec(memory_space=pltpu.SMEM)
    hbm = pl.BlockSpec(memory_space=pl.ANY)
    stay = functools.partial(pltpu.with_memory_space_constraint, memory_space=pltpu.HBM)
    params = pltpu.CompilerParams(vmem_limit_bytes=16 << 20)
    dma = pltpu.SemaphoreType.DMA
    here = lax.axis_index(CTX).astype(jnp.int32)

    message = pl.pallas_call(
        message_kernel,
        out_shape=jax.ShapeDtypeStruct((rows, size), BF16),
        in_specs=[hbm, hbm],
        out_specs=vmem,
        scratch_shapes=[pltpu.VMEM(q_latent.shape, BF16), pltpu.VMEM(q_rope.shape, BF16), dma((2,))],
        compiler_params=params,
        name="message",
    )(stay(q_latent), stay(q_rope))

    near = 4
    others = {k: lax.ppermute(message, CTX, xor_pairs(count, k)) for k in (1, 3, 2)}
    split = w_out.shape[0] // 2
    live, keys, w_uv, w_first = pl.pallas_call(
        functools.partial(fetch_kernel, page_len),
        out_shape=(
            pltpu.VMEM((rows, tokens), F32),
            pltpu.VMEM((tokens, width), BF16),
            pltpu.VMEM(w_uv.shape, BF16),
            pltpu.VMEM((split, w_out.shape[1]), BF16),
        ),
        in_specs=[smem, hbm, hbm, hbm, hbm, hbm],
        out_specs=(vmem, vmem, vmem, vmem),
        scratch_shapes=[
            pltpu.SMEM(lengths.shape, jnp.int32), pltpu.VMEM(page_table.shape, jnp.int32), dma((5,)),
        ],
        compiler_params=params,
        cost_estimate=pl.CostEstimate(flops=0, bytes_accessed=5 << 20, transcendentals=0),
        name="fetch",
    )(
        here.reshape(1), stay(lengths), stay(page_table), stay(latent_cache.reshape(tokens, width)),
        stay(w_uv), stay(w_out),
    )
    away = lax.broadcasted_iota(jnp.int32, (near, 1, 1), 0) ^ (here % near)
    column = jnp.broadcast_to(message[None], (near, rows, size))
    for k in (2, 1, 3):
        column = jnp.where(away == k, others[k][None], column)
    column, live, keys, w_uv, w_first = lax.optimization_barrier((column, live, keys, w_uv, w_first))
    planes = [[i * near + k for i in range(count // near)] for k in range(near)]
    query = lax.all_to_all(
        jnp.broadcast_to(column[None], (count // near, near, rows, size)),
        CTX, split_axis=0, concat_axis=0, axis_index_groups=planes, tiled=True,
    )

    state_size = heads * latent + LANES
    state = pl.pallas_call(
        functools.partial(attend_kernel, rows, heads, latent, rope),
        out_shape=jax.ShapeDtypeStruct((count * rows, state_size), BF16),
        in_specs=[vmem, vmem, vmem],
        out_specs=vmem,
        compiler_params=params,
        name="attend",
    )(query.reshape(count * rows, size), keys, live)

    state = lax.all_to_all(
        state.reshape(count, rows, state_size), CTX, split_axis=0, concat_axis=0, tiled=True
    )
    parts = 4
    term = pl.pallas_call(
        functools.partial(project_kernel, rows, heads, latent),
        out_shape=jax.ShapeDtypeStruct((rows, w_out.shape[1]), BF16),
        in_specs=[vmem, vmem, vmem, hbm],
        out_specs=vmem,
        scratch_shapes=[pltpu.VMEM((w_out.shape[0] - split, w_out.shape[1]), BF16), dma((parts,))],
        compiler_params=params,
        name="project",
    )(state.reshape(count * rows, state_size), w_uv, w_first, stay(w_out))
    for low in (4, 2, 0):
        term = sum_of_four(term, count, low).astype(BF16)
    return term


def solution(mesh):
    in_specs = (
        P("grp", "ctx", None),
        P("grp", "ctx", None),
        P(("grp", "ctx"), None, None),
        P("grp", None),
        P("grp"),
        P("ctx", None, None),
        P("ctx", None),
    )
    return jax.shard_map(local, mesh=mesh, in_specs=in_specs, out_specs=P("grp", None), check_vma=False)
```

```python
import functools
import jax
import jax.numpy as jnp
from jax import lax
from jax.experimental import pallas as pl
from jax.experimental.pallas import tpu as pltpu
from jax.sharding import PartitionSpec as P

ROPE = 64
V = 128
NEG = -1e30
CTX = "ctx"
LANES = 128
F32 = jnp.float32
BF16 = jnp.bfloat16


def xor_pairs(count, mask):
    return [(i, i ^ mask) for i in range(count)]


def sum_of_four(x, count, low):
    a, c, b = (lax.ppermute(x, CTX, xor_pairs(count, k << low)) for k in (1, 3, 2))
    return (x.astype(F32) + a.astype(F32)) + (c.astype(F32) + b.astype(F32))


def message_kernel(q_latent_hbm, q_rope_hbm, message_ref, q_latent_ref, q_rope_ref, sems):
    copies = [
        pltpu.make_async_copy(q_latent_hbm, q_latent_ref, sems.at[0]),
        pltpu.make_async_copy(q_rope_hbm, q_rope_ref, sems.at[1]),
    ]
    for copy in copies:
        copy.start()
    for copy in copies:
        copy.wait()
    rows, heads, _ = q_latent_ref.shape
    q_latent = q_latent_ref[...].astype(F32)
    q_rope = q_rope_ref[...].astype(F32)
    message = [
        jnp.concatenate(
            [q_latent[r, h : h + 1] for h in range(heads)] + [q_rope[r, h : h + 1] for h in range(heads)],
            axis=1,
        )
        for r in range(rows)
    ]
    message_ref[...] = jnp.concatenate(message, axis=0).astype(BF16)


def fetch_kernel(
    page_len, here_ref, lengths_hbm, table_hbm, cache_hbm, w_uv_hbm, w_out_hbm,
    live_ref, keys_ref, w_uv_ref, w_out_ref, lengths_ref, table_ref, sems,
):
    pairs = [
        (lengths_hbm, lengths_ref), (table_hbm, table_ref), (cache_hbm, keys_ref), (w_uv_hbm, w_uv_ref),
        (w_out_hbm.at[: w_out_ref.shape[0]], w_out_ref),
    ]
    copies = [pltpu.make_async_copy(a, b, sems.at[k]) for k, (a, b) in enumerate(pairs)]
    for copy in copies:
        copy.start()
    copies[0].wait()
    copies[1].wait()
    rows = live_ref.shape[0]
    tokens = keys_ref.shape[0]
    pages = tokens // page_len
    slots = table_ref.shape[1]
    page = here_ref[0] * pages + lax.broadcasted_iota(jnp.int32, (pages, slots), 0)
    place = lax.broadcasted_iota(jnp.int32, (pages, slots), 1)
    token = lax.broadcasted_iota(jnp.int32, (pages, tokens), 1)
    mine = token // page_len == lax.broadcasted_iota(jnp.int32, (pages, tokens), 0)
    for r in range(rows):
        hit = jnp.broadcast_to(table_ref[r : r + 1, :], (pages, slots)) == page
        room = jnp.where(hit, lengths_ref[r] - place * page_len, 0)
        room = jnp.max(room, axis=1, keepdims=True)
        alive = mine & (token % page_len < room)
        live_ref[r : r + 1, :] = jnp.max(jnp.where(alive, 1.0, 0.0), axis=0, keepdims=True)
    for copy in copies[2:]:
        copy.wait()


def attend_kernel(rows, heads, latent, rope, q_ref, keys_ref, live_ref, state_ref):
    count = q_ref.shape[0]
    tokens = keys_ref.shape[0]
    row = lax.broadcasted_iota(jnp.int32, (count, 1), 0) % rows
    live = jnp.broadcast_to(live_ref[0:1, :], (count, tokens))
    for r in range(1, rows):
        live = jnp.where(row == r, live_ref[r : r + 1, :], live)
    live = live > 0.5
    side = heads * latent
    lane = lax.broadcasted_iota(jnp.int32, (count, state_ref.shape[1] - side), 1)
    stats = jnp.zeros(lane.shape, F32)
    for h in range(heads):
        query = jnp.concatenate(
            [q_ref[:, h * latent : (h + 1) * latent], q_ref[:, side + h * rope : side + (h + 1) * rope]], axis=1
        )
        scores = lax.dot_general(
            query, keys_ref[...], (((1,), (1,)), ((), ())), preferred_element_type=F32
        ) * ((V + ROPE) ** (-0.5))
        scores = jnp.where(live, scores, NEG)
        shift = jnp.max(scores, axis=1, keepdims=True).astype(BF16).astype(F32)
        weights = jnp.where(live, jnp.exp(scores - shift), 0.0).astype(BF16)
        total = jnp.sum(weights.astype(F32), axis=1, keepdims=True)
        outs = jnp.dot(weights, keys_ref[:, :latent], preferred_element_type=F32)
        state_ref[:, h * latent : (h + 1) * latent] = outs.astype(BF16)
        high = total.astype(BF16).astype(F32)
        for k, value in enumerate((shift, high, total - high)):
            stats = jnp.where(lane == 3 * h + k, value, stats)
    state_ref[:, side:] = stats.astype(BF16)


def project_kernel(rows, heads, latent, state_ref, w_uv_ref, first_ref, w_out_hbm, term_ref, second_ref, sems):
    split = first_ref.shape[0]
    parts = sems.shape[0]
    step = second_ref.shape[0] // parts
    copies = [
        pltpu.make_async_copy(
            w_out_hbm.at[split + k * step : split + (k + 1) * step], second_ref.at[k * step : (k + 1) * step], sems.at[k]
        )
        for k in range(parts)
    ]
    for copy in copies:
        copy.start()
    count = state_ref.shape[0]
    mixed = rows * heads
    side = heads * latent
    lane = lax.broadcasted_iota(jnp.int32, (count, LANES), 1)
    row = lax.broadcasted_iota(jnp.int32, (count, LANES), 0) % rows
    column = lane % mixed
    own = (column // heads == row) & (lane < 2 * mixed)
    stats = state_ref[:, side:].astype(F32)
    shift = jnp.full((count, LANES), 2 * NEG, F32)
    for h in range(heads):
        shift = jnp.where(own & (column % heads == h), stats[:, 3 * h : 3 * h + 1], shift)
    best = jnp.max(shift, axis=0, keepdims=True)
    factor = jnp.where(own, jnp.exp(shift - best), 0.0)
    high = factor.astype(BF16).astype(F32)
    factor = jnp.where(lane < mixed, high, factor - high).astype(BF16)
    merged = lax.dot_general(
        factor, state_ref[...], (((0,), (0,)), ((), ())), preferred_element_type=F32
    )
    merged = merged[:mixed] + merged[mixed : 2 * mixed]
    parts = []
    for h in range(heads):
        total = merged[:, side + 3 * h + 1 : side + 3 * h + 2] + merged[:, side + 3 * h + 2 : side + 3 * h + 3]
        attended = (merged[:, h * latent : (h + 1) * latent] / total).astype(BF16)
        parts.append(jnp.dot(attended, w_uv_ref[h], preferred_element_type=F32))
    flat = jnp.concatenate(
        [
            jnp.concatenate([parts[h][r * heads + h : r * heads + h + 1] for h in range(heads)], axis=1)
            for r in range(rows)
        ],
        axis=0,
    ).astype(BF16)
    term = jnp.dot(flat[:, :split], first_ref[...], preferred_element_type=F32)
    for k, copy in enumerate(copies):
        copy.wait()
        term += jnp.dot(
            flat[:, split + k * step : split + (k + 1) * step],
            second_ref[k * step : (k + 1) * step],
            preferred_element_type=F32,
        )
    term_ref[...] = term.astype(term_ref.dtype)


def local(q_latent, q_rope, latent_cache, page_table, lengths, w_uv, w_out):
    rows, heads, latent = q_latent.shape
    rope = q_rope.shape[2]
    pages, page_len, width = latent_cache.shape
    tokens = pages * page_len
    count = lax.axis_size(CTX)
    size = heads * (latent + rope)
    vmem = pl.BlockSpec(memory_space=pltpu.VMEM)
    smem = pl.BlockSpec(memory_space=pltpu.SMEM)
    hbm = pl.BlockSpec(memory_space=pl.ANY)
    stay = functools.partial(pltpu.with_memory_space_constraint, memory_space=pltpu.HBM)
    params = pltpu.CompilerParams(vmem_limit_bytes=16 << 20)
    dma = pltpu.SemaphoreType.DMA
    here = lax.axis_index(CTX).astype(jnp.int32)

    message = pl.pallas_call(
        message_kernel,
        out_shape=jax.ShapeDtypeStruct((rows, size), BF16),
        in_specs=[hbm, hbm],
        out_specs=vmem,
        scratch_shapes=[pltpu.VMEM(q_latent.shape, BF16), pltpu.VMEM(q_rope.shape, BF16), dma((2,))],
        compiler_params=params,
        name="message",
    )(stay(q_latent), stay(q_rope))

    near = 4
    others = {k: lax.ppermute(message, CTX, xor_pairs(count, k)) for k in (1, 3, 2)}
    split = w_out.shape[0] // 2
    live, keys, w_uv, w_first = pl.pallas_call(
        functools.partial(fetch_kernel, page_len),
        out_shape=(
            pltpu.VMEM((rows, tokens), F32),
            pltpu.VMEM((tokens, width), BF16),
            pltpu.VMEM(w_uv.shape, BF16),
            pltpu.VMEM((split, w_out.shape[1]), BF16),
        ),
        in_specs=[smem, hbm, hbm, hbm, hbm, hbm],
        out_specs=(vmem, vmem, vmem, vmem),
        scratch_shapes=[
            pltpu.SMEM(lengths.shape, jnp.int32), pltpu.VMEM(page_table.shape, jnp.int32), dma((5,)),
        ],
        compiler_params=params,
        cost_estimate=pl.CostEstimate(flops=0, bytes_accessed=5 << 20, transcendentals=0),
        name="fetch",
    )(
        here.reshape(1), stay(lengths), stay(page_table), stay(latent_cache.reshape(tokens, width)),
        stay(w_uv), stay(w_out),
    )
    away = lax.broadcasted_iota(jnp.int32, (near, 1, 1), 0) ^ (here % near)
    column = jnp.broadcast_to(message[None], (near, rows, size))
    for k in (2, 1, 3):
        column = jnp.where(away == k, others[k][None], column)
    column, live, keys, w_uv, w_first = lax.optimization_barrier((column, live, keys, w_uv, w_first))
    planes = [[i * near + k for i in range(count // near)] for k in range(near)]
    query = lax.all_to_all(
        jnp.broadcast_to(column[None], (count // near, near, rows, size)),
        CTX, split_axis=0, concat_axis=0, axis_index_groups=planes, tiled=True,
    )

    state_size = heads * latent + LANES
    state = pl.pallas_call(
        functools.partial(attend_kernel, rows, heads, latent, rope),
        out_shape=jax.ShapeDtypeStruct((count * rows, state_size), BF16),
        in_specs=[vmem, vmem, vmem],
        out_specs=vmem,
        compiler_params=params,
        name="attend",
    )(query.reshape(count * rows, size), keys, live)

    state = lax.all_to_all(
        state.reshape(count, rows, state_size), CTX, split_axis=0, concat_axis=0, tiled=True
    )
    parts = 2
    term = pl.pallas_call(
        functools.partial(project_kernel, rows, heads, latent),
        out_shape=jax.ShapeDtypeStruct((rows, w_out.shape[1]), BF16),
        in_specs=[vmem, vmem, vmem, hbm],
        out_specs=vmem,
        scratch_shapes=[pltpu.VMEM((w_out.shape[0] - split, w_out.shape[1]), BF16), dma((parts,))],
        compiler_params=params,
        name="project",
    )(state.reshape(count * rows, state_size), w_uv, w_first, stay(w_out))
    for low in (4, 2, 0):
        term = sum_of_four(term, count, low).astype(BF16)
    return term


def solution(mesh):
    in_specs = (
        P("grp", "ctx", None),
        P("grp", "ctx", None),
        P(("grp", "ctx"), None, None),
        P("grp", None),
        P("grp"),
        P("ctx", None, None),
        P("ctx", None),
    )
    return jax.shard_map(local, mesh=mesh, in_specs=in_specs, out_specs=P("grp", None), check_vma=False)
```

```python
import functools
import jax
import jax.numpy as jnp
from jax import lax
from jax.experimental import pallas as pl
from jax.experimental.pallas import tpu as pltpu
from jax.sharding import PartitionSpec as P

ROPE = 64
V = 128
NEG = -1e30
CTX = "ctx"
LANES = 128
F32 = jnp.float32
BF16 = jnp.bfloat16


def xor_pairs(count, mask):
    return [(i, i ^ mask) for i in range(count)]


def sum_of_four(x, count, low):
    a, c, b = (lax.ppermute(x, CTX, xor_pairs(count, k << low)) for k in (1, 3, 2))
    return (x.astype(F32) + a.astype(F32)) + (c.astype(F32) + b.astype(F32))


def message_kernel(q_latent_hbm, q_rope_hbm, message_ref, q_latent_ref, q_rope_ref, sems):
    copies = [
        pltpu.make_async_copy(q_latent_hbm, q_latent_ref, sems.at[0]),
        pltpu.make_async_copy(q_rope_hbm, q_rope_ref, sems.at[1]),
    ]
    for copy in copies:
        copy.start()
    for copy in copies:
        copy.wait()
    rows, heads, _ = q_latent_ref.shape
    q_latent = q_latent_ref[...].astype(F32)
    q_rope = q_rope_ref[...].astype(F32)
    message = [
        jnp.concatenate(
            [q_latent[r, h : h + 1] for h in range(heads)] + [q_rope[r, h : h + 1] for h in range(heads)],
            axis=1,
        )
        for r in range(rows)
    ]
    message_ref[...] = jnp.concatenate(message, axis=0).astype(BF16)


def fetch_kernel(
    page_len, here_ref, lengths_hbm, table_hbm, cache_hbm, w_uv_hbm, w_out_hbm,
    live_ref, keys_ref, w_uv_ref, w_out_ref, lengths_ref, table_ref, sems,
):
    pairs = [
        (lengths_hbm, lengths_ref), (table_hbm, table_ref), (cache_hbm, keys_ref), (w_uv_hbm, w_uv_ref),
        (w_out_hbm, w_out_ref),
    ]
    copies = [pltpu.make_async_copy(a, b, sems.at[k]) for k, (a, b) in enumerate(pairs)]
    for copy in copies:
        copy.start()
    copies[0].wait()
    copies[1].wait()
    rows = live_ref.shape[0]
    tokens = keys_ref.shape[0]
    pages = tokens // page_len
    slots = table_ref.shape[1]
    page = here_ref[0] * pages + lax.broadcasted_iota(jnp.int32, (pages, slots), 0)
    place = lax.broadcasted_iota(jnp.int32, (pages, slots), 1)
    token = lax.broadcasted_iota(jnp.int32, (pages, tokens), 1)
    mine = token // page_len == lax.broadcasted_iota(jnp.int32, (pages, tokens), 0)
    for r in range(rows):
        hit = jnp.broadcast_to(table_ref[r : r + 1, :], (pages, slots)) == page
        room = jnp.where(hit, lengths_ref[r] - place * page_len, 0)
        room = jnp.max(room, axis=1, keepdims=True)
        alive = mine & (token % page_len < room)
        live_ref[r : r + 1, :] = jnp.max(jnp.where(alive, 1.0, 0.0), axis=0, keepdims=True)
    for copy in copies[2:]:
        copy.wait()


def attend_kernel(rows, heads, latent, rope, q_ref, keys_ref, live_ref, state_ref):
    size = q_ref.shape[2]
    count = q_ref.shape[0] * rows
    queries = q_ref[...].reshape(count, size)
    tokens = keys_ref.shape[0]
    row = lax.broadcasted_iota(jnp.int32, (count, 1), 0) % rows
    live = jnp.broadcast_to(live_ref[0:1, :], (count, tokens))
    for r in range(1, rows):
        live = jnp.where(row == r, live_ref[r : r + 1, :], live)
    live = live > 0.5
    side = heads * latent
    lane = lax.broadcasted_iota(jnp.int32, (count, LANES), 1)
    stats = jnp.zeros(lane.shape, F32)
    states = []
    for h in range(heads):
        query = jnp.concatenate(
            [queries[:, h * latent : (h + 1) * latent], queries[:, side + h * rope : side + (h + 1) * rope]], axis=1
        )
        scores = lax.dot_general(
            query, keys_ref[...], (((1,), (1,)), ((), ())), preferred_element_type=F32
        ) * ((V + ROPE) ** (-0.5))
        scores = jnp.where(live, scores, NEG)
        shift = jnp.max(scores, axis=1, keepdims=True).astype(BF16).astype(F32)
        weights = jnp.where(live, jnp.exp(scores - shift), 0.0).astype(BF16)
        total = jnp.sum(weights.astype(F32), axis=1, keepdims=True)
        outs = jnp.dot(weights, keys_ref[:, :latent], preferred_element_type=F32)
        states.append(outs.astype(BF16))
        high = total.astype(BF16).astype(F32)
        for k, value in enumerate((shift, high, total - high)):
            stats = jnp.where(lane == 3 * h + k, value, stats)
    states.append(stats.astype(BF16))
    state_ref[...] = jnp.concatenate(states, axis=1).reshape(state_ref.shape)


def project_kernel(rows, heads, latent, messages_ref, w_uv_ref, w_out_ref, term_ref):
    count = messages_ref.shape[0] * rows
    states = messages_ref[...].reshape(count, messages_ref.shape[2])
    mixed = rows * heads
    side = heads * latent
    lane = lax.broadcasted_iota(jnp.int32, (count, LANES), 1)
    row = lax.broadcasted_iota(jnp.int32, (count, LANES), 0) % rows
    column = lane % mixed
    own = (column // heads == row) & (lane < 2 * mixed)
    stats = states[:, side:].astype(F32)
    shift = jnp.full((count, LANES), 2 * NEG, F32)
    for h in range(heads):
        shift = jnp.where(own & (column % heads == h), stats[:, 3 * h : 3 * h + 1], shift)
    best = jnp.max(shift, axis=0, keepdims=True)
    factor = jnp.where(own, jnp.exp(shift - best), 0.0)
    high = factor.astype(BF16).astype(F32)
    factor = jnp.where(lane < mixed, high, factor - high).astype(BF16)
    merged = lax.dot_general(
        factor, states, (((0,), (0,)), ((), ())), preferred_element_type=F32
    )
    merged = merged[:mixed] + merged[mixed : 2 * mixed]
    parts = []
    for h in range(heads):
        total = merged[:, side + 3 * h + 1 : side + 3 * h + 2] + merged[:, side + 3 * h + 2 : side + 3 * h + 3]
        attended = (merged[:, h * latent : (h + 1) * latent] / total).astype(BF16)
        parts.append(jnp.dot(attended, w_uv_ref[h], preferred_element_type=F32))
    flat = jnp.concatenate(
        [
            jnp.concatenate([parts[h][r * heads + h : r * heads + h + 1] for h in range(heads)], axis=1)
            for r in range(rows)
        ],
        axis=0,
    ).astype(BF16)
    term_ref[...] = jnp.dot(flat, w_out_ref[...], preferred_element_type=F32).astype(term_ref.dtype)


def local(q_latent, q_rope, latent_cache, page_table, lengths, w_uv, w_out):
    rows, heads, latent = q_latent.shape
    rope = q_rope.shape[2]
    pages, page_len, width = latent_cache.shape
    tokens = pages * page_len
    count = lax.axis_size(CTX)
    size = heads * (latent + rope)
    vmem = pl.BlockSpec(memory_space=pltpu.VMEM)
    smem = pl.BlockSpec(memory_space=pltpu.SMEM)
    hbm = pl.BlockSpec(memory_space=pl.ANY)
    stay = functools.partial(pltpu.with_memory_space_constraint, memory_space=pltpu.HBM)
    params = pltpu.CompilerParams(vmem_limit_bytes=16 << 20)
    dma = pltpu.SemaphoreType.DMA
    here = lax.axis_index(CTX).astype(jnp.int32)

    message = pl.pallas_call(
        message_kernel,
        out_shape=jax.ShapeDtypeStruct((rows, size), BF16),
        in_specs=[hbm, hbm],
        out_specs=vmem,
        scratch_shapes=[pltpu.VMEM(q_latent.shape, BF16), pltpu.VMEM(q_rope.shape, BF16), dma((2,))],
        compiler_params=params,
        name="message",
    )(stay(q_latent), stay(q_rope))

    near = 4
    others = {k: lax.ppermute(message, CTX, xor_pairs(count, k)) for k in (1, 3, 2)}
    live, keys, w_uv, w_out_near = pl.pallas_call(
        functools.partial(fetch_kernel, page_len),
        out_shape=(
            pltpu.VMEM((rows, tokens), F32),
            pltpu.VMEM((tokens, width), BF16),
            pltpu.VMEM(w_uv.shape, BF16),
            pltpu.VMEM(w_out.shape, BF16),
        ),
        in_specs=[smem, hbm, hbm, hbm, hbm, hbm],
        out_specs=(vmem, vmem, vmem, vmem),
        scratch_shapes=[
            pltpu.SMEM(lengths.shape, jnp.int32), pltpu.VMEM(page_table.shape, jnp.int32), dma((5,)),
        ],
        compiler_params=params,
        cost_estimate=pl.CostEstimate(flops=0, bytes_accessed=5 << 20, transcendentals=0),
        name="fetch",
    )(
        here.reshape(1), stay(lengths), stay(page_table), stay(latent_cache.reshape(tokens, width)),
        stay(w_uv), stay(w_out),
    )
    away = lax.broadcasted_iota(jnp.int32, (near, 1, 1), 0) ^ (here % near)
    column = jnp.broadcast_to(message[None], (near, rows, size))
    for k in (2, 1, 3):
        column = jnp.where(away == k, others[k][None], column)
    column, live, keys, w_uv, w_out_near = lax.optimization_barrier((column, live, keys, w_uv, w_out_near))
    planes = [[i * near + k for i in range(count // near)] for k in range(near)]
    query = lax.all_to_all(
        jnp.broadcast_to(column[None], (count // near, near, rows, size)),
        CTX, split_axis=0, concat_axis=0, axis_index_groups=planes, tiled=True,
    )

    state_size = heads * latent + LANES
    state = pl.pallas_call(
        functools.partial(attend_kernel, rows, heads, latent, rope),
        out_shape=jax.ShapeDtypeStruct((count, rows, state_size), BF16),
        in_specs=[vmem, vmem, vmem],
        out_specs=vmem,
        compiler_params=params,
        name="attend",
    )(query.reshape(count, rows, size), keys, live)

    state = lax.all_to_all(state, CTX, split_axis=0, concat_axis=0, tiled=True)
    term = pl.pallas_call(
        functools.partial(project_kernel, rows, heads, latent),
        out_shape=jax.ShapeDtypeStruct((rows, w_out.shape[1]), BF16),
        in_specs=[vmem, vmem, vmem],
        out_specs=vmem,
        compiler_params=params,
        name="project",
    )(state, w_uv, w_out_near)
    for low in (4, 2, 0):
        term = sum_of_four(term, count, low).astype(BF16)
    return term


def solution(mesh):
    in_specs = (
        P("grp", "ctx", None),
        P("grp", "ctx", None),
        P(("grp", "ctx"), None, None),
        P("grp", None),
        P("grp"),
        P("ctx", None, None),
        P("ctx", None),
    )
    return jax.shard_map(local, mesh=mesh, in_specs=in_specs, out_specs=P("grp", None), check_vma=False)
```

```python
import functools
import jax
import jax.numpy as jnp
from jax import lax
from jax.experimental import pallas as pl
from jax.experimental.pallas import tpu as pltpu
from jax.sharding import PartitionSpec as P

ROPE = 64
V = 128
NEG = -1e30
CTX = "ctx"
LANES = 128
F32 = jnp.float32
BF16 = jnp.bfloat16


def xor_pairs(count, mask):
    return [(i, i ^ mask) for i in range(count)]


def sum_of_four(x, count, low):
    a, c, b = (lax.ppermute(x, CTX, xor_pairs(count, k << low)) for k in (1, 3, 2))
    return (x.astype(F32) + c.astype(F32)) + (a.astype(F32) + b.astype(F32))


def message_kernel(q_latent_hbm, q_rope_hbm, message_ref, q_latent_ref, q_rope_ref, sems):
    copies = [
        pltpu.make_async_copy(q_latent_hbm, q_latent_ref, sems.at[0]),
        pltpu.make_async_copy(q_rope_hbm, q_rope_ref, sems.at[1]),
    ]
    for copy in copies:
        copy.start()
    for copy in copies:
        copy.wait()
    rows, heads, _ = q_latent_ref.shape
    q_latent = q_latent_ref[...].astype(F32)
    q_rope = q_rope_ref[...].astype(F32)
    message = [
        jnp.concatenate(
            [q_latent[r, h : h + 1] for h in range(heads)] + [q_rope[r, h : h + 1] for h in range(heads)],
            axis=1,
        )
        for r in range(rows)
    ]
    message_ref[...] = jnp.concatenate(message, axis=0).astype(BF16)


def fetch_kernel(
    page_len, here_ref, lengths_hbm, table_hbm, cache_hbm, w_uv_hbm, w_out_hbm,
    live_ref, keys_ref, w_uv_ref, w_out_ref, lengths_ref, table_ref, sems,
):
    pairs = [
        (lengths_hbm, lengths_ref), (table_hbm, table_ref), (cache_hbm, keys_ref), (w_uv_hbm, w_uv_ref),
        (w_out_hbm, w_out_ref),
    ]
    copies = [pltpu.make_async_copy(a, b, sems.at[k]) for k, (a, b) in enumerate(pairs)]
    for copy in copies:
        copy.start()
    copies[0].wait()
    copies[1].wait()
    rows = live_ref.shape[0]
    tokens = keys_ref.shape[0]
    pages = tokens // page_len
    slots = table_ref.shape[1]
    page = here_ref[0] * pages + lax.broadcasted_iota(jnp.int32, (pages, slots), 0)
    place = lax.broadcasted_iota(jnp.int32, (pages, slots), 1)
    token = lax.broadcasted_iota(jnp.int32, (pages, tokens), 1)
    mine = token // page_len == lax.broadcasted_iota(jnp.int32, (pages, tokens), 0)
    for r in range(rows):
        hit = jnp.broadcast_to(table_ref[r : r + 1, :], (pages, slots)) == page
        room = jnp.where(hit, lengths_ref[r] - place * page_len, 0)
        room = jnp.max(room, axis=1, keepdims=True)
        alive = mine & (token % page_len < room)
        live_ref[r : r + 1, :] = jnp.max(jnp.where(alive, 1.0, 0.0), axis=0, keepdims=True)
    for copy in copies[2:]:
        copy.wait()


def attend_kernel(rows, heads, latent, rope, q_ref, keys_ref, live_ref, state_ref):
    size = q_ref.shape[2]
    count = q_ref.shape[0] * rows
    queries = q_ref[...].reshape(count, size)
    tokens = keys_ref.shape[0]
    row = lax.broadcasted_iota(jnp.int32, (count, 1), 0) % rows
    live = jnp.broadcast_to(live_ref[0:1, :], (count, tokens))
    for r in range(1, rows):
        live = jnp.where(row == r, live_ref[r : r + 1, :], live)
    live = live > 0.5
    side = heads * latent
    lane = lax.broadcasted_iota(jnp.int32, (count, LANES), 1)
    stats = jnp.zeros(lane.shape, F32)
    states = []
    for h in range(heads):
        query = jnp.concatenate(
            [queries[:, h * latent : (h + 1) * latent], queries[:, side + h * rope : side + (h + 1) * rope]], axis=1
        )
        scores = lax.dot_general(
            query, keys_ref[...], (((1,), (1,)), ((), ())), preferred_element_type=F32
        ) * ((V + ROPE) ** (-0.5))
        scores = jnp.where(live, scores, NEG)
        shift = jnp.max(scores, axis=1, keepdims=True).astype(BF16).astype(F32)
        weights = jnp.where(live, jnp.exp(scores - shift), 0.0).astype(BF16)
        total = jnp.sum(weights.astype(F32), axis=1, keepdims=True)
        outs = jnp.dot(weights, keys_ref[:, :latent], preferred_element_type=F32)
        states.append(outs.astype(BF16))
        high = total.astype(BF16).astype(F32)
        for k, value in enumerate((shift, high, total - high)):
            stats = jnp.where(lane == 3 * h + k, value, stats)
    states.append(stats.astype(BF16))
    state_ref[...] = jnp.concatenate(states, axis=1).reshape(state_ref.shape)


def project_kernel(rows, heads, latent, messages_ref, w_uv_ref, w_out_ref, term_ref):
    count = messages_ref.shape[0] * rows
    states = messages_ref[...].reshape(count, messages_ref.shape[2])
    mixed = rows * heads
    side = heads * latent
    lane = lax.broadcasted_iota(jnp.int32, (count, LANES), 1)
    row = lax.broadcasted_iota(jnp.int32, (count, LANES), 0) % rows
    column = lane % mixed
    own = (column // heads == row) & (lane < 2 * mixed)
    stats = states[:, side:].astype(F32)
    shift = jnp.full((count, LANES), 2 * NEG, F32)
    for h in range(heads):
        shift = jnp.where(own & (column % heads == h), stats[:, 3 * h : 3 * h + 1], shift)
    best = jnp.max(shift, axis=0, keepdims=True)
    factor = jnp.where(own, jnp.exp(shift - best), 0.0)
    high = factor.astype(BF16).astype(F32)
    factor = jnp.where(lane < mixed, high, factor - high).astype(BF16)
    merged = lax.dot_general(
        factor, states, (((0,), (0,)), ((), ())), preferred_element_type=F32
    )
    merged = merged[:mixed] + merged[mixed : 2 * mixed]
    parts = []
    for h in range(heads):
        total = merged[:, side + 3 * h + 1 : side + 3 * h + 2] + merged[:, side + 3 * h + 2 : side + 3 * h + 3]
        attended = (merged[:, h * latent : (h + 1) * latent] / total).astype(BF16)
        parts.append(jnp.dot(attended, w_uv_ref[h], preferred_element_type=F32))
    flat = jnp.concatenate(
        [
            jnp.concatenate([parts[h][r * heads + h : r * heads + h + 1] for h in range(heads)], axis=1)
            for r in range(rows)
        ],
        axis=0,
    ).astype(BF16)
    term_ref[...] = jnp.dot(flat, w_out_ref[...], preferred_element_type=F32).astype(term_ref.dtype)


def local(q_latent, q_rope, latent_cache, page_table, lengths, w_uv, w_out):
    rows, heads, latent = q_latent.shape
    rope = q_rope.shape[2]
    pages, page_len, width = latent_cache.shape
    tokens = pages * page_len
    count = lax.axis_size(CTX)
    size = heads * (latent + rope)
    vmem = pl.BlockSpec(memory_space=pltpu.VMEM)
    smem = pl.BlockSpec(memory_space=pltpu.SMEM)
    hbm = pl.BlockSpec(memory_space=pl.ANY)
    stay = functools.partial(pltpu.with_memory_space_constraint, memory_space=pltpu.HBM)
    params = pltpu.CompilerParams(vmem_limit_bytes=16 << 20)
    dma = pltpu.SemaphoreType.DMA
    here = lax.axis_index(CTX).astype(jnp.int32)

    message = pl.pallas_call(
        message_kernel,
        out_shape=jax.ShapeDtypeStruct((rows, size), BF16),
        in_specs=[hbm, hbm],
        out_specs=vmem,
        scratch_shapes=[pltpu.VMEM(q_latent.shape, BF16), pltpu.VMEM(q_rope.shape, BF16), dma((2,))],
        compiler_params=params,
        name="message",
    )(stay(q_latent), stay(q_rope))

    near = 4
    others = {k: lax.ppermute(message, CTX, xor_pairs(count, k)) for k in (1, 3, 2)}
    live, keys, w_uv, w_out_near = pl.pallas_call(
        functools.partial(fetch_kernel, page_len),
        out_shape=(
            pltpu.VMEM((rows, tokens), F32),
            pltpu.VMEM((tokens, width), BF16),
            pltpu.VMEM(w_uv.shape, BF16),
            pltpu.VMEM(w_out.shape, BF16),
        ),
        in_specs=[smem, hbm, hbm, hbm, hbm, hbm],
        out_specs=(vmem, vmem, vmem, vmem),
        scratch_shapes=[
            pltpu.SMEM(lengths.shape, jnp.int32), pltpu.VMEM(page_table.shape, jnp.int32), dma((5,)),
        ],
        compiler_params=params,
        cost_estimate=pl.CostEstimate(flops=0, bytes_accessed=5 << 20, transcendentals=0),
        name="fetch",
    )(
        here.reshape(1), stay(lengths), stay(page_table), stay(latent_cache.reshape(tokens, width)),
        stay(w_uv), stay(w_out),
    )
    away = lax.broadcasted_iota(jnp.int32, (near, 1, 1), 0) ^ (here % near)
    column = jnp.broadcast_to(message[None], (near, rows, size))
    for k in (2, 1, 3):
        column = jnp.where(away == k, others[k][None], column)
    column, live, keys, w_uv, w_out_near = lax.optimization_barrier((column, live, keys, w_uv, w_out_near))
    planes = [[i * near + k for i in range(count // near)] for k in range(near)]
    query = lax.all_to_all(
        jnp.broadcast_to(column[None], (count // near, near, rows, size)),
        CTX, split_axis=0, concat_axis=0, axis_index_groups=planes, tiled=True,
    )

    state_size = heads * latent + LANES
    state = pl.pallas_call(
        functools.partial(attend_kernel, rows, heads, latent, rope),
        out_shape=jax.ShapeDtypeStruct((count, rows, state_size), BF16),
        in_specs=[vmem, vmem, vmem],
        out_specs=vmem,
        compiler_params=params,
        name="attend",
    )(query.reshape(count, rows, size), keys, live)

    state = lax.all_to_all(state, CTX, split_axis=0, concat_axis=0, tiled=True)
    term = pl.pallas_call(
        functools.partial(project_kernel, rows, heads, latent),
        out_shape=jax.ShapeDtypeStruct((rows, w_out.shape[1]), BF16),
        in_specs=[vmem, vmem, vmem],
        out_specs=vmem,
        compiler_params=params,
        name="project",
    )(state, w_uv, w_out_near)
    for low in (4, 2, 0):
        term = sum_of_four(term, count, low).astype(BF16)
    return term


def solution(mesh):
    in_specs = (
        P("grp", "ctx", None),
        P("grp", "ctx", None),
        P(("grp", "ctx"), None, None),
        P("grp", None),
        P("grp"),
        P("ctx", None, None),
        P("ctx", None),
    )
    return jax.shard_map(local, mesh=mesh, in_specs=in_specs, out_specs=P("grp", None), check_vma=False)
```

```python
import functools
import jax
import jax.numpy as jnp
from jax import lax
from jax.experimental import pallas as pl
from jax.experimental.pallas import tpu as pltpu
from jax.sharding import PartitionSpec as P

ROPE = 64
V = 128
NEG = -1e30
CTX = "ctx"
LANES = 128
F32 = jnp.float32
BF16 = jnp.bfloat16


def xor_pairs(count, mask):
    return [(i, i ^ mask) for i in range(count)]


def sum_of_four(x, count, low):
    a, c, b = (lax.ppermute(x, CTX, xor_pairs(count, k << low)) for k in (1, 3, 2))
    return (x.astype(F32) + a.astype(F32)) + (c.astype(F32) + b.astype(F32))


def message_kernel(q_latent_hbm, q_rope_hbm, message_ref, q_latent_ref, q_rope_ref, sems):
    copies = [
        pltpu.make_async_copy(q_latent_hbm, q_latent_ref, sems.at[0]),
        pltpu.make_async_copy(q_rope_hbm, q_rope_ref, sems.at[1]),
    ]
    for copy in copies:
        copy.start()
    for copy in copies:
        copy.wait()
    rows, heads, _ = q_latent_ref.shape
    q_latent = q_latent_ref[...].astype(F32)
    q_rope = q_rope_ref[...].astype(F32)
    message = [
        jnp.concatenate(
            [q_latent[r, h : h + 1] for h in range(heads)] + [q_rope[r, h : h + 1] for h in range(heads)],
            axis=1,
        )
        for r in range(rows)
    ]
    message_ref[...] = jnp.concatenate(message, axis=0).astype(BF16)


def fetch_kernel(
    page_len, here_ref, lengths_hbm, table_hbm, cache_hbm, w_uv_hbm, w_out_hbm,
    live_ref, keys_ref, w_uv_ref, w_out_ref, lengths_ref, table_ref, sems,
):
    pairs = [
        (lengths_hbm, lengths_ref), (table_hbm, table_ref), (cache_hbm, keys_ref), (w_uv_hbm, w_uv_ref),
        (w_out_hbm, w_out_ref),
    ]
    copies = [pltpu.make_async_copy(a, b, sems.at[k]) for k, (a, b) in enumerate(pairs)]
    for copy in copies:
        copy.start()
    copies[0].wait()
    copies[1].wait()
    rows = live_ref.shape[0]
    tokens = keys_ref.shape[0]
    pages = tokens // page_len
    slots = table_ref.shape[1]
    page = here_ref[0] * pages + lax.broadcasted_iota(jnp.int32, (pages, slots), 0)
    place = lax.broadcasted_iota(jnp.int32, (pages, slots), 1)
    token = lax.broadcasted_iota(jnp.int32, (pages, tokens), 1)
    mine = token // page_len == lax.broadcasted_iota(jnp.int32, (pages, tokens), 0)
    for r in range(rows):
        hit = jnp.broadcast_to(table_ref[r : r + 1, :], (pages, slots)) == page
        room = jnp.where(hit, lengths_ref[r] - place * page_len, 0)
        room = jnp.max(room, axis=1, keepdims=True)
        alive = mine & (token % page_len < room)
        live_ref[r : r + 1, :] = jnp.max(jnp.where(alive, 1.0, 0.0), axis=0, keepdims=True)
    for copy in copies[2:]:
        copy.wait()


def attend_kernel(rows, heads, latent, rope, q_ref, keys_ref, live_ref, state_ref):
    size = q_ref.shape[2]
    count = q_ref.shape[0] * rows
    queries = q_ref[...].reshape(count, size)
    tokens = keys_ref.shape[0]
    row = lax.broadcasted_iota(jnp.int32, (count, 1), 0) % rows
    live = jnp.broadcast_to(live_ref[0:1, :], (count, tokens))
    for r in range(1, rows):
        live = jnp.where(row == r, live_ref[r : r + 1, :], live)
    live = live > 0.5
    side = heads * latent
    lane = lax.broadcasted_iota(jnp.int32, (count, LANES), 1)
    stats = jnp.zeros(lane.shape, F32)
    states = []
    for h in range(heads):
        query = jnp.concatenate(
            [queries[:, h * latent : (h + 1) * latent], queries[:, side + h * rope : side + (h + 1) * rope]], axis=1
        )
        scores = lax.dot_general(
            query, keys_ref[...], (((1,), (1,)), ((), ())), preferred_element_type=F32
        ) * ((V + ROPE) ** (-0.5))
        scores = jnp.where(live, scores, NEG)
        shift = jnp.max(scores, axis=1, keepdims=True).astype(BF16).astype(F32)
        weights = jnp.where(live, jnp.exp(scores - shift), 0.0).astype(BF16)
        total = jnp.sum(weights.astype(F32), axis=1, keepdims=True)
        outs = jnp.dot(weights, keys_ref[:, :latent], preferred_element_type=F32)
        states.append(outs.astype(BF16))
        high = total.astype(BF16).astype(F32)
        for k, value in enumerate((shift, high, total - high)):
            stats = jnp.where(lane == 3 * h + k, value, stats)
    states.append(stats.astype(BF16))
    state_ref[...] = jnp.concatenate(states, axis=1).reshape(state_ref.shape)


def project_kernel(rows, heads, latent, messages_ref, w_uv_ref, w_out_ref, term_ref):
    count = messages_ref.shape[0] * rows
    states = messages_ref[...].reshape(count, messages_ref.shape[2])
    mixed = rows * heads
    side = heads * latent
    lane = lax.broadcasted_iota(jnp.int32, (count, LANES), 1)
    row = lax.broadcasted_iota(jnp.int32, (count, LANES), 0) % rows
    column = lane % mixed
    own = (column // heads == row) & (lane < 2 * mixed)
    stats = states[:, side:].astype(F32)
    shift = jnp.full((count, LANES), 2 * NEG, F32)
    for h in range(heads):
        shift = jnp.where(own & (column % heads == h), stats[:, 3 * h : 3 * h + 1], shift)
    best = jnp.max(shift, axis=0, keepdims=True)
    factor = jnp.where(own, jnp.exp(shift - best), 0.0)
    high = factor.astype(BF16).astype(F32)
    factor = jnp.where(lane < mixed, high, factor - high).astype(BF16)
    merged = lax.dot_general(
        factor, states, (((0,), (0,)), ((), ())), preferred_element_type=F32
    )
    merged = merged[:mixed] + merged[mixed : 2 * mixed]
    parts = []
    for h in range(heads):
        total = merged[:, side + 3 * h + 1 : side + 3 * h + 2] + merged[:, side + 3 * h + 2 : side + 3 * h + 3]
        attended = (merged[:, h * latent : (h + 1) * latent] / total).astype(BF16)
        parts.append(jnp.dot(attended, w_uv_ref[h], preferred_element_type=F32))
    flat = jnp.concatenate(
        [
            jnp.concatenate([parts[h][r * heads + h : r * heads + h + 1] for h in range(heads)], axis=1)
            for r in range(rows)
        ],
        axis=0,
    ).astype(BF16)
    term_ref[...] = jnp.dot(flat, w_out_ref[...], preferred_element_type=F32).astype(term_ref.dtype)


def local(q_latent, q_rope, latent_cache, page_table, lengths, w_uv, w_out):
    rows, heads, latent = q_latent.shape
    rope = q_rope.shape[2]
    pages, page_len, width = latent_cache.shape
    tokens = pages * page_len
    count = lax.axis_size(CTX)
    size = heads * (latent + rope)
    vmem = pl.BlockSpec(memory_space=pltpu.VMEM)
    smem = pl.BlockSpec(memory_space=pltpu.SMEM)
    hbm = pl.BlockSpec(memory_space=pl.ANY)
    stay = functools.partial(pltpu.with_memory_space_constraint, memory_space=pltpu.HBM)
    params = pltpu.CompilerParams(vmem_limit_bytes=16 << 20)
    dma = pltpu.SemaphoreType.DMA
    here = lax.axis_index(CTX).astype(jnp.int32)

    message = pl.pallas_call(
        message_kernel,
        out_shape=jax.ShapeDtypeStruct((rows, size), BF16),
        in_specs=[hbm, hbm],
        out_specs=vmem,
        scratch_shapes=[pltpu.VMEM(q_latent.shape, BF16), pltpu.VMEM(q_rope.shape, BF16), dma((2,))],
        compiler_params=params,
        name="message",
    )(stay(q_latent), stay(q_rope))

    near = 4
    others = {k: lax.ppermute(message, CTX, xor_pairs(count, k)) for k in (1, 3, 2)}
    live, keys, w_uv, w_out_near = pl.pallas_call(
        functools.partial(fetch_kernel, page_len),
        out_shape=(
            pltpu.VMEM((rows, tokens), F32),
            pltpu.VMEM((tokens, width), BF16),
            pltpu.VMEM(w_uv.shape, BF16),
            pltpu.VMEM(w_out.shape, BF16),
        ),
        in_specs=[smem, hbm, hbm, hbm, hbm, hbm],
        out_specs=(vmem, vmem, vmem, vmem),
        scratch_shapes=[
            pltpu.SMEM(lengths.shape, jnp.int32), pltpu.VMEM(page_table.shape, jnp.int32), dma((5,)),
        ],
        compiler_params=params,
        cost_estimate=pl.CostEstimate(flops=0, bytes_accessed=5 << 20, transcendentals=0),
        name="fetch",
    )(
        here.reshape(1), stay(lengths), stay(page_table), stay(latent_cache.reshape(tokens, width)),
        stay(w_uv), stay(w_out),
    )
    away = lax.broadcasted_iota(jnp.int32, (near, 1, 1), 0) ^ (here % near)
    column = jnp.broadcast_to(message[None], (near, rows, size))
    for k in (2, 3, 1):
        column = jnp.where(away == k, others[k][None], column)
    column, live, keys, w_uv, w_out_near = lax.optimization_barrier((column, live, keys, w_uv, w_out_near))
    planes = [[i * near + k for i in range(count // near)] for k in range(near)]
    query = lax.all_to_all(
        jnp.broadcast_to(column[None], (count // near, near, rows, size)),
        CTX, split_axis=0, concat_axis=0, axis_index_groups=planes, tiled=True,
    )

    state_size = heads * latent + LANES
    state = pl.pallas_call(
        functools.partial(attend_kernel, rows, heads, latent, rope),
        out_shape=jax.ShapeDtypeStruct((count, rows, state_size), BF16),
        in_specs=[vmem, vmem, vmem],
        out_specs=vmem,
        compiler_params=params,
        name="attend",
    )(query.reshape(count, rows, size), keys, live)

    state = lax.all_to_all(state, CTX, split_axis=0, concat_axis=0, tiled=True)
    term = pl.pallas_call(
        functools.partial(project_kernel, rows, heads, latent),
        out_shape=jax.ShapeDtypeStruct((rows, w_out.shape[1]), BF16),
        in_specs=[vmem, vmem, vmem],
        out_specs=vmem,
        compiler_params=params,
        name="project",
    )(state, w_uv, w_out_near)
    for low in (4, 2, 0):
        term = sum_of_four(term, count, low).astype(BF16)
    return term


def solution(mesh):
    in_specs = (
        P("grp", "ctx", None),
        P("grp", "ctx", None),
        P(("grp", "ctx"), None, None),
        P("grp", None),
        P("grp"),
        P("ctx", None, None),
        P("ctx", None),
    )
    return jax.shard_map(local, mesh=mesh, in_specs=in_specs, out_specs=P("grp", None), check_vma=False)
```

```python
import functools
import jax
import jax.numpy as jnp
from jax import lax
from jax.experimental import pallas as pl
from jax.experimental.pallas import tpu as pltpu
from jax.sharding import PartitionSpec as P

ROPE = 64
V = 128
NEG = -1e30
CTX = "ctx"
LANES = 128
F32 = jnp.float32
BF16 = jnp.bfloat16


def xor_pairs(count, mask):
    return [(i, i ^ mask) for i in range(count)]


def sum_of_four(x, count, low):
    a, c, b = (lax.ppermute(x, CTX, xor_pairs(count, k << low)) for k in (1, 3, 2))
    return (x.astype(F32) + a.astype(F32)) + (c.astype(F32) + b.astype(F32))


def message_kernel(q_latent_hbm, q_rope_hbm, message_ref, q_latent_ref, q_rope_ref, sems):
    copies = [
        pltpu.make_async_copy(q_latent_hbm, q_latent_ref, sems.at[0]),
        pltpu.make_async_copy(q_rope_hbm, q_rope_ref, sems.at[1]),
    ]
    for copy in copies:
        copy.start()
    for copy in copies:
        copy.wait()
    rows, heads, _ = q_latent_ref.shape
    q_latent = q_latent_ref[...].astype(F32)
    q_rope = q_rope_ref[...].astype(F32)
    message = [
        jnp.concatenate(
            [q_latent[r, h : h + 1] for h in range(heads)] + [q_rope[r, h : h + 1] for h in range(heads)],
            axis=1,
        )
        for r in range(rows)
    ]
    message_ref[...] = jnp.concatenate(message, axis=0).astype(BF16)


def fetch_kernel(
    page_len, here_ref, lengths_hbm, table_hbm, cache_hbm, w_uv_hbm, w_out_hbm,
    live_ref, keys_ref, w_uv_ref, w_out_ref, lengths_ref, table_ref, sems,
):
    pairs = [
        (lengths_hbm, lengths_ref), (table_hbm, table_ref), (cache_hbm, keys_ref), (w_uv_hbm, w_uv_ref),
        (w_out_hbm, w_out_ref),
    ]
    copies = [pltpu.make_async_copy(a, b, sems.at[k]) for k, (a, b) in enumerate(pairs)]
    for copy in copies:
        copy.start()
    copies[0].wait()
    copies[1].wait()
    rows = live_ref.shape[0]
    tokens = keys_ref.shape[0]
    pages = tokens // page_len
    slots = table_ref.shape[1]
    page = here_ref[0] * pages + lax.broadcasted_iota(jnp.int32, (pages, slots), 0)
    place = lax.broadcasted_iota(jnp.int32, (pages, slots), 1)
    token = lax.broadcasted_iota(jnp.int32, (pages, tokens), 1)
    mine = token // page_len == lax.broadcasted_iota(jnp.int32, (pages, tokens), 0)
    for r in range(rows):
        hit = jnp.broadcast_to(table_ref[r : r + 1, :], (pages, slots)) == page
        room = jnp.where(hit, lengths_ref[r] - place * page_len, 0)
        room = jnp.max(room, axis=1, keepdims=True)
        alive = mine & (token % page_len < room)
        live_ref[r : r + 1, :] = jnp.max(jnp.where(alive, 1.0, 0.0), axis=0, keepdims=True)
    for copy in copies[2:]:
        copy.wait()


def spread_kernel(here_ref, *refs):
    *parts, out_ref = refs
    near = len(parts)
    values = [part[...].astype(F32) for part in parts]
    for k in range(near):
        away = lax.rem(here_ref[0], near) ^ k
        value = values[0]
        for j in range(1, near):
            value = jnp.where(away == j, values[j], value)
        out_ref[:, k] = jnp.broadcast_to(value[None], (out_ref.shape[0],) + value.shape).astype(BF16)


def attend_kernel(rows, heads, latent, rope, q_ref, keys_ref, live_ref, state_ref):
    size = q_ref.shape[2]
    count = q_ref.shape[0] * rows
    queries = q_ref[...].reshape(count, size)
    tokens = keys_ref.shape[0]
    row = lax.broadcasted_iota(jnp.int32, (count, 1), 0) % rows
    live = jnp.broadcast_to(live_ref[0:1, :], (count, tokens))
    for r in range(1, rows):
        live = jnp.where(row == r, live_ref[r : r + 1, :], live)
    live = live > 0.5
    side = heads * latent
    lane = lax.broadcasted_iota(jnp.int32, (count, LANES), 1)
    stats = jnp.zeros(lane.shape, F32)
    states = []
    for h in range(heads):
        query = jnp.concatenate(
            [queries[:, h * latent : (h + 1) * latent], queries[:, side + h * rope : side + (h + 1) * rope]], axis=1
        )
        scores = lax.dot_general(
            query, keys_ref[...], (((1,), (1,)), ((), ())), preferred_element_type=F32
        ) * ((V + ROPE) ** (-0.5))
        scores = jnp.where(live, scores, NEG)
        shift = jnp.max(scores, axis=1, keepdims=True).astype(BF16).astype(F32)
        weights = jnp.where(live, jnp.exp(scores - shift), 0.0).astype(BF16)
        total = jnp.sum(weights.astype(F32), axis=1, keepdims=True)
        outs = jnp.dot(weights, keys_ref[:, :latent], preferred_element_type=F32)
        states.append(outs.astype(BF16))
        high = total.astype(BF16).astype(F32)
        for k, value in enumerate((shift, high, total - high)):
            stats = jnp.where(lane == 3 * h + k, value, stats)
    states.append(stats.astype(BF16))
    state_ref[...] = jnp.concatenate(states, axis=1).reshape(state_ref.shape)


def project_kernel(rows, heads, latent, messages_ref, w_uv_ref, w_out_ref, term_ref):
    count = messages_ref.shape[0] * rows
    states = messages_ref[...].reshape(count, messages_ref.shape[2])
    mixed = rows * heads
    side = heads * latent
    lane = lax.broadcasted_iota(jnp.int32, (count, LANES), 1)
    row = lax.broadcasted_iota(jnp.int32, (count, LANES), 0) % rows
    column = lane % mixed
    own = (column // heads == row) & (lane < 2 * mixed)
    stats = states[:, side:].astype(F32)
    shift = jnp.full((count, LANES), 2 * NEG, F32)
    for h in range(heads):
        shift = jnp.where(own & (column % heads == h), stats[:, 3 * h : 3 * h + 1], shift)
    best = jnp.max(shift, axis=0, keepdims=True)
    factor = jnp.where(own, jnp.exp(shift - best), 0.0)
    high = factor.astype(BF16).astype(F32)
    factor = jnp.where(lane < mixed, high, factor - high).astype(BF16)
    merged = lax.dot_general(
        factor, states, (((0,), (0,)), ((), ())), preferred_element_type=F32
    )
    merged = merged[:mixed] + merged[mixed : 2 * mixed]
    parts = []
    for h in range(heads):
        total = merged[:, side + 3 * h + 1 : side + 3 * h + 2] + merged[:, side + 3 * h + 2 : side + 3 * h + 3]
        attended = (merged[:, h * latent : (h + 1) * latent] / total).astype(BF16)
        parts.append(jnp.dot(attended, w_uv_ref[h], preferred_element_type=F32))
    flat = jnp.concatenate(
        [
            jnp.concatenate([parts[h][r * heads + h : r * heads + h + 1] for h in range(heads)], axis=1)
            for r in range(rows)
        ],
        axis=0,
    ).astype(BF16)
    term_ref[...] = jnp.dot(flat, w_out_ref[...], preferred_element_type=F32).astype(term_ref.dtype)


def local(q_latent, q_rope, latent_cache, page_table, lengths, w_uv, w_out):
    rows, heads, latent = q_latent.shape
    rope = q_rope.shape[2]
    pages, page_len, width = latent_cache.shape
    tokens = pages * page_len
    count = lax.axis_size(CTX)
    size = heads * (latent + rope)
    vmem = pl.BlockSpec(memory_space=pltpu.VMEM)
    smem = pl.BlockSpec(memory_space=pltpu.SMEM)
    hbm = pl.BlockSpec(memory_space=pl.ANY)
    stay = functools.partial(pltpu.with_memory_space_constraint, memory_space=pltpu.HBM)
    params = pltpu.CompilerParams(vmem_limit_bytes=16 << 20)
    dma = pltpu.SemaphoreType.DMA
    here = lax.axis_index(CTX).astype(jnp.int32)

    message = pl.pallas_call(
        message_kernel,
        out_shape=jax.ShapeDtypeStruct((rows, size), BF16),
        in_specs=[hbm, hbm],
        out_specs=vmem,
        scratch_shapes=[pltpu.VMEM(q_latent.shape, BF16), pltpu.VMEM(q_rope.shape, BF16), dma((2,))],
        compiler_params=params,
        name="message",
    )(stay(q_latent), stay(q_rope))

    near = 4
    others = {k: lax.ppermute(message, CTX, xor_pairs(count, k)) for k in (1, 3, 2)}
    live, keys, w_uv, w_out_near = pl.pallas_call(
        functools.partial(fetch_kernel, page_len),
        out_shape=(
            pltpu.VMEM((rows, tokens), F32),
            pltpu.VMEM((tokens, width), BF16),
            pltpu.VMEM(w_uv.shape, BF16),
            pltpu.VMEM(w_out.shape, BF16),
        ),
        in_specs=[smem, hbm, hbm, hbm, hbm, hbm],
        out_specs=(vmem, vmem, vmem, vmem),
        scratch_shapes=[
            pltpu.SMEM(lengths.shape, jnp.int32), pltpu.VMEM(page_table.shape, jnp.int32), dma((5,)),
        ],
        compiler_params=params,
        cost_estimate=pl.CostEstimate(flops=0, bytes_accessed=5 << 20, transcendentals=0),
        name="fetch",
    )(
        here.reshape(1), stay(lengths), stay(page_table), stay(latent_cache.reshape(tokens, width)),
        stay(w_uv), stay(w_out),
    )
    ready = lax.optimization_barrier((message, *others.values(), live, keys, w_uv, w_out_near))
    message, live, keys, w_uv, w_out_near = ready[0], *ready[near:]
    others = dict(zip(others, ready[1:near]))
    query = pl.pallas_call(
        spread_kernel,
        out_shape=jax.ShapeDtypeStruct((count // near, near, rows, size), BF16),
        in_specs=[smem] + [vmem] * near,
        out_specs=vmem,
        compiler_params=params,
        name="spread",
    )(here.reshape(1), message, *[others[k] for k in range(1, near)])
    planes = [[i * near + k for i in range(count // near)] for k in range(near)]
    query = lax.all_to_all(
        query, CTX, split_axis=0, concat_axis=0, axis_index_groups=planes, tiled=True
    )

    state_size = heads * latent + LANES
    state = pl.pallas_call(
        functools.partial(attend_kernel, rows, heads, latent, rope),
        out_shape=jax.ShapeDtypeStruct((count, rows, state_size), BF16),
        in_specs=[vmem, vmem, vmem],
        out_specs=vmem,
        compiler_params=params,
        name="attend",
    )(query.reshape(count, rows, size), keys, live)

    state = lax.all_to_all(state, CTX, split_axis=0, concat_axis=0, tiled=True)
    term = pl.pallas_call(
        functools.partial(project_kernel, rows, heads, latent),
        out_shape=jax.ShapeDtypeStruct((rows, w_out.shape[1]), BF16),
        in_specs=[vmem, vmem, vmem],
        out_specs=vmem,
        compiler_params=params,
        name="project",
    )(state, w_uv, w_out_near)
    for low in (4, 2, 0):
        term = sum_of_four(term, count, low).astype(BF16)
    return term


def solution(mesh):
    in_specs = (
        P("grp", "ctx", None),
        P("grp", "ctx", None),
        P(("grp", "ctx"), None, None),
        P("grp", None),
        P("grp"),
        P("ctx", None, None),
        P("ctx", None),
    )
    return jax.shard_map(local, mesh=mesh, in_specs=in_specs, out_specs=P("grp", None), check_vma=False)
```
